128 devices in a mesh: ctx: 16 (over y, x_lo, core), db: 8 (over x_hi, z).
Axes of the slice: x: 4 (x_hi: 2, x_lo: 2; x = x_hi * 2 + x_lo), y: 4, z: 4, core: 2. Of those that a mesh axis runs over, the one named last changes fastest.
Arguments:
- queries: bfloat16 [8, 4096, 2048], P('db', 'ctx'), may hold values from -6 to 6
- keys: bfloat16 [8, 4096, 2048], P('db', 'ctx'), may hold values from -6 to 6
- values: bfloat16 [8, 4096, 2048], P('db', 'ctx'), may hold values from -6 to 6
- doc_ids: int32 [8, 4096], P('db', 'ctx'), may hold values from 0 to 3, never falling along the last dimension, each value on 1 to 3072 neighbouring positions
- nbr_owner: int32 [8, 64, 2], P('db', 'ctx'), may hold values from 0 to 7, all different within a row; in each aligned block of 4 rows (0 to 3, 4 to 7, ..., all dimensions but the last counted through in order) at most 2 rows name the same one
- nbr_local: int32 [8, 64, 2], P('db', 'ctx'), may hold values from 0 to 7
- db_keys: bfloat16 [8, 128, 64, 2048], P('db', 'ctx'), may hold values from -6 to 6
- db_values: bfloat16 [8, 128, 64, 2048], P('db', 'ctx'), may hold values from -6 to 6
Outputs:
- self_out: bfloat16 [8, 4096, 2048], P('db', 'ctx')
- cross_out: bfloat16 [8, 4096, 2048], P('db', 'ctx')
The draws below stay inside these ranges and needn't reach their ends.
Inputs may be any that keep to these rules, and one draw needn't show every extreme that they name: `nbr_owner`: the 2 neighbours of a query span lie in different shards. Among the 4 query spans of one device (aligned blocks of 4 spans) no shard is named more than 2 times, and on some devices one shard is named exactly 2 times. `nbr_local`: A neighbour of query span n lies among the 8 spans n // 4 * 8 to n // 4 * 8 + 7 of its shard. `doc_ids`: never falls along a sequence; at most 4 documents, the longest 3 * 1024 tokens.
All inputs are finite; a program needn't handle non-finite values.
Results may differ from the reference program's by a relative error of at most 0.0045.
Values may be sent and summed in bfloat16 or wider, within the bound.
No kernel may reach another device: no remote copies, remote signals or barrier semaphores. Data moves between devices by JAX's collectives and lax.ppermute only.
A program may use at most 256 MiB of HBM per device.

```python
import math
import jax
import jax.numpy as jnp
import numpy as np
from jax import lax

DH = 128
CH = 64
KN = 2
CAP = 2
DOCS = 4
DB_DEV = 8
HD = 2048
SEQ = 4096
NCH = 64
QC = 4
GROUPS = 8
SHARDS = 8
SLOTS = 128
N_CTX = 16


def rough_rows(key, shape):
    return jnp.clip(jax.random.normal(jax.random.fold_in(key, 1), shape, jnp.float32), -6.0, 6.0)


def draw_queries(key, part):
    base = rough_rows(jax.random.fold_in(key, 11), (GROUPS, SEQ, HD))
    return base.astype(jnp.bfloat16)


def draw_keys(key, part):
    base = rough_rows(jax.random.fold_in(key, 12), (GROUPS, SEQ, HD))
    return base.astype(jnp.bfloat16)


def draw_db_keys(key, part):
    base = rough_rows(jax.random.fold_in(key, 13), (SHARDS, SLOTS, CH, HD))
    return base.astype(jnp.bfloat16)


def place_ends(entries, rng, smallest, largest):
    place = [jax.random.randint(jax.random.fold_in(rng, axis), (), 0, length) for axis, length in enumerate(entries.shape)]
    main_axis = entries.shape.index(max(entries.shape))
    neighbour = place[:main_axis] + [(place[main_axis] + 1) % entries.shape[main_axis]] + place[main_axis + 1:]
    return entries.at[tuple(place)].set(smallest).at[tuple(neighbour)].set(largest)


def level_of(rng, dims, shards, smallest, largest):
    loudness = 1.0
    for position, parts in shards:
        draws = jax.random.uniform(jax.random.fold_in(jax.random.fold_in(rng, 6), position), (parts,), jnp.float32, smallest / len(shards), largest / len(shards))
        loudness = loudness * jnp.repeat(jnp.exp(draws), dims[position] // parts).reshape((-1,) + (1,) * (len(dims) - 1 - position))
    return loudness


def profile(number_of, total, bound, lean):
    weights = [(1 << 20) // math.isqrt(standing ** lean) + 1 for standing in range(2, number_of + 1)]
    surplus, holding = total - bound - (number_of - 1), [1] * (number_of - 1)
    while surplus > 0:
        candidates = [i for i in range(number_of - 1) if holding[i] < bound]
        mass, remaining = sum([weights[i] for i in candidates]), surplus
        for i in candidates:
            more = min(bound - holding[i], max(1, remaining * weights[i] // mass), surplus)
            holding[i] = holding[i] + more
            surplus = surplus - more
    return np.array([bound] + holding)


def uneven_parts(own_key, amount, total, bound, slope):
    if amount == 2:
        one = jax.random.randint(own_key, (), max(1, total - bound), min(bound, total - 1) + 1)
        return jnp.stack([one, total - one])
    sizes = jnp.asarray(profile(amount, total, bound, slope), jnp.int32)
    couples = (amount - 1) // 2
    giver, receiver = sizes[1:1 + 2 * couples:2], sizes[2:2 + 2 * couples:2]
    margin = jnp.minimum(giver - 1, bound - receiver)
    shifted = jax.random.randint(jax.random.fold_in(own_key, 1), (couples,), 0, 1 << 20) % (margin + 1)
    sizes = sizes.at[1:1 + 2 * couples:2].set(giver - shifted).at[2:2 + 2 * couples:2].set(receiver + shifted)
    return sizes[jax.random.permutation(jax.random.fold_in(own_key, 2), amount)]


def routed_block(key, own, number, rows, count, top, limit, skew):
    order = jax.random.permutation(key, count)
    heavy_load, common = portions_of(count, rows * top, limit, skew, True), portions_of(count, rows * top, limit, skew, False)
    places = jnp.arange(count)

    def named(tallies, offset_by):
        used = int((tallies > 0).sum())
        fixed = max(1, used // 4)
        shifted = fixed + (places - fixed + offset_by * (used - fixed)) % max(1, count - fixed)
        return jnp.zeros((count,), jnp.int32).at[order[jnp.where(places < fixed, places, shifted)]].set(jnp.asarray(tallies, jnp.int32))

    tallies = jnp.where(number % 4 == 0, named(heavy_load, number // 4), named(common, number - number // 4 - 1))
    mixed = jax.random.permutation(jax.random.fold_in(own, 3), count)
    source_of, taker = mixed[0:count // 2 * 2:2], mixed[1:count // 2 * 2:2]
    margin = jnp.minimum(tallies[source_of] - 1, limit - tallies[taker]) // 2
    margin = jnp.where((source_of == order[0]) | (taker == order[0]) | (tallies[taker] == 0), 0, jnp.maximum(margin, 0))
    shifted = jax.random.randint(jax.random.fold_in(own, 4), (count // 2,), 0, 1 << 20) % (margin + 1)
    tallies = tallies.at[source_of].add(-shifted).at[taker].add(shifted)
    items = jnp.searchsorted(jnp.cumsum(tallies), jnp.arange(rows * top), side="right").astype(jnp.int32)
    listing = items.reshape(top, rows).T
    listing = listing[jax.random.permutation(jax.random.fold_in(own, 1), rows)]
    offset_by = jax.random.randint(jax.random.fold_in(own, 2), (rows, 1), 0, top)
    return jnp.take_along_axis(listing, (jnp.arange(top)[None, :] + offset_by) % top, axis=1)


def portions_of(amount, total, limit, lean, full):
    portions = [(1 << 20) // math.isqrt(standing ** lean) + 1 for standing in range(1, amount + 1)]
    largest = limit if full else min(limit, max(-(-total // amount), total * portions[0] // sum(portions)))
    least = 1 if total - largest >= amount - 1 else 0
    given, spare = [largest] + [least] * (amount - 1), total - largest - least * (amount - 1)
    while spare > 0:
        free = [i for i in range(1, amount) if given[i] < largest] or [i for i in range(1, amount) if given[i] < limit]
        mass, budget = sum([portions[i] for i in free]), spare
        for i in free:
            addition = min(limit - given[i], max(1, budget * portions[i] // mass), spare)
            given[i] = given[i] + addition
            spare = spare - addition
    return np.array(given)


def noise(own_key, dims, scale, reach, split=(), kind=jnp.bfloat16):
    values = jax.random.normal(own_key, dims, jnp.float32) * scale
    if len(split) > 0:
        values = level_of(own_key, dims, split, -0.22, 0.18) * values
    return jnp.clip(values, min=-reach, max=reach).astype(kind)


def setup_inputs(seed: int = 0) -> dict:
    seeds = jax.random.split(jax.random.key(seed), 9)
    queries = draw_queries(jax.random.fold_in(seeds[8], 71), 0)
    keys = draw_keys(jax.random.fold_in(seeds[8], 71), 0)
    values = noise(seeds[2], (GROUPS, SEQ, HD), 1.0, 6.0, ((0, 8), (1, 16)))
    doc_ids = jax.vmap(lambda own: jnp.searchsorted(jnp.cumsum(uneven_parts(own, DOCS, SEQ, (3 * SEQ) // 4, 0)), jnp.arange(SEQ), side="right"))(jax.random.split(seeds[3], GROUPS)).reshape((GROUPS, SEQ)).astype(jnp.int32)
    nbr_owner_keys = jax.random.split(jax.random.fold_in(seeds[4], 1), GROUPS * NCH // QC)
    nbr_owner_turns = jax.random.permutation(jax.random.fold_in(seeds[4], 3), GROUPS * NCH // QC)
    nbr_owner = jax.vmap(lambda own, number: routed_block(jax.random.fold_in(seeds[4], 2), own, number, QC, SHARDS, KN, CAP, 2))(nbr_owner_keys, nbr_owner_turns).reshape((GROUPS, NCH, KN))
    nbr_local = place_ends(jax.random.randint(seeds[5], (GROUPS, NCH, KN), 0, DB_DEV), jax.random.fold_in(seeds[5], 1), 0, DB_DEV - 1).astype(jnp.int32)
    db_keys = draw_db_keys(jax.random.fold_in(seeds[8], 71), 0)
    db_values = noise(seeds[7], (SHARDS, SLOTS, CH, HD), 1.0, 6.0, ((0, 8), (1, 16)))
    return dict(queries=queries, keys=keys, values=values, doc_ids=doc_ids, nbr_owner=nbr_owner, nbr_local=nbr_local, db_keys=db_keys, db_values=db_values)


neg_fill = -1e+30

def attend_all(query_rows, key_rows, value_rows, docs):
    seq_len = query_rows.shape[0]
    head_count = query_rows.shape[1] // DH
    block_len = math.gcd(seq_len, 512)
    query_heads = query_rows.astype(jnp.float32).reshape(seq_len, head_count, DH)
    key_heads = key_rows.astype(jnp.float32).reshape(seq_len, head_count, DH)
    value_heads = value_rows.astype(jnp.float32).reshape(seq_len, head_count, DH)
    key_pos = jnp.arange(seq_len, dtype=jnp.int32)
    score_scale = 1.0 / math.sqrt(DH)

    def one_block(block_index):
        offset = block_index * block_len
        query_block = lax.dynamic_slice_in_dim(query_heads, offset, block_len, 0)
        query_pos = offset + jnp.arange(block_len, dtype=jnp.int32)
        query_docs = lax.dynamic_slice_in_dim(docs, offset, block_len, 0)
        allowed = (key_pos[None, :] <= query_pos[:, None]) & (docs[None, :] == query_docs[:, None])
        scores = jnp.einsum('thd,shd->hts', query_block, key_heads) * score_scale
        scores = jnp.where(allowed[None], scores, neg_fill)
        row_top = lax.optimization_barrier(jnp.max(scores, axis=2))
        expo = jnp.where(allowed[None], jnp.exp(scores - row_top[:, :, None]), 0.0)
        running_sum = lax.optimization_barrier(jnp.sum(expo, axis=2))
        weights = lax.optimization_barrier(expo.astype(jnp.bfloat16)).astype(jnp.float32)
        mixed = jnp.einsum('hts,shd->thd', weights, value_heads)
        return (mixed / jnp.swapaxes(running_sum, 0, 1)[:, :, None]).astype(jnp.bfloat16)
    results = lax.map(one_block, jnp.arange(seq_len // block_len, dtype=jnp.int32))
    return results.reshape(seq_len, head_count * DH)

def reference(queries, keys, values, doc_ids, nbr_owner, nbr_local, db_keys, db_values):
    self_out = lax.map(lambda bundle: attend_all(*bundle), (queries, keys, values, doc_ids))
    score_scale = 1.0 / math.sqrt(DH)

    def cross_group(bundle):
        query_rows, owner_ids, local_ids = bundle
        seq_len, row_width = query_rows.shape
        head_count = row_width // DH
        span_total = owner_ids.shape[0]
        per_column = span_total // N_CTX
        column = (jnp.arange(span_total, dtype=jnp.int32) // per_column)[:, None]
        slot_ids = (column * DB_DEV + local_ids).astype(jnp.int32)
        near_keys = db_keys[owner_ids, slot_ids].astype(jnp.float32)
        near_values = db_values[owner_ids, slot_ids].astype(jnp.float32)
        near_keys = near_keys.reshape(span_total, KN * CH, head_count, DH)
        near_values = near_values.reshape(span_total, KN * CH, head_count, DH)
        span_queries = query_rows.astype(jnp.float32).reshape(span_total, CH, head_count, DH)
        scores = jnp.einsum('cthd,cshd->chts', span_queries, near_keys) * score_scale
        row_top = lax.optimization_barrier(jnp.max(scores, axis=3))
        expo = jnp.exp(scores - row_top[..., None])
        running_sum = lax.optimization_barrier(jnp.sum(expo, axis=3))
        weights = lax.optimization_barrier(expo.astype(jnp.bfloat16)).astype(jnp.float32)
        mixed = jnp.einsum('chts,cshd->cthd', weights, near_values)
        mixed = mixed / jnp.swapaxes(running_sum, 1, 2)[..., None]
        return mixed.astype(jnp.bfloat16).reshape(seq_len, row_width)
    cross_out = lax.map(cross_group, (queries, nbr_owner, nbr_local))
    return (self_out, cross_out)
```

```python
import functools
import math

import jax
import jax.numpy as jnp
from jax import lax
from jax.experimental import pallas as pl
from jax.experimental.pallas import tpu as pltpu
from jax.sharding import PartitionSpec as P

DH = 128
CH = 64
NH = 16
TOK = 256
HD = 2048
NZ = 4
NC = 16
QT = 512
CHUNK = 3 * TOK + 16
NEG = -1e30
SCALE = math.log2(math.e) / math.sqrt(DH)
VMEM = 48 << 20

f32, bf16, i32 = jnp.float32, jnp.bfloat16, jnp.int32


def params():
    return pltpu.CompilerParams(vmem_limit_bytes=VMEM)


def cost(flops, nbytes):
    return pl.CostEstimate(flops=flops, bytes_accessed=nbytes, transcendentals=0)


def pack_heads_kernel(docs_ref, q_ref, k_ref, v_ref, out_ref):
    row = lax.broadcasted_iota(i32, (16, DH), 0)
    docs = docs_ref[...]
    left = jnp.broadcast_to(docs[:, :DH], (16, DH))
    right = jnp.broadcast_to(docs[:, DH:], (16, DH))
    packed = jnp.where(row == 0, left, jnp.where(row == 1, right, 4)).astype(f32).astype(bf16)
    for h in range(4):
        cols = slice(h * DH, (h + 1) * DH)
        out_ref[h, 0:TOK, :] = q_ref[:, cols]
        out_ref[h, TOK : 2 * TOK, :] = k_ref[:, cols]
        out_ref[h, 2 * TOK : 3 * TOK, :] = v_ref[:, cols]
        out_ref[h, 3 * TOK : CHUNK, :] = packed


def pack_heads(docs, q, k, v):
    wide = pl.BlockSpec((TOK, 4 * DH), lambda i: (0, i))
    return pl.pallas_call(
        pack_heads_kernel,
        grid=(4,),
        in_specs=[pl.BlockSpec((1, TOK), lambda i: (0, 0)), wide, wide, wide],
        out_specs=pl.BlockSpec((4, CHUNK, DH), lambda i: (i, 0, 0)),
        out_shape=jax.ShapeDtypeStruct((NC, CHUNK, DH), bf16),
        compiler_params=params(),
        cost_estimate=cost(0, 6 << 20),
        name="pack_heads",
    )(docs, q, k, v)


def unpack_heads_kernel(x_ref, out_ref):
    for h in range(4):
        out_ref[:, h * DH : (h + 1) * DH] = x_ref[h]


def unpack_heads(x):
    return pl.pallas_call(
        unpack_heads_kernel,
        grid=(4,),
        in_specs=[pl.BlockSpec((4, TOK, DH), lambda i: (i, 0, 0))],
        out_specs=pl.BlockSpec((TOK, 4 * DH), lambda i: (0, i)),
        out_shape=jax.ShapeDtypeStruct((TOK, HD), bf16),
        compiler_params=params(),
        cost_estimate=cost(0, 2 << 20),
        name="unpack_heads",
    )(x)


def self_kernel(x_ref, o_ref):
    docs = x_ref[:, 3 * TOK : CHUNK, :].astype(f32)
    ends = [jnp.sum(jnp.where(docs < d - 0.5, 1.0, 0.0)).astype(i32) for d in (1, 2, 3)]

    def start_of(p):
        s = jnp.where(p >= ends[0], ends[0], 0)
        s = jnp.maximum(s, jnp.where(p >= ends[1], ends[1], 0))
        return jnp.maximum(s, jnp.where(p >= ends[2], ends[2], 0))

    def rows(j, part):
        return x_ref[pl.ds(2 * j, 2), part * TOK : (part + 1) * TOK, :].reshape(QT, DH)

    local = lax.broadcasted_iota(i32, (QT, QT), 1)
    column = lax.broadcasted_iota(i32, (QT, 1), 0)

    def scores(q, j):
        s = lax.dot_general(q, rows(j, 1), (((1,), (1,)), ((), ())), preferred_element_type=f32)
        return s * SCALE

    def lanes(p):
        return (p[:, :DH] + p[:, DH : 2 * DH]) + (p[:, 2 * DH : 3 * DH] + p[:, 3 * DH :])

    def mix(p, j):
        return jnp.dot(p.astype(bf16), rows(j, 2), preferred_element_type=f32)

    def query_tile(i, carry):
        base = i * QT
        q = rows(i, 0)
        first = start_of(base + column)
        lo = start_of(base) // QT
        mid = jnp.minimum((start_of(base + QT - 1) + QT - 1) // QT, i)

        s = scores(q, i)
        s = jnp.where((local <= column) & (local >= first - base), s, NEG)
        top = jnp.max(s, axis=1, keepdims=True)
        p = jnp.exp2(s - top)
        state = (mix(p, i), top, lanes(p))

        def step(j, state, masked):
            acc, top, total = state
            s = scores(q, j)
            if masked:
                s = jnp.where(local >= first - j * QT, s, NEG)
            new = jnp.maximum(top, jnp.max(s, axis=1, keepdims=True))
            p = jnp.exp2(s - new)
            fade = jnp.exp2(top - new)
            return acc * fade + mix(p, j), new, total * fade + lanes(p)

        state = lax.fori_loop(lo, mid, functools.partial(step, masked=True), state)
        acc, top, total = lax.fori_loop(mid, i, functools.partial(step, masked=False), state)
        out = acc / jnp.sum(total, axis=1, keepdims=True)
        o_ref[pl.ds(2 * i, 2)] = out.astype(bf16).reshape(2, TOK, DH)
        return carry

    lax.fori_loop(0, NC * TOK // QT, query_tile, 0)


def self_attention(x):
    return pl.pallas_call(
        self_kernel,
        in_specs=[pl.BlockSpec(memory_space=pltpu.VMEM)],
        out_specs=pl.BlockSpec(memory_space=pltpu.VMEM),
        out_shape=jax.ShapeDtypeStruct((NC, TOK, DH), bf16),
        compiler_params=params(),
        cost_estimate=cost(16 << 30, 4 << 20),
        name="self_attention",
    )(x)


def pack_spans_kernel(tab_ref, keys_ref, values_ref, *refs):
    outs, sems = refs[:8], refs[8]
    me = lax.axis_index("db")
    plane, z = me // NZ, me % NZ
    copies = []
    for far in (1, 0):
        side = 1 - plane if far else plane
        for k in (1, 3, 2, 0):
            asker = side * NZ + (z + k) % NZ
            first, second, seen = jnp.int32(0), jnp.int32(0), jnp.int32(0)
            for r in range(8):
                hit = tab_ref[asker, r] == me
                span = tab_ref[asker, 8 + r]
                first = jnp.where(hit & (seen == 0), span, first)
                second = jnp.where(hit & (seen == 1), span, second)
                seen = seen + jnp.where(hit, 1, 0)
            for slot, span in ((0, first), (1, second)):
                for kind, src in ((0, keys_ref), (1, values_ref)):
                    copy = pltpu.make_async_copy(
                        src.at[span], outs[far * 4 + k].at[slot, kind], sems.at[far * 4 + k, slot, kind]
                    )
                    copy.start()
                    copies.append(copy)
    for copy in copies:
        copy.wait()


def pack_spans(table, keys, values):
    spec = pl.BlockSpec(memory_space=pl.ANY)
    return pl.pallas_call(
        pack_spans_kernel,
        in_specs=[pl.BlockSpec(memory_space=pltpu.SMEM), spec, spec],
        out_specs=[spec] * 8,
        out_shape=[jax.ShapeDtypeStruct((2, 2, CH, HD), bf16)] * 8,
        scratch_shapes=[pltpu.SemaphoreType.DMA((8, 2, 2))],
        compiler_params=params(),
        cost_estimate=cost(0, 16 << 20),
        name="pack_spans",
    )(table, keys, values)


def cross_kernel(far, tab_ref, q_ref, *refs):
    got = refs[:4]
    if far:
        out_ref, lse_ref, kbuf, vbuf, sems = refs[4:]
    else:
        part_ref, part_lse_ref, out_ref, kbuf, vbuf, sems = refs[4:]
    me = lax.axis_index("db")
    plane, z = me // NZ, me % NZ
    row = (1 - plane) * NZ + z if far else me
    here = []
    for r in range(8):
        owner = tab_ref[row, r]
        slot = jnp.int32(0)
        for earlier in range(r):
            slot = slot + jnp.where(tab_ref[row, earlier] == owner, 1, 0)
        here.append(jnp.where(owner // NZ == plane, 1, 0))
        shift = (z - owner % NZ + NZ) % NZ
        place = pl.ds((r % 2) * CH, CH)
        for k in range(4):

            @pl.when(shift == k)
            def _(k=k, slot=slot, place=place, r=r):
                pltpu.make_async_copy(got[k].at[slot, 0], kbuf.at[r // 2, place], sems.at[r, 0]).start()
                pltpu.make_async_copy(got[k].at[slot, 1], vbuf.at[r // 2, place], sems.at[r, 1]).start()

    lane = lax.broadcasted_iota(i32, (1, DH), 1)
    for n in range(4):
        for r in (2 * n, 2 * n + 1):
            place = pl.ds((r % 2) * CH, CH)
            pltpu.make_async_copy(got[0].at[0, 0], kbuf.at[n, place], sems.at[r, 0]).wait()
            pltpu.make_async_copy(got[0].at[0, 1], vbuf.at[n, place], sems.at[r, 1]).wait()
        mine = jnp.where(lane < CH, here[2 * n], here[2 * n + 1]) > 0
        toks = slice(n * CH, (n + 1) * CH)
        heads = [slice(h * DH, (h + 1) * DH) for h in range(NH)]
        s = [
            lax.dot_general(
                q_ref[toks, c], kbuf[n, :, c], (((1,), (1,)), ((), ())), preferred_element_type=f32
            )
            for c in heads
        ]
        s = [jnp.where(mine, x * SCALE, NEG) for x in s]
        top = [jnp.max(x, axis=1, keepdims=True) for x in s]
        p = [jnp.where(mine, jnp.exp2(x - t), 0.0) for x, t in zip(s, top)]
        total = [jnp.sum(x, axis=1, keepdims=True) for x in p]
        o = [jnp.dot(x.astype(bf16), vbuf[n, :, c], preferred_element_type=f32) for x, c in zip(p, heads)]
        if far:
            stats = jnp.full((CH, DH), NEG, f32)
            for h, c in enumerate(heads):
                safe = jnp.maximum(total[h], 1e-30)
                out_ref[toks, c] = (o[h] / safe).astype(bf16)
                lse = jnp.where(total[h] > 0, top[h] + jnp.log2(safe), NEG)
                stats = jnp.where(lane == h, lse, stats)
            lse_ref[toks, :] = stats
        else:
            for h, c in enumerate(heads):
                other = part_lse_ref[toks, h : h + 1]
                high = jnp.maximum(top[h], other)
                a, b = jnp.exp2(top[h] - high), jnp.exp2(other - high)
                mixed = o[h] * a + part_ref[toks, c].astype(f32) * b
                out_ref[toks, c] = (mixed / (total[h] * a + b)).astype(bf16)


def cross(far, table, q, got, part=()):
    vmem = pl.BlockSpec(memory_space=pltpu.VMEM)
    rows = jax.ShapeDtypeStruct((TOK, HD), bf16)
    stats = jax.ShapeDtypeStruct((TOK, DH), f32)
    return pl.pallas_call(
        functools.partial(cross_kernel, far),
        in_specs=[pl.BlockSpec(memory_space=pltpu.SMEM), vmem]
        + [pl.BlockSpec(memory_space=pl.ANY)] * 4
        + [vmem] * len(part),
        out_specs=[vmem, vmem] if far else vmem,
        out_shape=[rows, stats] if far else rows,
        scratch_shapes=[
            pltpu.VMEM((4, 2 * CH, HD), bf16),
            pltpu.VMEM((4, 2 * CH, HD), bf16),
            pltpu.SemaphoreType.DMA((8, 2)),
        ],
        compiler_params=params(),
        cost_estimate=cost(4 << 30, 6 << 20),
        name="cross_far" if far else "cross_near",
    )(table, q, *got, *part)


def per_device(queries, keys, values, doc_ids, nbr_owner, nbr_local, db_keys, db_values):
    q = queries[0]
    swap = [(d, (d + NZ) % 8) for d in range(8)]
    turn = lambda k: [(s * NZ + z, s * NZ + (z + k) % NZ) for s in range(2) for z in range(NZ)]
    far_q = lax.ppermute(q, "db", swap)

    asked = jnp.concatenate([nbr_owner[0].reshape(1, 8), nbr_local[0].reshape(1, 8)], axis=1)
    table = lax.all_gather(asked, "db", axis=0, tiled=True)
    packed = pack_spans(table, db_keys[0], db_values[0])
    near, far = list(packed[:4]), list(packed[4:])

    heads = pack_heads(doc_ids, q, keys[0], values[0])
    heads, far = lax.optimization_barrier((heads, far))
    far_got = [far[0]] + [lax.ppermute(far[k], "db", turn(k)) for k in (1, 2, 3)]
    heads = lax.all_to_all(heads, "ctx", split_axis=0, concat_axis=0, tiled=True)

    near, far_got = lax.optimization_barrier((near, far_got))
    near_got = [near[0]] + [lax.ppermute(near[k], "db", turn(k)) for k in (1, 2, 3)]
    part, lse = cross(True, table, far_q, far_got)
    part = lax.ppermute(part, "db", swap)
    lse = lax.ppermute(lse, "db", swap)

    self_rows = self_attention(heads)
    self_rows = lax.all_to_all(self_rows, "ctx", split_axis=0, concat_axis=0, tiled=True)
    self_rows = unpack_heads(self_rows)

    cross_rows = cross(False, table, q, near_got, (part, lse))
    return self_rows[None], cross_rows[None]


def solution(mesh):
    rows = P("db", "ctx", None)
    spans = P("db", "ctx", None, None)
    return jax.shard_map(
        per_device,
        mesh=mesh,
        in_specs=(rows, rows, rows, P("db", "ctx"), rows, rows, spans, spans),
        out_specs=(rows, rows),
        check_vma=False,
    )
```

```python
import functools
import math

import jax
import jax.numpy as jnp
from jax import lax
from jax.experimental import pallas as pl
from jax.experimental.pallas import tpu as pltpu
from jax.sharding import PartitionSpec as P

DH = 128
CH = 64
NH = 16
TOK = 256
HD = 2048
NZ = 4
NC = 16
QT = 512
CHUNK = 3 * TOK + 16
NEG = -1e30
SCALE = math.log2(math.e) / math.sqrt(DH)
VMEM = 48 << 20

f32, bf16, i32 = jnp.float32, jnp.bfloat16, jnp.int32


def params():
    return pltpu.CompilerParams(vmem_limit_bytes=VMEM)


def cost(flops, nbytes):
    return pl.CostEstimate(flops=flops // 64, bytes_accessed=nbytes // 16, transcendentals=0)


def pack_heads_kernel(docs_ref, q_ref, k_ref, v_ref, out_ref):
    row = lax.broadcasted_iota(i32, (16, DH), 0)
    docs = docs_ref[...]
    left = jnp.broadcast_to(docs[:, :DH], (16, DH))
    right = jnp.broadcast_to(docs[:, DH:], (16, DH))
    packed = jnp.where(row == 0, left, jnp.where(row == 1, right, 4)).astype(f32).astype(bf16)
    for h in range(4):
        cols = slice(h * DH, (h + 1) * DH)
        out_ref[h, 0:TOK, :] = q_ref[:, cols]
        out_ref[h, TOK : 2 * TOK, :] = k_ref[:, cols]
        out_ref[h, 2 * TOK : 3 * TOK, :] = v_ref[:, cols]
        out_ref[h, 3 * TOK : CHUNK, :] = packed


def pack_heads(docs, q, k, v):
    wide = pl.BlockSpec((TOK, 4 * DH), lambda i: (0, i))
    return pl.pallas_call(
        pack_heads_kernel,
        grid=(4,),
        in_specs=[pl.BlockSpec((1, TOK), lambda i: (0, 0)), wide, wide, wide],
        out_specs=pl.BlockSpec((4, CHUNK, DH), lambda i: (i, 0, 0)),
        out_shape=jax.ShapeDtypeStruct((NC, CHUNK, DH), bf16),
        compiler_params=params(),
        cost_estimate=cost(0, 6 << 20),
        name="pack_heads",
    )(docs, q, k, v)


def unpack_heads_kernel(x_ref, out_ref):
    for h in range(4):
        out_ref[:, h * DH : (h + 1) * DH] = x_ref[h]


def unpack_heads(x):
    return pl.pallas_call(
        unpack_heads_kernel,
        grid=(4,),
        in_specs=[pl.BlockSpec((4, TOK, DH), lambda i: (i, 0, 0))],
        out_specs=pl.BlockSpec((TOK, 4 * DH), lambda i: (0, i)),
        out_shape=jax.ShapeDtypeStruct((TOK, HD), bf16),
        compiler_params=params(),
        cost_estimate=cost(0, 2 << 20),
        name="unpack_heads",
    )(x)


def self_kernel(x_ref, o_ref):
    docs = x_ref[:, 3 * TOK : CHUNK, :].astype(f32)
    ends = [jnp.sum(jnp.where(docs < d - 0.5, 1.0, 0.0)).astype(i32) for d in (1, 2, 3)]

    def start_of(p):
        s = jnp.where(p >= ends[0], ends[0], 0)
        s = jnp.maximum(s, jnp.where(p >= ends[1], ends[1], 0))
        return jnp.maximum(s, jnp.where(p >= ends[2], ends[2], 0))

    def rows(j, part):
        return x_ref[pl.ds(2 * j, 2), part * TOK : (part + 1) * TOK, :].reshape(QT, DH)

    local = lax.broadcasted_iota(i32, (QT, QT), 1)
    column = lax.broadcasted_iota(i32, (QT, 1), 0)

    def scores(q, j):
        s = lax.dot_general(q, rows(j, 1), (((1,), (1,)), ((), ())), preferred_element_type=f32)
        return s * SCALE

    def lanes(p):
        return (p[:, :DH] + p[:, DH : 2 * DH]) + (p[:, 2 * DH : 3 * DH] + p[:, 3 * DH :])

    def mix(p, j):
        return jnp.dot(p.astype(bf16), rows(j, 2), preferred_element_type=f32)

    def query_tile(i, carry):
        base = i * QT
        q = rows(i, 0)
        first = start_of(base + column)
        lo = start_of(base) // QT
        mid = jnp.minimum((start_of(base + QT - 1) + QT - 1) // QT, i)

        s = scores(q, i)
        s = jnp.where((local <= column) & (local >= first - base), s, NEG)
        top = jnp.max(s, axis=1, keepdims=True)
        p = jnp.exp2(s - top)
        state = (mix(p, i), top, lanes(p))

        def step(j, state, masked):
            acc, top, total = state
            s = scores(q, j)
            if masked:
                s = jnp.where(local >= first - j * QT, s, NEG)
            new = jnp.maximum(top, jnp.max(s, axis=1, keepdims=True))
            p = jnp.exp2(s - new)
            fade = jnp.exp2(top - new)
            return acc * fade + mix(p, j), new, total * fade + lanes(p)

        state = lax.fori_loop(lo, mid, functools.partial(step, masked=True), state)
        acc, top, total = lax.fori_loop(mid, i, functools.partial(step, masked=False), state)
        out = acc / jnp.sum(total, axis=1, keepdims=True)
        o_ref[pl.ds(2 * i, 2)] = out.astype(bf16).reshape(2, TOK, DH)
        return carry

    lax.fori_loop(0, NC * TOK // QT, query_tile, 0)


def self_attention(x):
    return pl.pallas_call(
        self_kernel,
        in_specs=[pl.BlockSpec(memory_space=pltpu.VMEM)],
        out_specs=pl.BlockSpec(memory_space=pltpu.VMEM),
        out_shape=jax.ShapeDtypeStruct((NC, TOK, DH), bf16),
        compiler_params=params(),
        cost_estimate=cost(16 << 30, 4 << 20),
        name="self_attention",
    )(x)


SHIFTS = (1, 3, 2)


def pack_spans_kernel(far, tab_ref, keys_ref, values_ref, *refs):
    outs, sems = refs[:3], refs[3]
    me = lax.axis_index("db")
    plane, z = me // NZ, me % NZ
    side = 1 - plane if far else plane
    copies = []
    for i, k in enumerate(SHIFTS):
        asker = side * NZ + (z + k) % NZ
        first, second, seen = jnp.int32(0), jnp.int32(0), jnp.int32(0)
        for r in range(8):
            hit = tab_ref[asker, r // 2, r % 2] == me
            span = tab_ref[asker, r // 2, 2 + r % 2]
            first = jnp.where(hit & (seen == 0), span, first)
            second = jnp.where(hit & (seen == 1), span, second)
            seen = seen + jnp.where(hit, 1, 0)
        for slot, span in ((0, first), (1, second)):
            for kind, src in ((0, keys_ref), (1, values_ref)):
                copy = pltpu.make_async_copy(src.at[span], outs[i].at[slot, kind], sems.at[i, slot, kind])
                copy.start()
                copies.append(copy)
    for copy in copies:
        copy.wait()


def pack_spans(far, table, keys, values):
    anywhere = pl.BlockSpec(memory_space=pl.ANY)
    vmem = pl.BlockSpec(memory_space=pltpu.VMEM)
    return pl.pallas_call(
        functools.partial(pack_spans_kernel, far),
        in_specs=[pl.BlockSpec(memory_space=pltpu.SMEM), vmem, vmem],
        out_specs=[anywhere] * 3,
        out_shape=[jax.ShapeDtypeStruct((2, 2, CH, HD), bf16)] * 3,
        scratch_shapes=[pltpu.SemaphoreType.DMA((3, 2, 2))],
        compiler_params=params(),
        cost_estimate=cost(0, 7 << 20),
        name="pack_far" if far else "pack_near",
    )(table, keys, values)


def cross_kernel(far, tab_ref, q_ref, *refs):
    keys_ref, values_ref = refs[:2]
    got = refs[2:5]
    if far:
        out_ref, kbuf, vbuf, sems = refs[5:]
    else:
        part_ref, out_ref, kbuf, vbuf, sems = refs[5:]
    me = lax.axis_index("db")
    plane, z = me // NZ, me % NZ
    row = (1 - plane) * NZ + z if far else me
    here = []
    for r in range(8):
        owner = tab_ref[row, r // 2, r % 2]
        slot = jnp.int32(0)
        for earlier in range(r):
            slot = slot + jnp.where(tab_ref[row, earlier // 2, earlier % 2] == owner, 1, 0)
        here.append(jnp.where(owner // NZ == plane, 1, 0))
        shift = (z - owner % NZ + NZ) % NZ
        place = pl.ds((r % 2) * CH, CH)
        span = tab_ref[row, r // 2, 2 + r % 2]

        @pl.when(shift == 0)
        def _(span=span, place=place, r=r):
            pltpu.make_async_copy(keys_ref.at[span], kbuf.at[r // 2, place], sems.at[r, 0]).start()
            pltpu.make_async_copy(values_ref.at[span], vbuf.at[r // 2, place], sems.at[r, 1]).start()

        for i, k in enumerate(SHIFTS):

            @pl.when(shift == k)
            def _(i=i, slot=slot, place=place, r=r):
                pltpu.make_async_copy(got[i].at[slot, 0], kbuf.at[r // 2, place], sems.at[r, 0]).start()
                pltpu.make_async_copy(got[i].at[slot, 1], vbuf.at[r // 2, place], sems.at[r, 1]).start()

    lane = lax.broadcasted_iota(i32, (1, DH), 1)
    for n in range(4):
        for r in (2 * n, 2 * n + 1):
            place = pl.ds((r % 2) * CH, CH)
            pltpu.make_async_copy(keys_ref.at[0], kbuf.at[n, place], sems.at[r, 0]).wait()
            pltpu.make_async_copy(values_ref.at[0], vbuf.at[n, place], sems.at[r, 1]).wait()
        mine = jnp.where(lane < CH, here[2 * n], here[2 * n + 1]) > 0
        toks = slice(n * CH, (n + 1) * CH)
        heads = [slice(h * DH, (h + 1) * DH) for h in range(NH)]
        s = [
            lax.dot_general(
                q_ref[toks, c], kbuf[n, :, c], (((1,), (1,)), ((), ())), preferred_element_type=f32
            )
            for c in heads
        ]
        s = [jnp.where(mine, x * SCALE, NEG) for x in s]
        top = [jnp.max(x, axis=1, keepdims=True) for x in s]
        p = [jnp.where(mine, jnp.exp2(x - t), 0.0) for x, t in zip(s, top)]
        total = [jnp.sum(x, axis=1, keepdims=True) for x in p]
        o = [jnp.dot(x.astype(bf16), vbuf[n, :, c], preferred_element_type=f32) for x, c in zip(p, heads)]
        if far:
            stats = jnp.full((CH, DH), NEG, f32)
            for h, c in enumerate(heads):
                safe = jnp.maximum(total[h], 1e-30)
                out_ref[toks, c] = (o[h] / safe).astype(bf16)
                lse = jnp.where(total[h] > 0, top[h] + jnp.log2(safe), NEG)
                stats = jnp.where(lane % NH == h, lse, stats)
            high = stats.astype(bf16).astype(f32)
            low = (stats - high).astype(bf16).astype(f32)
            rest = stats - high - low
            stats = jnp.where(lane < NH, high, jnp.where(lane < 2 * NH, low, rest))
            out_ref[toks, HD:] = stats.astype(bf16)
        else:
            stats = part_ref[toks, HD:].astype(f32)
            lse = (stats[:, :NH] + stats[:, NH : 2 * NH]) + stats[:, 2 * NH : 3 * NH]
            for h, c in enumerate(heads):
                other = lse[:, h : h + 1]
                high = jnp.maximum(top[h], other)
                a, b = jnp.exp2(top[h] - high), jnp.exp2(other - high)
                mixed = o[h] * a + part_ref[toks, c].astype(f32) * b
                out_ref[toks, c] = (mixed / (total[h] * a + b)).astype(bf16)


def cross(far, table, q, keys, values, got, part=()):
    vmem = pl.BlockSpec(memory_space=pltpu.VMEM)
    return pl.pallas_call(
        functools.partial(cross_kernel, far),
        in_specs=[pl.BlockSpec(memory_space=pltpu.SMEM), vmem]
        + [pl.BlockSpec(memory_space=pl.ANY)] * 5
        + [vmem] * len(part),
        out_specs=vmem,
        out_shape=jax.ShapeDtypeStruct((TOK, HD + DH if far else HD), bf16),
        scratch_shapes=[
            pltpu.VMEM((4, 2 * CH, HD), bf16),
            pltpu.VMEM((4, 2 * CH, HD), bf16),
            pltpu.SemaphoreType.DMA((8, 2)),
        ],
        compiler_params=params(),
        cost_estimate=cost(4 << 30, 6 << 20),
        name="cross_far" if far else "cross_near",
    )(table, q, keys, values, *got, *part)


def per_device(queries, keys, values, doc_ids, nbr_owner, nbr_local, db_keys, db_values):
    q, db_k, db_v = queries[0], db_keys[0], db_values[0]
    swap = [(d, (d + NZ) % 8) for d in range(8)]
    turn = lambda k: [(s * NZ + z, s * NZ + (z + k) % NZ) for s in range(2) for z in range(NZ)]
    far_q = lax.ppermute(q, "db", swap)

    asked = jnp.concatenate([nbr_owner, nbr_local], axis=2)
    mine = lax.broadcasted_iota(i32, (8, 4, 4), 0) == lax.axis_index("db")
    table = lax.psum(jnp.where(mine, asked, 0), "db")
    far = pack_spans(True, table, db_k, db_v)
    far_got = [lax.ppermute(x, "db", turn(k)) for x, k in zip(far, SHIFTS)]

    heads = pack_heads(doc_ids, q, keys[0], values[0])
    heads = lax.all_to_all(heads, "ctx", split_axis=0, concat_axis=0, tiled=True)

    near = list(pack_spans(False, table, db_k, db_v))
    near_got = []
    for i, k in enumerate(SHIFTS):
        near[i], far_got[i] = lax.optimization_barrier((near[i], far_got[i]))
        near_got.append(lax.ppermute(near[i], "db", turn(k)))
    part = lax.ppermute(cross(True, table, far_q, db_k, db_v, far_got), "db", swap)

    self_rows = self_attention(heads)
    self_rows = lax.all_to_all(self_rows, "ctx", split_axis=0, concat_axis=0, tiled=True)
    self_rows = unpack_heads(self_rows)

    cross_rows = cross(False, table, q, db_k, db_v, near_got, (part,))
    return self_rows[None], cross_rows[None]


def solution(mesh):
    rows = P("db", "ctx", None)
    spans = P("db", "ctx", None, None)
    return jax.shard_map(
        per_device,
        mesh=mesh,
        in_specs=(rows, rows, rows, P("db", "ctx"), rows, rows, spans, spans),
        out_specs=(rows, rows),
        check_vma=False,
    )
```

```python
import functools
import math

import jax
import jax.numpy as jnp
from jax import lax
from jax.experimental import pallas as pl
from jax.experimental.pallas import tpu as pltpu
from jax.sharding import PartitionSpec as P

DH = 128
CH = 64
NH = 16
TOK = 256
HD = 2048
NZ = 4
NC = 16
QT = 512
CHUNK = 3 * TOK + 16
NEG = -1e30
SCALE = math.log2(math.e) / math.sqrt(DH)
VMEM = 48 << 20

f32, bf16, i32 = jnp.float32, jnp.bfloat16, jnp.int32


def params():
    return pltpu.CompilerParams(vmem_limit_bytes=VMEM)


def cost(flops, nbytes):
    return pl.CostEstimate(flops=flops // 64, bytes_accessed=nbytes // 16, transcendentals=0)


def pack_heads_kernel(token_ref, docs_ref, q_ref, k_ref, v_ref, out_ref):
    row = lax.broadcasted_iota(i32, (16, DH), 0)
    docs = docs_ref[...]
    left = jnp.broadcast_to(docs[:, :DH], (16, DH))
    right = jnp.broadcast_to(docs[:, DH:], (16, DH))
    packed = jnp.where(row == 0, left, jnp.where(row == 1, right, 4)).astype(f32).astype(bf16)
    for h in range(4):
        cols = slice(h * DH, (h + 1) * DH)
        out_ref[h, 0:TOK, :] = q_ref[:, cols]
        out_ref[h, TOK : 2 * TOK, :] = k_ref[:, cols]
        out_ref[h, 2 * TOK : 3 * TOK, :] = v_ref[:, cols]
        out_ref[h, 3 * TOK : CHUNK, :] = packed


def pack_heads(token, docs, q, k, v):
    wide = pl.BlockSpec((TOK, 4 * DH), lambda i: (0, i))
    return pl.pallas_call(
        pack_heads_kernel,
        grid=(4,),
        in_specs=[
            pl.BlockSpec((8, DH), lambda i: (0, 0)),
            pl.BlockSpec((1, TOK), lambda i: (0, 0)),
            wide,
            wide,
            wide,
        ],
        out_specs=pl.BlockSpec((4, CHUNK, DH), lambda i: (i, 0, 0)),
        out_shape=jax.ShapeDtypeStruct((NC, CHUNK, DH), bf16),
        compiler_params=params(),
        cost_estimate=cost(0, 6 << 20),
        name="pack_heads",
    )(token, docs, q, k, v)


def unpack_heads_kernel(x_ref, out_ref):
    for h in range(4):
        out_ref[:, h * DH : (h + 1) * DH] = x_ref[h]


def unpack_heads(x):
    return pl.pallas_call(
        unpack_heads_kernel,
        grid=(4,),
        in_specs=[pl.BlockSpec((4, TOK, DH), lambda i: (i, 0, 0))],
        out_specs=pl.BlockSpec((TOK, 4 * DH), lambda i: (0, i)),
        out_shape=jax.ShapeDtypeStruct((TOK, HD), bf16),
        compiler_params=params(),
        cost_estimate=cost(0, 2 << 20),
        name="unpack_heads",
    )(x)


def self_kernel(x_ref, o_ref):
    docs = x_ref[:, 3 * TOK : CHUNK, :].astype(f32)
    ends = [jnp.sum(jnp.where(docs < d - 0.5, 1.0, 0.0)).astype(i32) for d in (1, 2, 3)]

    def start_of(p):
        s = jnp.where(p >= ends[0], ends[0], 0)
        s = jnp.maximum(s, jnp.where(p >= ends[1], ends[1], 0))
        return jnp.maximum(s, jnp.where(p >= ends[2], ends[2], 0))

    def rows(j, part):
        return x_ref[pl.ds(2 * j, 2), part * TOK : (part + 1) * TOK, :].reshape(QT, DH)

    local = lax.broadcasted_iota(i32, (QT, QT), 1)
    column = lax.broadcasted_iota(i32, (QT, 1), 0)

    def scores(q, j):
        s = lax.dot_general(q, rows(j, 1), (((1,), (1,)), ((), ())), preferred_element_type=f32)
        return s * SCALE

    def lanes(p):
        return (p[:, :DH] + p[:, DH : 2 * DH]) + (p[:, 2 * DH : 3 * DH] + p[:, 3 * DH :])

    def mix(p, j):
        return jnp.dot(p.astype(bf16), rows(j, 2), preferred_element_type=f32)

    def query_tile(i, carry):
        base = i * QT
        q = rows(i, 0)
        first = start_of(base + column)
        lo = start_of(base) // QT
        mid = jnp.minimum((start_of(base + QT - 1) + QT - 1) // QT, i)

        s = scores(q, i)
        s = jnp.where((local <= column) & (local >= first - base), s, NEG)
        top = jnp.max(s, axis=1, keepdims=True)
        p = jnp.exp2(s - top)
        state = (mix(p, i), top, lanes(p))

        def step(j, state, masked):
            acc, top, total = state
            s = scores(q, j)
            if masked:
                s = jnp.where(local >= first - j * QT, s, NEG)
            new = jnp.maximum(top, jnp.max(s, axis=1, keepdims=True))
            p = jnp.exp2(s - new)
            fade = jnp.exp2(top - new)
            return acc * fade + mix(p, j), new, total * fade + lanes(p)

        state = lax.fori_loop(lo, mid, functools.partial(step, masked=True), state)
        acc, top, total = lax.fori_loop(mid, i, functools.partial(step, masked=False), state)
        out = acc / jnp.sum(total, axis=1, keepdims=True)
        o_ref[pl.ds(2 * i, 2)] = out.astype(bf16).reshape(2, TOK, DH)
        return carry

    lax.fori_loop(0, NC * TOK // QT, query_tile, 0)


def self_attention(x):
    return pl.pallas_call(
        self_kernel,
        in_specs=[pl.BlockSpec(memory_space=pltpu.VMEM)],
        out_specs=pl.BlockSpec(memory_space=pltpu.VMEM),
        out_shape=jax.ShapeDtypeStruct((NC, TOK, DH), bf16),
        compiler_params=params(),
        cost_estimate=cost(16 << 30, 4 << 20),
        name="self_attention",
    )(x)


SHIFTS = (1, 3, 2)


def pack_spans_kernel(far, tab_ref, keys_ref, values_ref, *refs):
    outs, token_ref, sems = refs[:3], refs[3], refs[4]
    token_ref[...] = jnp.zeros_like(token_ref)
    me = lax.axis_index("db")
    plane, z = me // NZ, me % NZ
    side = 1 - plane if far else plane
    copies = []
    for i, k in enumerate(SHIFTS):
        asker = side * NZ + (z + k) % NZ
        first, second, seen = jnp.int32(0), jnp.int32(0), jnp.int32(0)
        for r in range(8):
            hit = tab_ref[asker, r // 2, r % 2] == me
            span = tab_ref[asker, r // 2, 2 + r % 2]
            first = jnp.where(hit & (seen == 0), span, first)
            second = jnp.where(hit & (seen == 1), span, second)
            seen = seen + jnp.where(hit, 1, 0)
        for slot, span in ((0, first), (1, second)):
            for kind, src in ((0, keys_ref), (1, values_ref)):
                copy = pltpu.make_async_copy(src.at[span], outs[i].at[slot, kind], sems.at[i, slot, kind])
                copy.start()
                copies.append(copy)
    for copy in copies:
        copy.wait()


def pack_spans(far, table, keys, values):
    anywhere = pl.BlockSpec(memory_space=pl.ANY)
    vmem = pl.BlockSpec(memory_space=pltpu.VMEM)
    return pl.pallas_call(
        functools.partial(pack_spans_kernel, far),
        in_specs=[pl.BlockSpec(memory_space=pltpu.SMEM), vmem, vmem],
        out_specs=[anywhere] * 3 + [vmem],
        out_shape=[jax.ShapeDtypeStruct((2, 2, CH, HD), bf16)] * 3 + [jax.ShapeDtypeStruct((8, DH), i32)],
        scratch_shapes=[pltpu.SemaphoreType.DMA((3, 2, 2))],
        compiler_params=params(),
        cost_estimate=cost(0, 7 << 20),
        name="pack_far" if far else "pack_near",
    )(table, keys, values)


def cross_kernel(far, tab_ref, q_ref, *refs):
    keys_ref, values_ref = refs[:2]
    got = refs[2:5]
    if far:
        out_ref, kbuf, vbuf, sems = refs[5:]
    else:
        part_ref, out_ref, kbuf, vbuf, sems = refs[5:]
    me = lax.axis_index("db")
    plane, z = me // NZ, me % NZ
    row = (1 - plane) * NZ + z if far else me
    here = []
    for r in range(8):
        owner = tab_ref[row, r // 2, r % 2]
        slot = jnp.int32(0)
        for earlier in range(r):
            slot = slot + jnp.where(tab_ref[row, earlier // 2, earlier % 2] == owner, 1, 0)
        here.append(jnp.where(owner // NZ == plane, 1, 0))
        shift = (z - owner % NZ + NZ) % NZ
        place = pl.ds((r % 2) * CH, CH)
        span = tab_ref[row, r // 2, 2 + r % 2]

        @pl.when(shift == 0)
        def _(span=span, place=place, r=r):
            pltpu.make_async_copy(keys_ref.at[span], kbuf.at[r // 2, place], sems.at[r, 0]).start()
            pltpu.make_async_copy(values_ref.at[span], vbuf.at[r // 2, place], sems.at[r, 1]).start()

        for i, k in enumerate(SHIFTS):

            @pl.when(shift == k)
            def _(i=i, slot=slot, place=place, r=r):
                pltpu.make_async_copy(got[i].at[slot, 0], kbuf.at[r // 2, place], sems.at[r, 0]).start()
                pltpu.make_async_copy(got[i].at[slot, 1], vbuf.at[r // 2, place], sems.at[r, 1]).start()

    lane = lax.broadcasted_iota(i32, (1, DH), 1)
    for n in range(4):
        for r in (2 * n, 2 * n + 1):
            place = pl.ds((r % 2) * CH, CH)
            pltpu.make_async_copy(keys_ref.at[0], kbuf.at[n, place], sems.at[r, 0]).wait()
            pltpu.make_async_copy(values_ref.at[0], vbuf.at[n, place], sems.at[r, 1]).wait()
        mine = jnp.where(lane < CH, here[2 * n], here[2 * n + 1]) > 0
        toks = slice(n * CH, (n + 1) * CH)
        heads = [slice(h * DH, (h + 1) * DH) for h in range(NH)]
        s = [
            lax.dot_general(
                q_ref[toks, c], kbuf[n, :, c], (((1,), (1,)), ((), ())), preferred_element_type=f32
            )
            for c in heads
        ]
        s = [jnp.where(mine, x * SCALE, NEG) for x in s]
        top = [jnp.max(x, axis=1, keepdims=True) for x in s]
        p = [jnp.where(mine, jnp.exp2(x - t), 0.0) for x, t in zip(s, top)]
        total = [jnp.sum(x, axis=1, keepdims=True) for x in p]
        o = [jnp.dot(x.astype(bf16), vbuf[n, :, c], preferred_element_type=f32) for x, c in zip(p, heads)]
        if far:
            stats = jnp.full((CH, DH), NEG, f32)
            for h, c in enumerate(heads):
                safe = jnp.maximum(total[h], 1e-30)
                out_ref[toks, c] = (o[h] / safe).astype(bf16)
                lse = jnp.where(total[h] > 0, top[h] + jnp.log2(safe), NEG)
                stats = jnp.where(lane % NH == h, lse, stats)
            high = stats.astype(bf16).astype(f32)
            low = (stats - high).astype(bf16).astype(f32)
            rest = stats - high - low
            stats = jnp.where(lane < NH, high, jnp.where(lane < 2 * NH, low, rest))
            out_ref[toks, HD:] = stats.astype(bf16)
        else:
            stats = part_ref[toks, HD:].astype(f32)
            lse = (stats[:, :NH] + stats[:, NH : 2 * NH]) + stats[:, 2 * NH : 3 * NH]
            for h, c in enumerate(heads):
                other = lse[:, h : h + 1]
                high = jnp.maximum(top[h], other)
                a, b = jnp.exp2(top[h] - high), jnp.exp2(other - high)
                mixed = o[h] * a + part_ref[toks, c].astype(f32) * b
                out_ref[toks, c] = (mixed / (total[h] * a + b)).astype(bf16)


def cross(far, table, q, keys, values, got, part=()):
    vmem = pl.BlockSpec(memory_space=pltpu.VMEM)
    return pl.pallas_call(
        functools.partial(cross_kernel, far),
        in_specs=[pl.BlockSpec(memory_space=pltpu.SMEM), vmem]
        + [pl.BlockSpec(memory_space=pl.ANY)] * 5
        + [vmem] * len(part),
        out_specs=vmem,
        out_shape=jax.ShapeDtypeStruct((TOK, HD + DH if far else HD), bf16),
        scratch_shapes=[
            pltpu.VMEM((4, 2 * CH, HD), bf16),
            pltpu.VMEM((4, 2 * CH, HD), bf16),
            pltpu.SemaphoreType.DMA((8, 2)),
        ],
        compiler_params=params(),
        cost_estimate=cost(4 << 30, 6 << 20),
        name="cross_far" if far else "cross_near",
    )(table, q, keys, values, *got, *part)


def arrived_kernel(*refs):
    pass


def arrived(xs):
    anywhere = pl.BlockSpec(memory_space=pl.ANY)
    return pl.pallas_call(
        arrived_kernel,
        in_specs=[anywhere] * len(xs),
        out_specs=[anywhere] * len(xs),
        out_shape=[jax.ShapeDtypeStruct(x.shape, x.dtype) for x in xs],
        input_output_aliases={i: i for i in range(len(xs))},
        compiler_params=params(),
        cost_estimate=pl.CostEstimate(flops=32 << 30, bytes_accessed=0, transcendentals=0),
        name="arrived",
    )(*xs)


def per_device(queries, keys, values, doc_ids, nbr_owner, nbr_local, db_keys, db_values):
    q, db_k, db_v = queries[0], db_keys[0], db_values[0]
    swap = [(d, (d + NZ) % 8) for d in range(8)]
    turn = lambda k: [(s * NZ + z, s * NZ + (z + k) % NZ) for s in range(2) for z in range(NZ)]
    far_q = lax.ppermute(q, "db", swap)

    asked = jnp.concatenate([nbr_owner, nbr_local], axis=2)
    mine = lax.broadcasted_iota(i32, (8, 4, 4), 0) == lax.axis_index("db")
    table = lax.psum(jnp.where(mine, asked, 0), "db")
    *far, token = pack_spans(True, table, db_k, db_v)
    far_got = [lax.ppermute(x, "db", turn(k)) for x, k in zip(far, SHIFTS)]

    heads = pack_heads(token, doc_ids, q, keys[0], values[0])
    heads = lax.all_to_all(heads, "ctx", split_axis=0, concat_axis=0, tiled=True)

    near = list(pack_spans(False, table, db_k, db_v)[:3])
    near_got = []
    for i, k in enumerate(SHIFTS):
        near[i], far_got[i] = lax.optimization_barrier((near[i], far_got[i]))
        near_got.append(lax.ppermute(near[i], "db", turn(k)))
    part = lax.ppermute(cross(True, table, far_q, db_k, db_v, far_got), "db", swap)

    self_rows = self_attention(heads)
    self_rows = lax.all_to_all(self_rows, "ctx", split_axis=0, concat_axis=0, tiled=True)
    self_rows = unpack_heads(self_rows)

    near_got = arrived(near_got)
    cross_rows = cross(False, table, q, db_k, db_v, near_got, (part,))
    return self_rows[None], cross_rows[None]


def solution(mesh):
    rows = P("db", "ctx", None)
    spans = P("db", "ctx", None, None)
    return jax.shard_map(
        per_device,
        mesh=mesh,
        in_specs=(rows, rows, rows, P("db", "ctx"), rows, rows, spans, spans),
        out_specs=(rows, rows),
        check_vma=False,
    )
```

```python
import functools
import math

import jax
import jax.numpy as jnp
from jax import lax
from jax.experimental import pallas as pl
from jax.experimental.pallas import tpu as pltpu
from jax.sharding import PartitionSpec as P

DH = 128
CH = 64
NH = 16
TOK = 256
HD = 2048
NZ = 4
NC = 16
QT = 512
CHUNK = 3 * TOK + 16
NEG = -1e30
SCALE = math.log2(math.e) / math.sqrt(DH)
VMEM = 48 << 20

f32, bf16, i32 = jnp.float32, jnp.bfloat16, jnp.int32


def params():
    return pltpu.CompilerParams(vmem_limit_bytes=VMEM)


def cost(flops, nbytes):
    return pl.CostEstimate(flops=flops // 64, bytes_accessed=nbytes // 16, transcendentals=0)


def pack_heads_kernel(token_ref, docs_ref, q_ref, k_ref, v_ref, out_ref):
    row = lax.broadcasted_iota(i32, (16, DH), 0)
    docs = docs_ref[...]
    left = jnp.broadcast_to(docs[:, :DH], (16, DH))
    right = jnp.broadcast_to(docs[:, DH:], (16, DH))
    packed = jnp.where(row == 0, left, jnp.where(row == 1, right, 4)).astype(f32).astype(bf16)
    for h in range(4):
        cols = slice(h * DH, (h + 1) * DH)
        out_ref[h, 0:TOK, :] = q_ref[:, cols]
        out_ref[h, TOK : 2 * TOK, :] = k_ref[:, cols]
        out_ref[h, 2 * TOK : 3 * TOK, :] = v_ref[:, cols]
        out_ref[h, 3 * TOK : CHUNK, :] = packed


def pack_heads(token, docs, q, k, v):
    wide = pl.BlockSpec((TOK, 4 * DH), lambda i: (0, i))
    return pl.pallas_call(
        pack_heads_kernel,
        grid=(4,),
        in_specs=[
            pl.BlockSpec((8, DH), lambda i: (0, 0)),
            pl.BlockSpec((1, TOK), lambda i: (0, 0)),
            wide,
            wide,
            wide,
        ],
        out_specs=pl.BlockSpec((4, CHUNK, DH), lambda i: (i, 0, 0)),
        out_shape=jax.ShapeDtypeStruct((NC, CHUNK, DH), bf16),
        compiler_params=params(),
        cost_estimate=cost(0, 6 << 20),
        name="pack_heads",
    )(token, docs, q, k, v)


def unpack_heads_kernel(x_ref, out_ref):
    for h in range(4):
        out_ref[:, h * DH : (h + 1) * DH] = x_ref[h]


def unpack_heads(x):
    return pl.pallas_call(
        unpack_heads_kernel,
        grid=(4,),
        in_specs=[pl.BlockSpec((4, TOK, DH), lambda i: (i, 0, 0))],
        out_specs=pl.BlockSpec((TOK, 4 * DH), lambda i: (0, i)),
        out_shape=jax.ShapeDtypeStruct((TOK, HD), bf16),
        compiler_params=params(),
        cost_estimate=cost(0, 2 << 20),
        name="unpack_heads",
    )(x)


def self_kernel(x_ref, o_ref):
    docs = x_ref[:, 3 * TOK : CHUNK, :].astype(f32)
    ends = [jnp.sum(jnp.where(docs < d - 0.5, 1.0, 0.0)).astype(i32) for d in (1, 2, 3)]

    def start_of(p):
        s = jnp.where(p >= ends[0], ends[0], 0)
        s = jnp.maximum(s, jnp.where(p >= ends[1], ends[1], 0))
        return jnp.maximum(s, jnp.where(p >= ends[2], ends[2], 0))

    def rows(j, part):
        return x_ref[pl.ds(2 * j, 2), part * TOK : (part + 1) * TOK, :].reshape(QT, DH)

    local = lax.broadcasted_iota(i32, (QT, QT), 1)
    column = lax.broadcasted_iota(i32, (QT, 1), 0)

    def scores(q, j):
        s = lax.dot_general(q, rows(j, 1), (((1,), (1,)), ((), ())), preferred_element_type=f32)
        return s * SCALE

    def lanes(p):
        return (p[:, :DH] + p[:, DH : 2 * DH]) + (p[:, 2 * DH : 3 * DH] + p[:, 3 * DH :])

    def mix(p, j):
        return jnp.dot(p.astype(bf16), rows(j, 2), preferred_element_type=f32)

    def query_tile(i, carry):
        base = i * QT
        q = rows(i, 0)
        first = start_of(base + column)
        lo = start_of(base) // QT
        mid = jnp.minimum((start_of(base + QT - 1) + QT - 1) // QT, i)

        s = scores(q, i)
        s = jnp.where((local <= column) & (local >= first - base), s, NEG)
        top = jnp.max(s, axis=1, keepdims=True)
        p = jnp.exp2(s - top)
        state = (mix(p, i), top, lanes(p))

        def step(j, state, masked):
            acc, top, total = state
            s = scores(q, j)
            if masked:
                s = jnp.where(local >= first - j * QT, s, NEG)
            new = jnp.maximum(top, jnp.max(s, axis=1, keepdims=True))
            p = jnp.exp2(s - new)
            fade = jnp.exp2(top - new)
            return acc * fade + mix(p, j), new, total * fade + lanes(p)

        state = lax.fori_loop(lo, mid, functools.partial(step, masked=True), state)
        acc, top, total = lax.fori_loop(mid, i, functools.partial(step, masked=False), state)
        out = acc / jnp.sum(total, axis=1, keepdims=True)
        o_ref[pl.ds(2 * i, 2)] = out.astype(bf16).reshape(2, TOK, DH)
        return carry

    lax.fori_loop(0, NC * TOK // QT, query_tile, 0)


def self_attention(x):
    return pl.pallas_call(
        self_kernel,
        in_specs=[pl.BlockSpec(memory_space=pltpu.VMEM)],
        out_specs=pl.BlockSpec(memory_space=pltpu.VMEM),
        out_shape=jax.ShapeDtypeStruct((NC, TOK, DH), bf16),
        compiler_params=params(),
        cost_estimate=cost(16 << 30, 4 << 20),
        name="self_attention",
    )(x)


SHIFTS = (1, 3, 2)


def pack_spans_kernel(far, *refs):
    tabs, keys_ref, values_ref = refs[:3], refs[3], refs[4]
    outs, token_ref, sems = refs[5:8], refs[8], refs[9]
    token_ref[...] = jnp.zeros_like(token_ref)
    me = lax.axis_index("db")
    copies = []
    for i in range(3):
        first, second, seen = jnp.int32(0), jnp.int32(0), jnp.int32(0)
        for r in range(8):
            hit = tabs[i][far, r // 2, r % 2] == me
            span = tabs[i][far, r // 2, 2 + r % 2]
            first = jnp.where(hit & (seen == 0), span, first)
            second = jnp.where(hit & (seen == 1), span, second)
            seen = seen + jnp.where(hit, 1, 0)
        for slot, span in ((0, first), (1, second)):
            for kind, src in ((0, keys_ref), (1, values_ref)):
                copy = pltpu.make_async_copy(src.at[span], outs[i].at[slot, kind], sems.at[i, slot, kind])
                copy.start()
                copies.append(copy)
    for copy in copies:
        copy.wait()


def pack_spans(far, tables, keys, values):
    anywhere = pl.BlockSpec(memory_space=pl.ANY)
    vmem = pl.BlockSpec(memory_space=pltpu.VMEM)
    return pl.pallas_call(
        functools.partial(pack_spans_kernel, int(far)),
        in_specs=[pl.BlockSpec(memory_space=pltpu.SMEM)] * 3 + [vmem, vmem],
        out_specs=[anywhere] * 3 + [vmem],
        out_shape=[jax.ShapeDtypeStruct((2, 2, CH, HD), bf16)] * 3 + [jax.ShapeDtypeStruct((8, DH), i32)],
        scratch_shapes=[pltpu.SemaphoreType.DMA((3, 2, 2))],
        compiler_params=params(),
        cost_estimate=cost(0, 7 << 20),
        name="pack_far" if far else "pack_near",
    )(*tables, keys, values)


def cross_kernel(far, tab_ref, q_ref, *refs):
    keys_ref, values_ref = refs[:2]
    got = refs[2:5]
    if far:
        out_ref, kbuf, vbuf, sems = refs[5:]
    else:
        part_ref, out_ref, kbuf, vbuf, sems = refs[5:]
    me = lax.axis_index("db")
    plane, z = me // NZ, me % NZ
    row = 1 if far else 0
    here = []
    for r in range(8):
        owner = tab_ref[row, r // 2, r % 2]
        slot = jnp.int32(0)
        for earlier in range(r):
            slot = slot + jnp.where(tab_ref[row, earlier // 2, earlier % 2] == owner, 1, 0)
        here.append(jnp.where(owner // NZ == plane, 1, 0))
        shift = (z - owner % NZ + NZ) % NZ
        place = pl.ds((r % 2) * CH, CH)
        span = tab_ref[row, r // 2, 2 + r % 2]

        @pl.when(shift == 0)
        def _(span=span, place=place, r=r):
            pltpu.make_async_copy(keys_ref.at[span], kbuf.at[r // 2, place], sems.at[r, 0]).start()
            pltpu.make_async_copy(values_ref.at[span], vbuf.at[r // 2, place], sems.at[r, 1]).start()

        for i, k in enumerate(SHIFTS):

            @pl.when(shift == k)
            def _(i=i, slot=slot, place=place, r=r):
                pltpu.make_async_copy(got[i].at[slot, 0], kbuf.at[r // 2, place], sems.at[r, 0]).start()
                pltpu.make_async_copy(got[i].at[slot, 1], vbuf.at[r // 2, place], sems.at[r, 1]).start()

    lane = lax.broadcasted_iota(i32, (1, DH), 1)
    for n in range(4):
        for r in (2 * n, 2 * n + 1):
            place = pl.ds((r % 2) * CH, CH)
            pltpu.make_async_copy(keys_ref.at[0], kbuf.at[n, place], sems.at[r, 0]).wait()
            pltpu.make_async_copy(values_ref.at[0], vbuf.at[n, place], sems.at[r, 1]).wait()
        mine = jnp.where(lane < CH, here[2 * n], here[2 * n + 1]) > 0
        toks = slice(n * CH, (n + 1) * CH)
        heads = [slice(h * DH, (h + 1) * DH) for h in range(NH)]
        s = [
            lax.dot_general(
                q_ref[toks, c], kbuf[n, :, c], (((1,), (1,)), ((), ())), preferred_element_type=f32
            )
            for c in heads
        ]
        s = [jnp.where(mine, x * SCALE, NEG) for x in s]
        top = [jnp.max(x, axis=1, keepdims=True) for x in s]
        p = [jnp.where(mine, jnp.exp2(x - t), 0.0) for x, t in zip(s, top)]
        total = [jnp.sum(x, axis=1, keepdims=True) for x in p]
        o = [jnp.dot(x.astype(bf16), vbuf[n, :, c], preferred_element_type=f32) for x, c in zip(p, heads)]
        if far:
            stats = jnp.full((CH, DH), NEG, f32)
            for h, c in enumerate(heads):
                safe = jnp.maximum(total[h], 1e-30)
                out_ref[toks, c] = (o[h] / safe).astype(bf16)
                lse = jnp.where(total[h] > 0, top[h] + jnp.log2(safe), NEG)
                stats = jnp.where(lane % NH == h, lse, stats)
            high = stats.astype(bf16).astype(f32)
            low = (stats - high).astype(bf16).astype(f32)
            rest = stats - high - low
            stats = jnp.where(lane < NH, high, jnp.where(lane < 2 * NH, low, rest))
            out_ref[toks, HD:] = stats.astype(bf16)
        else:
            stats = part_ref[toks, HD:].astype(f32)
            lse = (stats[:, :NH] + stats[:, NH : 2 * NH]) + stats[:, 2 * NH : 3 * NH]
            for h, c in enumerate(heads):
                other = lse[:, h : h + 1]
                high = jnp.maximum(top[h], other)
                a, b = jnp.exp2(top[h] - high), jnp.exp2(other - high)
                mixed = o[h] * a + part_ref[toks, c].astype(f32) * b
                out_ref[toks, c] = (mixed / (total[h] * a + b)).astype(bf16)


def cross(far, table, q, keys, values, got, part=()):
    vmem = pl.BlockSpec(memory_space=pltpu.VMEM)
    return pl.pallas_call(
        functools.partial(cross_kernel, far),
        in_specs=[pl.BlockSpec(memory_space=pltpu.SMEM), vmem]
        + [pl.BlockSpec(memory_space=pl.ANY)] * 5
        + [vmem] * len(part),
        out_specs=vmem,
        out_shape=jax.ShapeDtypeStruct((TOK, HD + DH if far else HD), bf16),
        scratch_shapes=[
            pltpu.VMEM((4, 2 * CH, HD), bf16),
            pltpu.VMEM((4, 2 * CH, HD), bf16),
            pltpu.SemaphoreType.DMA((8, 2)),
        ],
        compiler_params=params(),
        cost_estimate=pl.CostEstimate(flops=32 << 30 if far else 1 << 26, bytes_accessed=0, transcendentals=0),
        name="cross_far" if far else "cross_near",
    )(table, q, keys, values, *got, *part)


def arrived_kernel(*refs):
    pass


def arrived(xs):
    anywhere = pl.BlockSpec(memory_space=pl.ANY)
    return pl.pallas_call(
        arrived_kernel,
        in_specs=[anywhere] * len(xs),
        out_specs=[anywhere] * len(xs),
        out_shape=[jax.ShapeDtypeStruct(x.shape, x.dtype) for x in xs],
        input_output_aliases={i: i for i in range(len(xs))},
        compiler_params=params(),
        cost_estimate=pl.CostEstimate(flops=32 << 30, bytes_accessed=0, transcendentals=0),
        name="arrived",
    )(*xs)


def per_device(queries, keys, values, doc_ids, nbr_owner, nbr_local, db_keys, db_values):
    q, db_k, db_v = queries[0], db_keys[0], db_values[0]
    swap = [(d, (d + NZ) % 8) for d in range(8)]
    turn = lambda k: [(s * NZ + z, s * NZ + (z + k) % NZ) for s in range(2) for z in range(NZ)]
    far_q = lax.ppermute(q, "db", swap)

    asked = jnp.concatenate([nbr_owner, nbr_local], axis=2)
    table = jnp.concatenate([asked, lax.ppermute(asked, "db", swap)], axis=0)
    tables = [lax.ppermute(table, "db", turn(NZ - k)) for k in SHIFTS]
    *far, token = pack_spans(True, tables, db_k, db_v)
    far_got = [lax.ppermute(x, "db", turn(k)) for x, k in zip(far, SHIFTS)]

    heads = pack_heads(token, doc_ids, q, keys[0], values[0])
    heads = lax.all_to_all(heads, "ctx", split_axis=0, concat_axis=0, tiled=True)

    near = list(pack_spans(False, tables, db_k, db_v)[:3])
    near_got = []
    for i, k in enumerate(SHIFTS):
        near[i], far_got[i] = lax.optimization_barrier((near[i], far_got[i]))
        near_got.append(lax.ppermute(near[i], "db", turn(k)))
    part = lax.ppermute(cross(True, table, far_q, db_k, db_v, far_got), "db", swap)

    self_rows = self_attention(heads)
    self_rows = lax.all_to_all(self_rows, "ctx", split_axis=0, concat_axis=0, tiled=True)
    self_rows = unpack_heads(self_rows)

    near_got = arrived(near_got)
    cross_rows = cross(False, table, q, db_k, db_v, near_got, (part,))
    return self_rows[None], cross_rows[None]


def solution(mesh):
    rows = P("db", "ctx", None)
    spans = P("db", "ctx", None, None)
    return jax.shard_map(
        per_device,
        mesh=mesh,
        in_specs=(rows, rows, rows, P("db", "ctx"), rows, rows, spans, spans),
        out_specs=(rows, rows),
        check_vma=False,
    )
```

```python
import functools
import math

import jax
import jax.numpy as jnp
from jax import lax
from jax.experimental import pallas as pl
from jax.experimental.pallas import tpu as pltpu
from jax.sharding import PartitionSpec as P

DH = 128
CH = 64
NH = 16
TOK = 256
HD = 2048
NZ = 4
NC = 16
QT = 1024
CHUNK = 3 * TOK + 16
NEG = -1e30
SCALE = math.log2(math.e) / math.sqrt(DH)
VMEM = 48 << 20

f32, bf16, i32 = jnp.float32, jnp.bfloat16, jnp.int32


def params():
    return pltpu.CompilerParams(vmem_limit_bytes=VMEM)


def cost(flops, nbytes):
    return pl.CostEstimate(flops=flops // 64, bytes_accessed=nbytes // 16, transcendentals=0)


def pack_heads_kernel(token_ref, docs_ref, q_ref, k_ref, v_ref, out_ref):
    row = lax.broadcasted_iota(i32, (16, DH), 0)
    docs = docs_ref[...]
    left = jnp.broadcast_to(docs[:, :DH], (16, DH))
    right = jnp.broadcast_to(docs[:, DH:], (16, DH))
    packed = jnp.where(row == 0, left, jnp.where(row == 1, right, 4)).astype(f32).astype(bf16)
    for h in range(4):
        cols = slice(h * DH, (h + 1) * DH)
        out_ref[h, 0:TOK, :] = q_ref[:, cols]
        out_ref[h, TOK : 2 * TOK, :] = k_ref[:, cols]
        out_ref[h, 2 * TOK : 3 * TOK, :] = v_ref[:, cols]
        out_ref[h, 3 * TOK : CHUNK, :] = packed


def pack_heads(token, docs, q, k, v):
    wide = pl.BlockSpec((TOK, 4 * DH), lambda i: (0, i))
    return pl.pallas_call(
        pack_heads_kernel,
        grid=(4,),
        in_specs=[
            pl.BlockSpec((2, 4, 4), lambda i: (0, 0, 0)),
            pl.BlockSpec((1, TOK), lambda i: (0, 0)),
            wide,
            wide,
            wide,
        ],
        out_specs=pl.BlockSpec((4, CHUNK, DH), lambda i: (i, 0, 0)),
        out_shape=jax.ShapeDtypeStruct((NC, CHUNK, DH), bf16),
        compiler_params=params(),
        cost_estimate=cost(0, 6 << 20),
        name="pack_heads",
    )(token, docs, q, k, v)


def unpack_heads_kernel(x_ref, out_ref):
    for h in range(4):
        out_ref[:, h * DH : (h + 1) * DH] = x_ref[h]


def unpack_heads(x):
    return pl.pallas_call(
        unpack_heads_kernel,
        grid=(4,),
        in_specs=[pl.BlockSpec((4, TOK, DH), lambda i: (i, 0, 0))],
        out_specs=pl.BlockSpec((TOK, 4 * DH), lambda i: (0, i)),
        out_shape=jax.ShapeDtypeStruct((TOK, HD), bf16),
        compiler_params=params(),
        cost_estimate=cost(0, 2 << 20),
        name="unpack_heads",
    )(x)


def self_kernel(x_ref, o_ref):
    docs = x_ref[:, 3 * TOK : CHUNK, :].astype(f32)
    ends = [jnp.sum(jnp.where(docs < d - 0.5, 1.0, 0.0)).astype(i32) for d in (1, 2, 3)]
    per = QT // TOK

    def start_of(p):
        s = jnp.where(p >= ends[0], ends[0], 0)
        s = jnp.maximum(s, jnp.where(p >= ends[1], ends[1], 0))
        return jnp.maximum(s, jnp.where(p >= ends[2], ends[2], 0))

    def rows(j, part):
        return x_ref[pl.ds(per * j, per), part * TOK : (part + 1) * TOK, :].reshape(QT, DH)

    def lanes(p):
        return sum(p[:, c : c + DH] for c in range(0, p.shape[1], DH))

    def query_tile(i, carry):
        base = i * QT
        qs = [x_ref[per * i + u, 0:TOK, :] for u in range(per)]
        columns = [lax.broadcasted_iota(i32, (TOK, 1), 0) + u * TOK for u in range(per)]
        firsts = [start_of(base + c) for c in columns]
        lo = start_of(base) // QT
        mid = jnp.minimum((start_of(base + QT - 1) + QT - 1) // QT, i)

        def step(j, state, kind):
            k, v = rows(j, 1), rows(j, 2)
            ss = []
            for u in range(per):
                width = (u + 1) * TOK if kind == "diagonal" else QT
                s = lax.dot_general(qs[u], k[:width], (((1,), (1,)), ((), ())), preferred_element_type=f32)
                s = s * SCALE
                if kind != "open":
                    local = lax.broadcasted_iota(i32, (TOK, width), 1)
                    seen = local >= firsts[u] - j * QT
                    if kind == "diagonal":
                        seen = seen & (local <= columns[u])
                    s = jnp.where(seen, s, NEG)
                ss.append(s)
            out = []
            for u, s in enumerate(ss):
                new = jnp.max(s, axis=1, keepdims=True)
                if state is not None:
                    acc, top, total = state[u]
                    new = jnp.maximum(top, new)
                p = jnp.exp2(s - new)
                mixed = jnp.dot(p.astype(bf16), v[: s.shape[1]], preferred_element_type=f32)
                weight = lanes(p)
                if state is not None:
                    fade = jnp.exp2(top - new)
                    mixed = acc * fade + mixed
                    weight = total * fade + weight
                out.append((mixed, new, weight))
            return tuple(out)

        state = step(i, None, "diagonal")
        state = lax.fori_loop(lo, mid, functools.partial(step, kind="masked"), state)
        state = lax.fori_loop(mid, i, functools.partial(step, kind="open"), state)
        for u, (acc, top, total) in enumerate(state):
            o_ref[per * i + u] = (acc / jnp.sum(total, axis=1, keepdims=True)).astype(bf16)
        return carry

    lax.fori_loop(0, NC * TOK // QT, query_tile, 0)


def self_attention(x):
    return pl.pallas_call(
        self_kernel,
        in_specs=[pl.BlockSpec(memory_space=pltpu.VMEM)],
        out_specs=pl.BlockSpec(memory_space=pltpu.VMEM),
        out_shape=jax.ShapeDtypeStruct((NC, TOK, DH), bf16),
        compiler_params=params(),
        cost_estimate=cost(16 << 30, 4 << 20),
        name="self_attention",
    )(x)


SHIFTS = (1, 3, 2)


def pack_spans_kernel(far, *refs):
    tabs, keys_ref, values_ref = refs[:3], refs[3], refs[4]
    outs, token_ref, sems = refs[5:8], refs[8], refs[9]
    token_ref[...] = jnp.zeros_like(token_ref)
    me = lax.axis_index("db")
    copies = []
    for i in range(3):
        first, second, seen = jnp.int32(0), jnp.int32(0), jnp.int32(0)
        for r in range(8):
            hit = tabs[i][far, r // 2, r % 2] == me
            span = tabs[i][far, r // 2, 2 + r % 2]
            first = jnp.where(hit & (seen == 0), span, first)
            second = jnp.where(hit & (seen == 1), span, second)
            seen = seen + jnp.where(hit, 1, 0)
        for slot, span in ((0, first), (1, second)):
            for kind, src in ((0, keys_ref), (1, values_ref)):
                copy = pltpu.make_async_copy(src.at[span], outs[i].at[slot, kind], sems.at[i, slot, kind])
                copy.start()
                copies.append(copy)
    for copy in copies:
        copy.wait()


def pack_spans(far, tables, keys, values):
    anywhere = pl.BlockSpec(memory_space=pl.ANY)
    vmem = pl.BlockSpec(memory_space=pltpu.VMEM)
    return pl.pallas_call(
        functools.partial(pack_spans_kernel, int(far)),
        in_specs=[pl.BlockSpec(memory_space=pltpu.SMEM)] * 3 + [vmem, vmem],
        out_specs=[anywhere] * 3 + [vmem],
        out_shape=[jax.ShapeDtypeStruct((2, 2, CH, HD), bf16)] * 3 + [jax.ShapeDtypeStruct((8, DH), i32)],
        scratch_shapes=[pltpu.SemaphoreType.DMA((3, 2, 2))],
        compiler_params=params(),
        cost_estimate=cost(0, 7 << 20),
        name="pack_far" if far else "pack_near",
    )(*tables, keys, values)


def cross_kernel(far, tab_ref, q_ref, *refs):
    keys_ref, values_ref = refs[:2]
    got = refs[2:5]
    if far:
        out_ref, kbuf, vbuf, sems = refs[5:]
    else:
        part_ref, out_ref, kbuf, vbuf, sems = refs[5:]
    me = lax.axis_index("db")
    plane, z = me // NZ, me % NZ
    row = 1 if far else 0
    here = []
    for r in range(8):
        owner = tab_ref[row, r // 2, r % 2]
        slot = jnp.int32(0)
        for earlier in range(r):
            slot = slot + jnp.where(tab_ref[row, earlier // 2, earlier % 2] == owner, 1, 0)
        here.append(jnp.where(owner // NZ == plane, 1, 0))
        shift = (z - owner % NZ + NZ) % NZ
        place = pl.ds((r % 2) * CH, CH)
        span = tab_ref[row, r // 2, 2 + r % 2]

        @pl.when(shift == 0)
        def _(span=span, place=place, r=r):
            pltpu.make_async_copy(keys_ref.at[span], kbuf.at[r // 2, place], sems.at[r, 0]).start()
            pltpu.make_async_copy(values_ref.at[span], vbuf.at[r // 2, place], sems.at[r, 1]).start()

        for i, k in enumerate(SHIFTS):

            @pl.when(shift == k)
            def _(i=i, slot=slot, place=place, r=r):
                pltpu.make_async_copy(got[i].at[slot, 0], kbuf.at[r // 2, place], sems.at[r, 0]).start()
                pltpu.make_async_copy(got[i].at[slot, 1], vbuf.at[r // 2, place], sems.at[r, 1]).start()

    lane = lax.broadcasted_iota(i32, (1, DH), 1)
    for n in range(4):
        for r in (2 * n, 2 * n + 1):
            place = pl.ds((r % 2) * CH, CH)
            pltpu.make_async_copy(keys_ref.at[0], kbuf.at[n, place], sems.at[r, 0]).wait()
            pltpu.make_async_copy(values_ref.at[0], vbuf.at[n, place], sems.at[r, 1]).wait()
        mine = jnp.where(lane < CH, here[2 * n], here[2 * n + 1]) > 0
        toks = slice(n * CH, (n + 1) * CH)
        heads = [slice(h * DH, (h + 1) * DH) for h in range(NH)]
        s = [
            lax.dot_general(
                q_ref[toks, c], kbuf[n, :, c], (((1,), (1,)), ((), ())), preferred_element_type=f32
            )
            for c in heads
        ]
        s = [jnp.where(mine, x * SCALE, NEG) for x in s]
        top = [jnp.max(x, axis=1, keepdims=True) for x in s]
        p = [jnp.where(mine, jnp.exp2(x - t), 0.0) for x, t in zip(s, top)]
        total = [jnp.sum(x, axis=1, keepdims=True) for x in p]
        o = [jnp.dot(x.astype(bf16), vbuf[n, :, c], preferred_element_type=f32) for x, c in zip(p, heads)]
        if far:
            stats = jnp.full((CH, DH), NEG, f32)
            for h, c in enumerate(heads):
                safe = jnp.maximum(total[h], 1e-30)
                out_ref[toks, c] = (o[h] / safe).astype(bf16)
                lse = jnp.where(total[h] > 0, top[h] + jnp.log2(safe), NEG)
                stats = jnp.where(lane % NH == h, lse, stats)
            high = stats.astype(bf16).astype(f32)
            low = (stats - high).astype(bf16).astype(f32)
            rest = stats - high - low
            stats = jnp.where(lane < NH, high, jnp.where(lane < 2 * NH, low, rest))
            out_ref[toks, HD:] = stats.astype(bf16)
        else:
            stats = part_ref[toks, HD:].astype(f32)
            other = (stats[:, :NH] + stats[:, NH : 2 * NH]) + stats[:, 2 * NH : 3 * NH]
            tops = jnp.full((CH, NH), NEG, f32)
            sums = jnp.zeros((CH, NH), f32)
            slot = lax.broadcasted_iota(i32, (1, NH), 1)
            for h in range(NH):
                tops = jnp.where(slot == h, top[h], tops)
                sums = jnp.where(slot == h, total[h], sums)
            high = jnp.maximum(tops, other)
            a, b = jnp.exp2(tops - high), jnp.exp2(other - high)
            inverse = 1.0 / (sums * a + b)
            a, b = a * inverse, b * inverse
            for h, c in enumerate(heads):
                mixed = o[h] * a[:, h : h + 1] + part_ref[toks, c].astype(f32) * b[:, h : h + 1]
                out_ref[toks, c] = mixed.astype(bf16)


def cross(far, table, q, keys, values, got, part=()):
    vmem = pl.BlockSpec(memory_space=pltpu.VMEM)
    return pl.pallas_call(
        functools.partial(cross_kernel, far),
        in_specs=[pl.BlockSpec(memory_space=pltpu.SMEM), vmem]
        + [pl.BlockSpec(memory_space=pl.ANY)] * 5
        + [vmem] * len(part),
        out_specs=vmem,
        out_shape=jax.ShapeDtypeStruct((TOK, HD + DH if far else HD), bf16),
        scratch_shapes=[
            pltpu.VMEM((4, 2 * CH, HD), bf16),
            pltpu.VMEM((4, 2 * CH, HD), bf16),
            pltpu.SemaphoreType.DMA((8, 2)),
        ],
        compiler_params=params(),
        cost_estimate=pl.CostEstimate(flops=32 << 30 if far else 1 << 26, bytes_accessed=0, transcendentals=0),
        name="cross_far" if far else "cross_near",
    )(table, q, keys, values, *got, *part)


def arrived_kernel(*refs):
    pass


def arrived(xs):
    anywhere = pl.BlockSpec(memory_space=pl.ANY)
    return pl.pallas_call(
        arrived_kernel,
        in_specs=[anywhere] * len(xs),
        out_specs=[anywhere] * len(xs),
        out_shape=[jax.ShapeDtypeStruct(x.shape, x.dtype) for x in xs],
        input_output_aliases={i: i for i in range(len(xs))},
        compiler_params=params(),
        cost_estimate=pl.CostEstimate(flops=32 << 30, bytes_accessed=0, transcendentals=0),
        name="arrived",
    )(*xs)


def per_device(queries, keys, values, doc_ids, nbr_owner, nbr_local, db_keys, db_values):
    q, db_k, db_v = queries[0], db_keys[0], db_values[0]
    swap = [(d, (d + NZ) % 8) for d in range(8)]
    turn = lambda k: [(s * NZ + z, s * NZ + (z + k) % NZ) for s in range(2) for z in range(NZ)]
    far_q = lax.ppermute(q, "db", swap)

    asked = jnp.concatenate([nbr_owner, nbr_local], axis=2)
    table = jnp.concatenate([asked, lax.ppermute(asked, "db", swap)], axis=0)
    tables = [lax.ppermute(table, "db", turn(NZ - k)) for k in SHIFTS]
    *far, token = pack_spans(True, tables, db_k, db_v)
    far_got = [lax.ppermute(x, "db", turn(k)) for x, k in zip(far, SHIFTS)]

    heads = pack_heads(table, doc_ids, q, keys[0], values[0])
    heads = lax.all_to_all(heads, "ctx", split_axis=0, concat_axis=0, tiled=True)

    near = list(pack_spans(False, tables, db_k, db_v)[:3])
    near_got = []
    for i, k in enumerate(SHIFTS):
        near_got.append(lax.ppermute(near[i], "db", turn(k)))
    part = lax.ppermute(cross(True, table, far_q, db_k, db_v, far_got), "db", swap)

    self_rows = self_attention(heads)
    self_rows = lax.all_to_all(self_rows, "ctx", split_axis=0, concat_axis=0, tiled=True)
    self_rows = unpack_heads(self_rows)

    near_got = arrived(near_got)
    cross_rows = cross(False, table, q, db_k, db_v, near_got, (part,))
    return self_rows[None], cross_rows[None]


def solution(mesh):
    rows = P("db", "ctx", None)
    spans = P("db", "ctx", None, None)
    return jax.shard_map(
        per_device,
        mesh=mesh,
        in_specs=(rows, rows, rows, P("db", "ctx"), rows, rows, spans, spans),
        out_specs=(rows, rows),
        check_vma=False,
    )
```

```python
import functools
import math

import jax
import jax.numpy as jnp
from jax import lax
from jax.experimental import pallas as pl
from jax.experimental.pallas import tpu as pltpu
from jax.sharding import PartitionSpec as P

DH = 128
CH = 64
NH = 16
TOK = 256
HD = 2048
NZ = 4
NC = 16
QT = 2048
CHUNK = 3 * TOK + 16
NEG = -1e30
SCALE = math.log2(math.e) / math.sqrt(DH)
VMEM = 48 << 20

f32, bf16, i32 = jnp.float32, jnp.bfloat16, jnp.int32


def params():
    return pltpu.CompilerParams(vmem_limit_bytes=VMEM)


def cost(flops, nbytes):
    return pl.CostEstimate(flops=flops // 64, bytes_accessed=nbytes // 16, transcendentals=0)


def pack_heads_kernel(token_ref, docs_ref, q_ref, k_ref, v_ref, out_ref):
    row = lax.broadcasted_iota(i32, (16, DH), 0)
    docs = docs_ref[...]
    left = jnp.broadcast_to(docs[:, :DH], (16, DH))
    right = jnp.broadcast_to(docs[:, DH:], (16, DH))
    packed = jnp.where(row == 0, left, jnp.where(row == 1, right, 4)).astype(f32).astype(bf16)
    for h in range(4):
        cols = slice(h * DH, (h + 1) * DH)
        out_ref[h, 0:TOK, :] = q_ref[:, cols]
        out_ref[h, TOK : 2 * TOK, :] = k_ref[:, cols]
        out_ref[h, 2 * TOK : 3 * TOK, :] = v_ref[:, cols]
        out_ref[h, 3 * TOK : CHUNK, :] = packed


def pack_heads(token, docs, q, k, v):
    wide = pl.BlockSpec((TOK, 4 * DH), lambda i: (0, i))
    return pl.pallas_call(
        pack_heads_kernel,
        grid=(4,),
        in_specs=[
            pl.BlockSpec((2, 4, 2), lambda i: (0, 0, 0)),
            pl.BlockSpec((1, TOK), lambda i: (0, 0)),
            wide,
            wide,
            wide,
        ],
        out_specs=pl.BlockSpec((4, CHUNK, DH), lambda i: (i, 0, 0)),
        out_shape=jax.ShapeDtypeStruct((NC, CHUNK, DH), bf16),
        compiler_params=params(),
        cost_estimate=cost(0, 6 << 20),
        name="pack_heads",
    )(token, docs, q, k, v)


def unpack_heads_kernel(x_ref, out_ref):
    for h in range(4):
        out_ref[:, h * DH : (h + 1) * DH] = x_ref[h]


def unpack_heads(x):
    return pl.pallas_call(
        unpack_heads_kernel,
        grid=(4,),
        in_specs=[pl.BlockSpec((4, TOK, DH), lambda i: (i, 0, 0))],
        out_specs=pl.BlockSpec((TOK, 4 * DH), lambda i: (0, i)),
        out_shape=jax.ShapeDtypeStruct((TOK, HD), bf16),
        compiler_params=params(),
        cost_estimate=cost(0, 2 << 20),
        name="unpack_heads",
    )(x)


def self_kernel(x_ref, o_ref):
    docs = x_ref[:, 3 * TOK : CHUNK, :].astype(f32)
    ends = [jnp.sum(jnp.where(docs < d - 0.5, 1.0, 0.0)).astype(i32) for d in (1, 2, 3)]
    per = QT // TOK

    def start_of(p):
        s = jnp.where(p >= ends[0], ends[0], 0)
        s = jnp.maximum(s, jnp.where(p >= ends[1], ends[1], 0))
        return jnp.maximum(s, jnp.where(p >= ends[2], ends[2], 0))

    def rows(j, part):
        return x_ref[pl.ds(per * j, per), part * TOK : (part + 1) * TOK, :].reshape(QT, DH)

    def lanes(p):
        return sum(p[:, c : c + DH] for c in range(0, p.shape[1], DH))

    def query_tile(i, carry):
        base = i * QT
        qs = [x_ref[per * i + u, 0:TOK, :] for u in range(per)]
        columns = [lax.broadcasted_iota(i32, (TOK, 1), 0) + u * TOK for u in range(per)]
        firsts = [start_of(base + c) for c in columns]
        lo = start_of(base) // QT
        mid = jnp.minimum((start_of(base + QT - 1) + QT - 1) // QT, i)

        def step(j, state, kind):
            k, v = rows(j, 1), rows(j, 2)
            ss = []
            for u in range(per):
                width = (u + 1) * TOK if kind == "diagonal" else QT
                s = lax.dot_general(qs[u], k[:width], (((1,), (1,)), ((), ())), preferred_element_type=f32)
                s = s * SCALE
                if kind != "open":
                    local = lax.broadcasted_iota(i32, (TOK, width), 1)
                    seen = local >= firsts[u] - j * QT
                    if kind == "diagonal":
                        seen = seen & (local <= columns[u])
                    s = jnp.where(seen, s, NEG)
                ss.append(s)
            out = []
            for u, s in enumerate(ss):
                new = jnp.max(s, axis=1, keepdims=True)
                if state is not None:
                    acc, top, total = state[u]
                    new = jnp.maximum(top, new)
                p = jnp.exp2(s - new)
                mixed = jnp.dot(p.astype(bf16), v[: s.shape[1]], preferred_element_type=f32)
                weight = lanes(p)
                if state is not None:
                    fade = jnp.exp2(top - new)
                    mixed = acc * fade + mixed
                    weight = total * fade + weight
                out.append((mixed, new, weight))
            return tuple(out)

        state = step(i, None, "diagonal")
        state = lax.fori_loop(lo, mid, functools.partial(step, kind="masked"), state)
        state = lax.fori_loop(mid, i, functools.partial(step, kind="open"), state)
        for u, (acc, top, total) in enumerate(state):
            o_ref[per * i + u] = (acc / jnp.sum(total, axis=1, keepdims=True)).astype(bf16)
        return carry

    lax.fori_loop(0, NC * TOK // QT, query_tile, 0)


def self_attention(x):
    return pl.pallas_call(
        self_kernel,
        in_specs=[pl.BlockSpec(memory_space=pltpu.VMEM)],
        out_specs=pl.BlockSpec(memory_space=pltpu.VMEM),
        out_shape=jax.ShapeDtypeStruct((NC, TOK, DH), bf16),
        compiler_params=params(),
        cost_estimate=cost(16 << 30, 4 << 20),
        name="self_attention",
    )(x)


SHIFTS = (1, 3, 2)


def pack_spans_kernel(far, *refs):
    tabs, keys_ref, values_ref = refs[:3], refs[3], refs[4]
    outs, hold, loads, stores = refs[5:8], refs[8], refs[9], refs[10]
    me = lax.axis_index("db")
    moves = []
    for i in range(3):
        first, second, seen = jnp.int32(0), jnp.int32(0), jnp.int32(0)
        for r in range(8):
            entry = tabs[i][far, r // 2, r % 2]
            hit = entry // 8 == me
            span = entry % 8
            first = jnp.where(hit & (seen == 0), span, first)
            second = jnp.where(hit & (seen == 1), span, second)
            seen = seen + jnp.where(hit, 1, 0)
        for slot, span in ((0, first), (1, second)):
            for kind, src in ((0, keys_ref), (1, values_ref)):
                at = (i, slot, kind)
                load = pltpu.make_async_copy(src.at[span], hold.at[at], loads.at[at])
                load.start()
                moves.append((load, pltpu.make_async_copy(hold.at[at], outs[i].at[slot, kind], stores.at[at])))
    for load, store in moves:
        load.wait()
        store.start()
    for load, store in moves:
        store.wait()


def pack_spans(far, tables, keys, values):
    anywhere = pl.BlockSpec(memory_space=pl.ANY)
    return pl.pallas_call(
        functools.partial(pack_spans_kernel, int(far)),
        in_specs=[pl.BlockSpec(memory_space=pltpu.SMEM)] * 3 + [anywhere, anywhere],
        out_specs=[anywhere] * 3,
        out_shape=[jax.ShapeDtypeStruct((2, 2, CH, HD), bf16)] * 3,
        scratch_shapes=[
            pltpu.VMEM((3, 2, 2, CH, HD), bf16),
            pltpu.SemaphoreType.DMA((3, 2, 2)),
            pltpu.SemaphoreType.DMA((3, 2, 2)),
        ],
        compiler_params=params(),
        cost_estimate=cost(0, 7 << 20),
        name="pack_far" if far else "pack_near",
    )(*tables, keys, values)


def cross_kernel(far, tab_ref, q_ref, *refs):
    keys_ref, values_ref = refs[:2]
    got = refs[2:5]
    if far:
        out_ref, kbuf, vbuf, sems = refs[5:]
    else:
        part_ref, out_ref, kbuf, vbuf, sems = refs[5:]
    me = lax.axis_index("db")
    plane, z = me // NZ, me % NZ
    row = 1 if far else 0
    here = []
    for r in range(8):
        owner = tab_ref[row, r // 2, r % 2] // 8
        slot = jnp.int32(0)
        for earlier in range(r):
            slot = slot + jnp.where(tab_ref[row, earlier // 2, earlier % 2] // 8 == owner, 1, 0)
        here.append(jnp.where(owner // NZ == plane, 1, 0))
        shift = (z - owner % NZ + NZ) % NZ
        place = pl.ds((r % 2) * CH, CH)
        span = tab_ref[row, r // 2, r % 2] % 8

        @pl.when(shift == 0)
        def _(span=span, place=place, r=r):
            pltpu.make_async_copy(keys_ref.at[span], kbuf.at[r // 2, place], sems.at[r, 0]).start()
            pltpu.make_async_copy(values_ref.at[span], vbuf.at[r // 2, place], sems.at[r, 1]).start()

        for i, k in enumerate(SHIFTS):

            @pl.when(shift == k)
            def _(i=i, slot=slot, place=place, r=r):
                pltpu.make_async_copy(got[i].at[slot, 0], kbuf.at[r // 2, place], sems.at[r, 0]).start()
                pltpu.make_async_copy(got[i].at[slot, 1], vbuf.at[r // 2, place], sems.at[r, 1]).start()

    lane = lax.broadcasted_iota(i32, (1, DH), 1)
    for n in range(4):
        for r in (2 * n, 2 * n + 1):
            place = pl.ds((r % 2) * CH, CH)
            pltpu.make_async_copy(keys_ref.at[0], kbuf.at[n, place], sems.at[r, 0]).wait()
            pltpu.make_async_copy(values_ref.at[0], vbuf.at[n, place], sems.at[r, 1]).wait()
        mine = jnp.where(lane < CH, here[2 * n], here[2 * n + 1]) > 0
        toks = slice(n * CH, (n + 1) * CH)
        heads = [slice(h * DH, (h + 1) * DH) for h in range(NH)]
        s = [
            lax.dot_general(
                q_ref[toks, c], kbuf[n, :, c], (((1,), (1,)), ((), ())), preferred_element_type=f32
            )
            for c in heads
        ]
        s = [jnp.where(mine, x * SCALE, NEG) for x in s]
        top = [jnp.max(x, axis=1, keepdims=True) for x in s]
        p = [jnp.where(mine, jnp.exp2(x - t), 0.0) for x, t in zip(s, top)]
        total = [jnp.sum(x, axis=1, keepdims=True) for x in p]
        o = [jnp.dot(x.astype(bf16), vbuf[n, :, c], preferred_element_type=f32) for x, c in zip(p, heads)]
        if far:
            stats = jnp.full((CH, DH), NEG, f32)
            for h, c in enumerate(heads):
                safe = jnp.maximum(total[h], 1e-30)
                out_ref[toks, c] = (o[h] / safe).astype(bf16)
                lse = jnp.where(total[h] > 0, top[h] + jnp.log2(safe), NEG)
                stats = jnp.where(lane % NH == h, lse, stats)
            high = stats.astype(bf16).astype(f32)
            low = (stats - high).astype(bf16).astype(f32)
            rest = stats - high - low
            stats = jnp.where(lane < NH, high, jnp.where(lane < 2 * NH, low, rest))
            out_ref[toks, HD:] = stats.astype(bf16)
        else:
            stats = part_ref[toks, HD:].astype(f32)
            other = (stats[:, :NH] + stats[:, NH : 2 * NH]) + stats[:, 2 * NH : 3 * NH]
            tops = jnp.full((CH, NH), NEG, f32)
            sums = jnp.zeros((CH, NH), f32)
            slot = lax.broadcasted_iota(i32, (1, NH), 1)
            for h in range(NH):
                tops = jnp.where(slot == h, top[h], tops)
                sums = jnp.where(slot == h, total[h], sums)
            high = jnp.maximum(tops, other)
            a, b = jnp.exp2(tops - high), jnp.exp2(other - high)
            inverse = 1.0 / (sums * a + b)
            a, b = a * inverse, b * inverse
            for h, c in enumerate(heads):
                mixed = o[h] * a[:, h : h + 1] + part_ref[toks, c].astype(f32) * b[:, h : h + 1]
                out_ref[toks, c] = mixed.astype(bf16)


def cross(far, table, q, keys, values, got, part=()):
    vmem = pl.BlockSpec(memory_space=pltpu.VMEM)
    return pl.pallas_call(
        functools.partial(cross_kernel, far),
        in_specs=[pl.BlockSpec(memory_space=pltpu.SMEM), vmem]
        + [pl.BlockSpec(memory_space=pl.ANY)] * 5
        + [vmem] * len(part),
        out_specs=vmem,
        out_shape=jax.ShapeDtypeStruct((TOK, HD + DH if far else HD), bf16),
        scratch_shapes=[
            pltpu.VMEM((4, 2 * CH, HD), bf16),
            pltpu.VMEM((4, 2 * CH, HD), bf16),
            pltpu.SemaphoreType.DMA((8, 2)),
        ],
        compiler_params=params(),
        cost_estimate=pl.CostEstimate(flops=32 << 30 if far else 1 << 26, bytes_accessed=0, transcendentals=0),
        name="cross_far" if far else "cross_near",
    )(table, q, keys, values, *got, *part)


def arrived_kernel(*refs):
    pass


def arrived(xs):
    anywhere = pl.BlockSpec(memory_space=pl.ANY)
    return pl.pallas_call(
        arrived_kernel,
        in_specs=[anywhere] * len(xs),
        out_specs=[anywhere] * len(xs),
        out_shape=[jax.ShapeDtypeStruct(x.shape, x.dtype) for x in xs],
        input_output_aliases={i: i for i in range(len(xs))},
        compiler_params=params(),
        cost_estimate=pl.CostEstimate(flops=32 << 30, bytes_accessed=0, transcendentals=0),
        name="arrived",
    )(*xs)


def per_device(queries, keys, values, doc_ids, nbr_owner, nbr_local, db_keys, db_values):
    q, db_k, db_v = queries[0], db_keys[0], db_values[0]
    swap = [(d, (d + NZ) % 8) for d in range(8)]
    turn = lambda k: [(s * NZ + z, s * NZ + (z + k) % NZ) for s in range(2) for z in range(NZ)]
    far_q = lax.ppermute(q, "db", swap)

    asked = lax.optimization_barrier(nbr_owner * 8 + nbr_local)
    table = jnp.concatenate([asked, lax.ppermute(asked, "db", swap)], axis=0)
    tables = [lax.ppermute(table, "db", turn(NZ - k)) for k in SHIFTS]
    far = pack_spans(True, tables, db_k, db_v)
    far_got = [lax.ppermute(x, "db", turn(k)) for x, k in zip(far, SHIFTS)]

    heads = pack_heads(table, doc_ids, q, keys[0], values[0])
    heads = lax.all_to_all(heads, "ctx", split_axis=0, concat_axis=0, tiled=True)

    near = pack_spans(False, tables, db_k, db_v)
    near_got = []
    for i, k in enumerate(SHIFTS):
        near_got.append(lax.ppermute(near[i], "db", turn(k)))
    part = lax.ppermute(cross(True, table, far_q, db_k, db_v, far_got), "db", swap)

    self_rows = self_attention(heads)
    self_rows = lax.all_to_all(self_rows, "ctx", split_axis=0, concat_axis=0, tiled=True)
    self_rows = unpack_heads(self_rows)

    near_got = arrived(near_got)
    cross_rows = cross(False, table, q, db_k, db_v, near_got, (part,))
    return self_rows[None], cross_rows[None]


def solution(mesh):
    rows = P("db", "ctx", None)
    spans = P("db", "ctx", None, None)
    return jax.shard_map(
        per_device,
        mesh=mesh,
        in_specs=(rows, rows, rows, P("db", "ctx"), rows, rows, spans, spans),
        out_specs=(rows, rows),
        check_vma=False,
    )
```

```python
import functools
import math

import jax
import jax.numpy as jnp
from jax import lax
from jax.experimental import pallas as pl
from jax.experimental.pallas import tpu as pltpu
from jax.sharding import PartitionSpec as P

DH = 128
CH = 64
NH = 16
TOK = 256
HD = 2048
NZ = 4
NC = 16
QT = 1024
CHUNK = 3 * TOK + 16
NEG = -1e30
SCALE = math.log2(math.e) / math.sqrt(DH)
VMEM = 48 << 20

f32, bf16, i32 = jnp.float32, jnp.bfloat16, jnp.int32


def params():
    return pltpu.CompilerParams(vmem_limit_bytes=VMEM)


def cost(flops, nbytes):
    return pl.CostEstimate(flops=flops // 64, bytes_accessed=nbytes // 16, transcendentals=0)


def pack_heads_kernel(token_ref, docs_ref, q_ref, k_ref, v_ref, out_ref):
    row = lax.broadcasted_iota(i32, (16, DH), 0)
    docs = docs_ref[...]
    left = jnp.broadcast_to(docs[:, :DH], (16, DH))
    right = jnp.broadcast_to(docs[:, DH:], (16, DH))
    packed = jnp.where(row == 0, left, jnp.where(row == 1, right, 4)).astype(f32).astype(bf16)
    for h in range(4):
        cols = slice(h * DH, (h + 1) * DH)
        out_ref[h, 0:TOK, :] = q_ref[:, cols]
        out_ref[h, TOK : 2 * TOK, :] = k_ref[:, cols]
        out_ref[h, 2 * TOK : 3 * TOK, :] = v_ref[:, cols]
        out_ref[h, 3 * TOK : CHUNK, :] = packed


def pack_heads(token, docs, q, k, v):
    wide = pl.BlockSpec((TOK, 4 * DH), lambda i: (0, i))
    return pl.pallas_call(
        pack_heads_kernel,
        grid=(4,),
        in_specs=[
            pl.BlockSpec((4, 4, 2), lambda i: (0, 0, 0)),
            pl.BlockSpec((1, TOK), lambda i: (0, 0)),
            wide,
            wide,
            wide,
        ],
        out_specs=pl.BlockSpec((4, CHUNK, DH), lambda i: (i, 0, 0)),
        out_shape=jax.ShapeDtypeStruct((NC, CHUNK, DH), bf16),
        compiler_params=params(),
        cost_estimate=cost(0, 6 << 20),
        name="pack_heads",
    )(token, docs, q, k, v)


def unpack_heads_kernel(x_ref, out_ref):
    for h in range(4):
        out_ref[:, h * DH : (h + 1) * DH] = x_ref[h]


def unpack_heads(x):
    return pl.pallas_call(
        unpack_heads_kernel,
        grid=(4,),
        in_specs=[pl.BlockSpec((4, TOK, DH), lambda i: (i, 0, 0))],
        out_specs=pl.BlockSpec((TOK, 4 * DH), lambda i: (0, i)),
        out_shape=jax.ShapeDtypeStruct((TOK, HD), bf16),
        compiler_params=params(),
        cost_estimate=cost(0, 2 << 20),
        name="unpack_heads",
    )(x)


def self_kernel(x_ref, o_ref):
    docs = x_ref[:, 3 * TOK : CHUNK, :].astype(f32)
    ends = [jnp.sum(jnp.where(docs < d - 0.5, 1.0, 0.0)).astype(i32) for d in (1, 2, 3)]
    per = QT // TOK

    def start_of(p):
        s = jnp.where(p >= ends[0], ends[0], 0)
        s = jnp.maximum(s, jnp.where(p >= ends[1], ends[1], 0))
        return jnp.maximum(s, jnp.where(p >= ends[2], ends[2], 0))

    def rows(j, part):
        return x_ref[pl.ds(per * j, per), part * TOK : (part + 1) * TOK, :].reshape(QT, DH)

    def lanes(p):
        return sum(p[:, c : c + DH] for c in range(0, p.shape[1], DH))

    def query_tile(i, carry):
        base = i * QT
        qs = [x_ref[per * i + u, 0:TOK, :] for u in range(per)]
        columns = [lax.broadcasted_iota(i32, (TOK, 1), 0) + u * TOK for u in range(per)]
        firsts = [start_of(base + c) for c in columns]
        lo = start_of(base) // QT
        mid = jnp.minimum((start_of(base + QT - 1) + QT - 1) // QT, i)

        def step(j, state, kind):
            k, v = rows(j, 1), rows(j, 2)
            ss = []
            for u in range(per):
                width = (u + 1) * TOK if kind == "diagonal" else QT
                s = lax.dot_general(qs[u], k[:width], (((1,), (1,)), ((), ())), preferred_element_type=f32)
                s = s * SCALE
                if kind != "open":
                    local = lax.broadcasted_iota(i32, (TOK, width), 1)
                    seen = local >= firsts[u] - j * QT
                    if kind == "diagonal":
                        seen = seen & (local <= columns[u])
                    s = jnp.where(seen, s, NEG)
                ss.append(s)
            out = []
            for u, s in enumerate(ss):
                new = jnp.max(s, axis=1, keepdims=True)
                if state is not None:
                    acc, top, total = state[u]
                    new = jnp.maximum(top, new)
                p = jnp.exp2(s - new)
                mixed = jnp.dot(p.astype(bf16), v[: s.shape[1]], preferred_element_type=f32)
                weight = lanes(p)
                if state is not None:
                    fade = jnp.exp2(top - new)
                    mixed = acc * fade + mixed
                    weight = total * fade + weight
                out.append((mixed, new, weight))
            return tuple(out)

        state = step(i, None, "diagonal")
        state = lax.fori_loop(lo, mid, functools.partial(step, kind="masked"), state)
        state = lax.fori_loop(mid, i, functools.partial(step, kind="open"), state)
        for u, (acc, top, total) in enumerate(state):
            o_ref[per * i + u] = (acc / jnp.sum(total, axis=1, keepdims=True)).astype(bf16)
        return carry

    lax.fori_loop(0, NC * TOK // QT, query_tile, 0)


def self_attention(x):
    return pl.pallas_call(
        self_kernel,
        in_specs=[pl.BlockSpec(memory_space=pltpu.VMEM)],
        out_specs=pl.BlockSpec(memory_space=pltpu.VMEM),
        out_shape=jax.ShapeDtypeStruct((NC, TOK, DH), bf16),
        compiler_params=params(),
        cost_estimate=cost(16 << 30, 4 << 20),
        name="self_attention",
    )(x)


SHIFTS = (1, 3, 2)


def asked_of(tab_ref, row, owner, value):
    first, second, seen = jnp.int32(0), jnp.int32(0), jnp.int32(0)
    for r in range(8):
        entry = tab_ref[row, r // 2, r % 2]
        hit = entry // 8 == owner
        first = jnp.where(hit & (seen == 0), value(r, entry), first)
        second = jnp.where(hit & (seen == 1), value(r, entry), second)
        seen = seen + jnp.where(hit, 1, 0)
    return first, second


def pack_spans_kernel(tab_ref, keys_ref, values_ref, *refs):
    outs, hold, loads, stores = refs[:3], refs[3], refs[4], refs[5]
    me = lax.axis_index("db")
    moves = []
    for i in range(3):
        first, second = asked_of(tab_ref, 1 + i, me, lambda r, entry: entry % 8)
        for slot, span in ((0, first), (1, second)):
            for kind, src in ((0, keys_ref), (1, values_ref)):
                at = (i, slot, kind)
                load = pltpu.make_async_copy(src.at[span], hold.at[at], loads.at[at])
                load.start()
                moves.append((load, pltpu.make_async_copy(hold.at[at], outs[i].at[slot, kind], stores.at[at])))
    for load, store in moves:
        load.wait()
        store.start()
    for load, store in moves:
        store.wait()


def pack_spans(table, keys, values):
    anywhere = pl.BlockSpec(memory_space=pl.ANY)
    return pl.pallas_call(
        pack_spans_kernel,
        in_specs=[pl.BlockSpec(memory_space=pltpu.SMEM), anywhere, anywhere],
        out_specs=[anywhere] * 3,
        out_shape=[jax.ShapeDtypeStruct((2, 2, CH, HD), bf16)] * 3,
        scratch_shapes=[
            pltpu.VMEM((3, 2, 2, CH, HD), bf16),
            pltpu.SemaphoreType.DMA((3, 2, 2)),
            pltpu.SemaphoreType.DMA((3, 2, 2)),
        ],
        compiler_params=params(),
        cost_estimate=cost(0, 7 << 20),
        name="pack_far",
    )(table, keys, values)


def pack_queries_kernel(tab_ref, q_ref, *refs):
    outs, sems = refs[:3], refs[3]
    me = lax.axis_index("db")
    plane, z = me // NZ, me % NZ
    copies = []
    for i, k in enumerate(SHIFTS):
        for slot, n in enumerate(asked_of(tab_ref, 0, plane * NZ + (z + k) % NZ, lambda r, entry: r // 2)):
            src = q_ref.at[pl.ds(pl.multiple_of(n * CH, CH), CH)]
            copy = pltpu.make_async_copy(src, outs[i].at[slot], sems.at[i, slot])
            copy.start()
            copies.append(copy)
    for copy in copies:
        copy.wait()


def pack_queries(asked, q):
    anywhere = pl.BlockSpec(memory_space=pl.ANY)
    return pl.pallas_call(
        pack_queries_kernel,
        in_specs=[pl.BlockSpec(memory_space=pltpu.SMEM), pl.BlockSpec(memory_space=pltpu.VMEM)],
        out_specs=[anywhere] * 3,
        out_shape=[jax.ShapeDtypeStruct((2, CH, HD), bf16)] * 3,
        scratch_shapes=[pltpu.SemaphoreType.DMA((3, 2))],
        compiler_params=params(),
        cost_estimate=cost(0, 3 << 20),
        name="pack_queries",
    )(asked, q)


HEADS = [slice(h * DH, (h + 1) * DH) for h in range(NH)]


def encode(stats, lane):
    high = stats.astype(bf16).astype(f32)
    low = (stats - high).astype(bf16).astype(f32)
    rest = stats - high - low
    return jnp.where(lane < NH, high, jnp.where(lane < 2 * NH, low, rest)).astype(bf16)


def decode(stats):
    stats = stats.astype(f32)
    return (stats[:, :NH] + stats[:, NH : 2 * NH]) + stats[:, 2 * NH : 3 * NH]


def serve_kernel(tab_ref, q_ref, keys_ref, values_ref, *refs):
    got, outs = refs[:3], refs[3:7]
    me = lax.axis_index("db")
    lane = lax.broadcasted_iota(i32, (1, DH), 1)
    for i in range(4):
        row = 0 if i == 3 else 1 + SHIFTS.index(NZ - SHIFTS[i])
        spans = asked_of(tab_ref, row, me, lambda r, entry: entry % 8)
        if i == 3:
            own = asked_of(tab_ref, row, me, lambda r, entry: r // 2)
        for slot, span in enumerate(spans):
            if i == 3:
                toks = pl.ds(pl.multiple_of(own[slot] * CH, CH), CH)
                q = [q_ref[toks, c] for c in HEADS]
            else:
                q = [got[i][slot, :, c] for c in HEADS]
            k = [keys_ref[span, :, c] for c in HEADS]
            s = [
                lax.dot_general(x, y, (((1,), (1,)), ((), ())), preferred_element_type=f32) * SCALE
                for x, y in zip(q, k)
            ]
            top = [jnp.max(x, axis=1, keepdims=True) for x in s]
            p = [jnp.exp2(x - t) for x, t in zip(s, top)]
            total = [jnp.sum(x, axis=1, keepdims=True) for x in p]
            o = [
                jnp.dot(x.astype(bf16), values_ref[span, :, c], preferred_element_type=f32)
                for x, c in zip(p, HEADS)
            ]
            stats = jnp.zeros((CH, DH), f32)
            for h, c in enumerate(HEADS):
                outs[i][slot, :, c] = (o[h] / total[h]).astype(bf16)
                stats = jnp.where(lane % NH == h, top[h] + jnp.log2(total[h]), stats)
            outs[i][slot, :, HD:] = encode(stats, lane)


def serve(table, q, keys, values, got):
    vmem = pl.BlockSpec(memory_space=pltpu.VMEM)
    return pl.pallas_call(
        serve_kernel,
        in_specs=[pl.BlockSpec(memory_space=pltpu.SMEM)] + [vmem] * 6,
        out_specs=[vmem] * 4,
        out_shape=[jax.ShapeDtypeStruct((2, CH, HD + DH), bf16)] * 4,
        compiler_params=params(),
        cost_estimate=cost(4 << 30, 6 << 20),
        name="serve",
    )(table, q, keys, values, *got)


def combine_kernel(tab_ref, *refs):
    got, part_ref, out_ref, hold, sems = refs[:4], refs[4], refs[5], refs[6], refs[7]
    me = lax.axis_index("db")
    plane, z = me // NZ, me % NZ
    here = []
    for r in range(8):
        owner = tab_ref[0, r // 2, r % 2] // 8
        slot = jnp.int32(0)
        for earlier in range(r):
            slot = slot + jnp.where(tab_ref[0, earlier // 2, earlier % 2] // 8 == owner, 1, 0)
        here.append(jnp.where(owner // NZ == plane, 1, 0))
        shift = (owner % NZ - z + NZ) % NZ
        for i, k in enumerate(SHIFTS + (0,)):

            @pl.when(shift == k)
            def _(i=i, slot=slot, r=r):
                pltpu.make_async_copy(got[i].at[slot], hold.at[r], sems.at[r]).start()

    for n in range(4):
        toks = slice(n * CH, (n + 1) * CH)
        lse = [decode(part_ref[toks, HD:])]
        for r in (2 * n, 2 * n + 1):
            pltpu.make_async_copy(got[0].at[0], hold.at[r], sems.at[r]).wait()
            lse.append(jnp.where(here[r] > 0, decode(hold[r, :, HD:]), NEG))
        high = jnp.maximum(jnp.maximum(lse[0], lse[1]), lse[2])
        w = [jnp.exp2(x - high) for x in lse]
        inverse = 1.0 / (w[0] + w[1] + w[2])
        w = [x * inverse for x in w]
        for h, c in enumerate(HEADS):
            a, b, d = (x[:, h : h + 1] for x in w)
            mixed = part_ref[toks, c].astype(f32) * a
            mixed = mixed + hold[2 * n, :, c].astype(f32) * b
            mixed = mixed + hold[2 * n + 1, :, c].astype(f32) * d
            out_ref[toks, c] = mixed.astype(bf16)


def combine(asked, got, part):
    vmem = pl.BlockSpec(memory_space=pltpu.VMEM)
    return pl.pallas_call(
        combine_kernel,
        in_specs=[pl.BlockSpec(memory_space=pltpu.SMEM)] + [pl.BlockSpec(memory_space=pl.ANY)] * 4 + [vmem],
        out_specs=vmem,
        out_shape=jax.ShapeDtypeStruct((TOK, HD), bf16),
        scratch_shapes=[pltpu.VMEM((8, CH, HD + DH), bf16), pltpu.SemaphoreType.DMA((8,))],
        compiler_params=params(),
        cost_estimate=cost(1 << 26, 4 << 20),
        name="combine",
    )(asked, *got, part)


def cross_kernel(tab_ref, q_ref, keys_ref, values_ref, *refs):
    got, out_ref, kbuf, vbuf, sems = refs[:3], refs[3], refs[4], refs[5], refs[6]
    me = lax.axis_index("db")
    plane, z = me // NZ, me % NZ
    row = 0
    here = []
    for r in range(8):
        owner = tab_ref[row, r // 2, r % 2] // 8
        slot = jnp.int32(0)
        for earlier in range(r):
            slot = slot + jnp.where(tab_ref[row, earlier // 2, earlier % 2] // 8 == owner, 1, 0)
        here.append(jnp.where(owner // NZ == plane, 1, 0))
        shift = (z - owner % NZ + NZ) % NZ
        place = pl.ds((r % 2) * CH, CH)
        span = tab_ref[row, r // 2, r % 2] % 8

        @pl.when(shift == 0)
        def _(span=span, place=place, r=r):
            pltpu.make_async_copy(keys_ref.at[span], kbuf.at[r // 2, place], sems.at[r, 0]).start()
            pltpu.make_async_copy(values_ref.at[span], vbuf.at[r // 2, place], sems.at[r, 1]).start()

        for i, k in enumerate(SHIFTS):

            @pl.when(shift == k)
            def _(i=i, slot=slot, place=place, r=r):
                pltpu.make_async_copy(got[i].at[slot, 0], kbuf.at[r // 2, place], sems.at[r, 0]).start()
                pltpu.make_async_copy(got[i].at[slot, 1], vbuf.at[r // 2, place], sems.at[r, 1]).start()

    lane = lax.broadcasted_iota(i32, (1, DH), 1)
    for n in range(4):
        for r in (2 * n, 2 * n + 1):
            place = pl.ds((r % 2) * CH, CH)
            pltpu.make_async_copy(keys_ref.at[0], kbuf.at[n, place], sems.at[r, 0]).wait()
            pltpu.make_async_copy(values_ref.at[0], vbuf.at[n, place], sems.at[r, 1]).wait()
        mine = jnp.where(lane < CH, here[2 * n], here[2 * n + 1]) > 0
        toks = slice(n * CH, (n + 1) * CH)
        heads = [slice(h * DH, (h + 1) * DH) for h in range(NH)]
        s = [
            lax.dot_general(
                q_ref[toks, c], kbuf[n, :, c], (((1,), (1,)), ((), ())), preferred_element_type=f32
            )
            for c in heads
        ]
        s = [jnp.where(mine, x * SCALE, NEG) for x in s]
        top = [jnp.max(x, axis=1, keepdims=True) for x in s]
        p = [jnp.where(mine, jnp.exp2(x - t), 0.0) for x, t in zip(s, top)]
        total = [jnp.sum(x, axis=1, keepdims=True) for x in p]
        o = [jnp.dot(x.astype(bf16), vbuf[n, :, c], preferred_element_type=f32) for x, c in zip(p, heads)]
        stats = jnp.full((CH, DH), NEG, f32)
        for h, c in enumerate(heads):
            safe = jnp.maximum(total[h], 1e-30)
            out_ref[toks, c] = (o[h] / safe).astype(bf16)
            lse = jnp.where(total[h] > 0, top[h] + jnp.log2(safe), NEG)
            stats = jnp.where(lane % NH == h, lse, stats)
        out_ref[toks, HD:] = encode(stats, lane)


def cross(table, q, keys, values, got):
    vmem = pl.BlockSpec(memory_space=pltpu.VMEM)
    return pl.pallas_call(
        cross_kernel,
        in_specs=[pl.BlockSpec(memory_space=pltpu.SMEM), vmem]
        + [pl.BlockSpec(memory_space=pl.ANY)] * 5,
        out_specs=vmem,
        out_shape=jax.ShapeDtypeStruct((TOK, HD + DH), bf16),
        scratch_shapes=[
            pltpu.VMEM((4, 2 * CH, HD), bf16),
            pltpu.VMEM((4, 2 * CH, HD), bf16),
            pltpu.SemaphoreType.DMA((8, 2)),
        ],
        compiler_params=params(),
        cost_estimate=pl.CostEstimate(flops=20 << 30, bytes_accessed=0, transcendentals=0),
        name="cross_far",
    )(table, q, keys, values, *got)


def arrived_kernel(*refs):
    pass


def arrived(xs):
    anywhere = pl.BlockSpec(memory_space=pl.ANY)
    return pl.pallas_call(
        arrived_kernel,
        in_specs=[anywhere] * len(xs),
        out_specs=[anywhere] * len(xs),
        out_shape=[jax.ShapeDtypeStruct(x.shape, x.dtype) for x in xs],
        input_output_aliases={i: i for i in range(len(xs))},
        compiler_params=params(),
        cost_estimate=pl.CostEstimate(flops=32 << 30, bytes_accessed=0, transcendentals=0),
        name="arrived",
    )(*xs)


def per_device(queries, keys, values, doc_ids, nbr_owner, nbr_local, db_keys, db_values):
    q, db_k, db_v = queries[0], db_keys[0], db_values[0]
    swap = [(d, (d + NZ) % 8) for d in range(8)]
    turn = lambda k: [(s * NZ + z, s * NZ + (z + k) % NZ) for s in range(2) for z in range(NZ)]

    asked = lax.optimization_barrier(nbr_owner * 8 + nbr_local)
    table = jnp.concatenate([asked] + [lax.ppermute(asked, "db", turn(NZ - k)) for k in SHIFTS], axis=0)
    table = lax.optimization_barrier(table)
    far_table = lax.ppermute(table, "db", swap)
    far_q = lax.ppermute(q, "db", swap)
    sent = pack_queries(asked, q)
    sent = [lax.ppermute(x, "db", turn(k)) for x, k in zip(sent, SHIFTS)]

    heads = pack_heads(table, doc_ids, q, keys[0], values[0])
    heads = lax.all_to_all(heads, "ctx", split_axis=0, concat_axis=0, tiled=True)

    far = pack_spans(far_table, db_k, db_v)
    far_got = [lax.ppermute(x, "db", turn(k)) for x, k in zip(far, SHIFTS)]
    *near, own = serve(table, q, db_k, db_v, sent)
    near_got = [lax.ppermute(x, "db", turn(NZ - k)) for x, k in zip(near, SHIFTS)]
    part = lax.ppermute(cross(far_table, far_q, db_k, db_v, far_got), "db", swap)

    self_rows = self_attention(heads)
    self_rows = lax.all_to_all(self_rows, "ctx", split_axis=0, concat_axis=0, tiled=True)
    self_rows = unpack_heads(self_rows)

    near_got = arrived(near_got)
    cross_rows = combine(asked, list(near_got) + [own], part)
    return self_rows[None], cross_rows[None]


def solution(mesh):
    rows = P("db", "ctx", None)
    spans = P("db", "ctx", None, None)
    return jax.shard_map(
        per_device,
        mesh=mesh,
        in_specs=(rows, rows, rows, P("db", "ctx"), rows, rows, spans, spans),
        out_specs=(rows, rows),
        check_vma=False,
    )
```

```python
import functools
import math

import jax
import jax.numpy as jnp
from jax import lax
from jax.experimental import pallas as pl
from jax.experimental.pallas import tpu as pltpu
from jax.sharding import PartitionSpec as P

DH = 128
CH = 64
NH = 16
TOK = 256
HD = 2048
NZ = 4
NC = 16
QT = 1024
CHUNK = 3 * TOK + 16
NEG = -1e30
SCALE = math.log2(math.e) / math.sqrt(DH)
VMEM = 48 << 20

f32, bf16, i32 = jnp.float32, jnp.bfloat16, jnp.int32


def params():
    return pltpu.CompilerParams(vmem_limit_bytes=VMEM)


def cost(flops, nbytes):
    return pl.CostEstimate(flops=flops // 64, bytes_accessed=nbytes // 16, transcendentals=0)


def pack_heads_kernel(token_ref, docs_ref, q_ref, k_ref, v_ref, out_ref):
    row = lax.broadcasted_iota(i32, (16, DH), 0)
    docs = docs_ref[...]
    left = jnp.broadcast_to(docs[:, :DH], (16, DH))
    right = jnp.broadcast_to(docs[:, DH:], (16, DH))
    packed = jnp.where(row == 0, left, jnp.where(row == 1, right, 4)).astype(f32).astype(bf16)
    for h in range(4):
        cols = slice(h * DH, (h + 1) * DH)
        out_ref[h, 0:TOK, :] = q_ref[:, cols]
        out_ref[h, TOK : 2 * TOK, :] = k_ref[:, cols]
        out_ref[h, 2 * TOK : 3 * TOK, :] = v_ref[:, cols]
        out_ref[h, 3 * TOK : CHUNK, :] = packed


def pack_heads(token, docs, q, k, v):
    wide = pl.BlockSpec((TOK, 4 * DH), lambda i: (0, i))
    return pl.pallas_call(
        pack_heads_kernel,
        grid=(4,),
        in_specs=[
            pl.BlockSpec(memory_space=pl.ANY),
            pl.BlockSpec((1, TOK), lambda i: (0, 0)),
            wide,
            wide,
            wide,
        ],
        out_specs=pl.BlockSpec((4, CHUNK, DH), lambda i: (i, 0, 0)),
        out_shape=jax.ShapeDtypeStruct((NC, CHUNK, DH), bf16),
        compiler_params=params(),
        cost_estimate=cost(0, 6 << 20),
        name="pack_heads",
    )(token, docs, q, k, v)


def unpack_heads_kernel(x_ref, out_ref):
    for h in range(4):
        out_ref[:, h * DH : (h + 1) * DH] = x_ref[h]


def unpack_heads(x):
    return pl.pallas_call(
        unpack_heads_kernel,
        grid=(4,),
        in_specs=[pl.BlockSpec((4, TOK, DH), lambda i: (i, 0, 0))],
        out_specs=pl.BlockSpec((TOK, 4 * DH), lambda i: (0, i)),
        out_shape=jax.ShapeDtypeStruct((TOK, HD), bf16),
        compiler_params=params(),
        cost_estimate=cost(0, 2 << 20),
        name="unpack_heads",
    )(x)


def self_kernel(x_ref, o_ref):
    docs = x_ref[:, 3 * TOK : CHUNK, :].astype(f32)
    ends = [jnp.sum(jnp.where(docs < d - 0.5, 1.0, 0.0)).astype(i32) for d in (1, 2, 3)]
    per = QT // TOK

    def start_of(p):
        s = jnp.where(p >= ends[0], ends[0], 0)
        s = jnp.maximum(s, jnp.where(p >= ends[1], ends[1], 0))
        return jnp.maximum(s, jnp.where(p >= ends[2], ends[2], 0))

    def rows(j, part):
        return x_ref[pl.ds(per * j, per), part * TOK : (part + 1) * TOK, :].reshape(QT, DH)

    def lanes(p):
        return sum(p[:, c : c + DH] for c in range(0, p.shape[1], DH))

    def query_tile(i, carry):
        base = i * QT
        qs = [x_ref[per * i + u, 0:TOK, :] for u in range(per)]
        columns = [lax.broadcasted_iota(i32, (TOK, 1), 0) + u * TOK for u in range(per)]
        firsts = [start_of(base + c) for c in columns]
        lo = start_of(base) // QT
        mid = jnp.minimum((start_of(base + QT - 1) + QT - 1) // QT, i)

        def step(j, state, kind):
            k, v = rows(j, 1), rows(j, 2)
            ss = []
            for u in range(per):
                width = (u + 1) * TOK if kind == "diagonal" else QT
                s = lax.dot_general(qs[u], k[:width], (((1,), (1,)), ((), ())), preferred_element_type=f32)
                s = s * SCALE
                if kind != "open":
                    local = lax.broadcasted_iota(i32, (TOK, width), 1)
                    seen = local >= firsts[u] - j * QT
                    if kind == "diagonal":
                        seen = seen & (local <= columns[u])
                    s = jnp.where(seen, s, NEG)
                ss.append(s)
            out = []
            for u, s in enumerate(ss):
                new = jnp.max(s, axis=1, keepdims=True)
                if state is not None:
                    acc, top, total = state[u]
                    new = jnp.maximum(top, new)
                p = jnp.exp2(s - new)
                mixed = jnp.dot(p.astype(bf16), v[: s.shape[1]], preferred_element_type=f32)
                weight = lanes(p)
                if state is not None:
                    fade = jnp.exp2(top - new)
                    mixed = acc * fade + mixed
                    weight = total * fade + weight
                out.append((mixed, new, weight))
            return tuple(out)

        state = step(i, None, "diagonal")
        state = lax.fori_loop(lo, mid, functools.partial(step, kind="masked"), state)
        state = lax.fori_loop(mid, i, functools.partial(step, kind="open"), state)
        for u, (acc, top, total) in enumerate(state):
            o_ref[per * i + u] = (acc / jnp.sum(total, axis=1, keepdims=True)).astype(bf16)
        return carry

    lax.fori_loop(0, NC * TOK // QT, query_tile, 0)


def self_attention(x):
    return pl.pallas_call(
        self_kernel,
        in_specs=[pl.BlockSpec(memory_space=pltpu.VMEM)],
        out_specs=pl.BlockSpec(memory_space=pltpu.VMEM),
        out_shape=jax.ShapeDtypeStruct((NC, TOK, DH), bf16),
        compiler_params=params(),
        cost_estimate=cost(16 << 30, 4 << 20),
        name="self_attention",
    )(x)


SHIFTS = (1, 3, 2)


def asked_of(tab_ref, row, owner, value):
    first, second, seen = jnp.int32(0), jnp.int32(0), jnp.int32(0)
    for r in range(8):
        entry = tab_ref[row, r // 2, r % 2]
        hit = entry // 8 == owner
        first = jnp.where(hit & (seen == 0), value(r, entry), first)
        second = jnp.where(hit & (seen == 1), value(r, entry), second)
        seen = seen + jnp.where(hit, 1, 0)
    return first, second


def pack_spans_kernel(tab_ref, keys_ref, values_ref, after_ref, *refs):
    outs, hold, loads, stores = refs[:3], refs[3], refs[4], refs[5]
    me = lax.axis_index("db")
    moves = []
    for i in range(3):
        first, second = asked_of(tab_ref, 1 + i, me, lambda r, entry: entry % 8)
        for slot, span in ((0, first), (1, second)):
            for kind, src in ((0, keys_ref), (1, values_ref)):
                at = (i, slot, kind)
                load = pltpu.make_async_copy(src.at[span], hold.at[at], loads.at[at])
                load.start()
                moves.append((load, pltpu.make_async_copy(hold.at[at], outs[i].at[slot, kind], stores.at[at])))
    for load, store in moves:
        load.wait()
        store.start()
    for load, store in moves:
        store.wait()


def pack_spans(table, keys, values, after):
    anywhere = pl.BlockSpec(memory_space=pl.ANY)
    return pl.pallas_call(
        pack_spans_kernel,
        in_specs=[pl.BlockSpec(memory_space=pltpu.SMEM), anywhere, anywhere, anywhere],
        out_specs=[anywhere] * 3,
        out_shape=[jax.ShapeDtypeStruct((2, 2, CH, HD), bf16)] * 3,
        scratch_shapes=[
            pltpu.VMEM((3, 2, 2, CH, HD), bf16),
            pltpu.SemaphoreType.DMA((3, 2, 2)),
            pltpu.SemaphoreType.DMA((3, 2, 2)),
        ],
        compiler_params=params(),
        cost_estimate=cost(0, 7 << 20),
        name="pack_far",
    )(table, keys, values, after)


def pack_queries_kernel(tab_ref, q_ref, *refs):
    outs, sems = refs[:3], refs[3]
    me = lax.axis_index("db")
    plane, z = me // NZ, me % NZ
    copies = []
    for i, k in enumerate(SHIFTS):
        for slot, n in enumerate(asked_of(tab_ref, 0, plane * NZ + (z + k) % NZ, lambda r, entry: r // 2)):
            src = q_ref.at[pl.ds(pl.multiple_of(n * CH, CH), CH)]
            copy = pltpu.make_async_copy(src, outs[i].at[slot], sems.at[i, slot])
            copy.start()
            copies.append(copy)
    for copy in copies:
        copy.wait()


def pack_queries(asked, q):
    anywhere = pl.BlockSpec(memory_space=pl.ANY)
    return pl.pallas_call(
        pack_queries_kernel,
        in_specs=[pl.BlockSpec(memory_space=pltpu.SMEM), pl.BlockSpec(memory_space=pltpu.VMEM)],
        out_specs=[anywhere] * 3,
        out_shape=[jax.ShapeDtypeStruct((2, CH, HD), bf16)] * 3,
        scratch_shapes=[pltpu.SemaphoreType.DMA((3, 2))],
        compiler_params=params(),
        cost_estimate=cost(0, 3 << 20),
        name="pack_queries",
    )(asked, q)


HEADS = [slice(h * DH, (h + 1) * DH) for h in range(NH)]


def encode(stats, lane):
    high = stats.astype(bf16).astype(f32)
    low = (stats - high).astype(bf16).astype(f32)
    rest = stats - high - low
    return jnp.where(lane < NH, high, jnp.where(lane < 2 * NH, low, rest)).astype(bf16)


def decode(stats):
    stats = stats.astype(f32)
    return (stats[:, :NH] + stats[:, NH : 2 * NH]) + stats[:, 2 * NH : 3 * NH]


def serve_kernel(tab_ref, q_ref, keys_ref, values_ref, *refs):
    got, outs = refs[:3], refs[3:7]
    me = lax.axis_index("db")
    lane = lax.broadcasted_iota(i32, (1, DH), 1)
    for i in range(4):
        row = 0 if i == 3 else 1 + SHIFTS.index(NZ - SHIFTS[i])
        spans = asked_of(tab_ref, row, me, lambda r, entry: entry % 8)
        if i == 3:
            own = asked_of(tab_ref, row, me, lambda r, entry: r // 2)
        for slot, span in enumerate(spans):
            if i == 3:
                toks = pl.ds(pl.multiple_of(own[slot] * CH, CH), CH)
                q = [q_ref[toks, c] for c in HEADS]
            else:
                q = [got[i][slot, :, c] for c in HEADS]
            k = [keys_ref[span, :, c] for c in HEADS]
            s = [
                lax.dot_general(x, y, (((1,), (1,)), ((), ())), preferred_element_type=f32) * SCALE
                for x, y in zip(q, k)
            ]
            top = [jnp.max(x, axis=1, keepdims=True) for x in s]
            p = [jnp.exp2(x - t) for x, t in zip(s, top)]
            total = [jnp.sum(x, axis=1, keepdims=True) for x in p]
            o = [
                jnp.dot(x.astype(bf16), values_ref[span, :, c], preferred_element_type=f32)
                for x, c in zip(p, HEADS)
            ]
            stats = jnp.zeros((CH, DH), f32)
            for h, c in enumerate(HEADS):
                outs[i][slot, :, c] = (o[h] / total[h]).astype(bf16)
                stats = jnp.where(lane % NH == h, top[h] + jnp.log2(total[h]), stats)
            outs[i][slot, :, HD:] = encode(stats, lane)


def serve(table, q, keys, values, got):
    vmem = pl.BlockSpec(memory_space=pltpu.VMEM)
    return pl.pallas_call(
        serve_kernel,
        in_specs=[pl.BlockSpec(memory_space=pltpu.SMEM)] + [vmem] * 6,
        out_specs=[vmem] * 4,
        out_shape=[jax.ShapeDtypeStruct((2, CH, HD + DH), bf16)] * 4,
        compiler_params=params(),
        cost_estimate=cost(4 << 30, 6 << 20),
        name="serve",
    )(table, q, keys, values, *got)


def combine_kernel(tab_ref, *refs):
    got, part_ref, out_ref, hold, sems = refs[:4], refs[4], refs[5], refs[6], refs[7]
    me = lax.axis_index("db")
    plane, z = me // NZ, me % NZ
    here = []
    for r in range(8):
        owner = tab_ref[0, r // 2, r % 2] // 8
        slot = jnp.int32(0)
        for earlier in range(r):
            slot = slot + jnp.where(tab_ref[0, earlier // 2, earlier % 2] // 8 == owner, 1, 0)
        here.append(jnp.where(owner // NZ == plane, 1, 0))
        shift = (owner % NZ - z + NZ) % NZ
        for i, k in enumerate(SHIFTS + (0,)):

            @pl.when(shift == k)
            def _(i=i, slot=slot, r=r):
                pltpu.make_async_copy(got[i].at[slot], hold.at[r], sems.at[r]).start()

    for n in range(4):
        toks = slice(n * CH, (n + 1) * CH)
        lse = [decode(part_ref[toks, HD:])]
        for r in (2 * n, 2 * n + 1):
            pltpu.make_async_copy(got[0].at[0], hold.at[r], sems.at[r]).wait()
            lse.append(jnp.where(here[r] > 0, decode(hold[r, :, HD:]), NEG))
        high = jnp.maximum(jnp.maximum(lse[0], lse[1]), lse[2])
        w = [jnp.exp2(x - high) for x in lse]
        inverse = 1.0 / (w[0] + w[1] + w[2])
        w = [x * inverse for x in w]
        for h, c in enumerate(HEADS):
            a, b, d = (x[:, h : h + 1] for x in w)
            mixed = part_ref[toks, c].astype(f32) * a
            mixed = mixed + hold[2 * n, :, c].astype(f32) * b
            mixed = mixed + hold[2 * n + 1, :, c].astype(f32) * d
            out_ref[toks, c] = mixed.astype(bf16)


def combine(asked, got, part):
    vmem = pl.BlockSpec(memory_space=pltpu.VMEM)
    return pl.pallas_call(
        combine_kernel,
        in_specs=[pl.BlockSpec(memory_space=pltpu.SMEM)] + [pl.BlockSpec(memory_space=pl.ANY)] * 4 + [vmem],
        out_specs=vmem,
        out_shape=jax.ShapeDtypeStruct((TOK, HD), bf16),
        scratch_shapes=[pltpu.VMEM((8, CH, HD + DH), bf16), pltpu.SemaphoreType.DMA((8,))],
        compiler_params=params(),
        cost_estimate=cost(1 << 26, 4 << 20),
        name="combine",
    )(asked, *got, part)


def cross_kernel(tab_ref, q_ref, keys_ref, values_ref, *refs):
    got, out_ref, kbuf, vbuf, sems = refs[:3], refs[3], refs[4], refs[5], refs[6]
    me = lax.axis_index("db")
    plane, z = me // NZ, me % NZ
    row = 0
    here = []
    for r in range(8):
        owner = tab_ref[row, r // 2, r % 2] // 8
        slot = jnp.int32(0)
        for earlier in range(r):
            slot = slot + jnp.where(tab_ref[row, earlier // 2, earlier % 2] // 8 == owner, 1, 0)
        here.append(jnp.where(owner // NZ == plane, 1, 0))
        shift = (z - owner % NZ + NZ) % NZ
        place = pl.ds((r % 2) * CH, CH)
        span = tab_ref[row, r // 2, r % 2] % 8

        @pl.when(shift == 0)
        def _(span=span, place=place, r=r):
            pltpu.make_async_copy(keys_ref.at[span], kbuf.at[r // 2, place], sems.at[r, 0]).start()
            pltpu.make_async_copy(values_ref.at[span], vbuf.at[r // 2, place], sems.at[r, 1]).start()

        for i, k in enumerate(SHIFTS):

            @pl.when(shift == k)
            def _(i=i, slot=slot, place=place, r=r):
                pltpu.make_async_copy(got[i].at[slot, 0], kbuf.at[r // 2, place], sems.at[r, 0]).start()
                pltpu.make_async_copy(got[i].at[slot, 1], vbuf.at[r // 2, place], sems.at[r, 1]).start()

    lane = lax.broadcasted_iota(i32, (1, DH), 1)
    for n in range(4):
        for r in (2 * n, 2 * n + 1):
            place = pl.ds((r % 2) * CH, CH)
            pltpu.make_async_copy(keys_ref.at[0], kbuf.at[n, place], sems.at[r, 0]).wait()
            pltpu.make_async_copy(values_ref.at[0], vbuf.at[n, place], sems.at[r, 1]).wait()
        mine = jnp.where(lane < CH, here[2 * n], here[2 * n + 1]) > 0
        toks = slice(n * CH, (n + 1) * CH)
        heads = [slice(h * DH, (h + 1) * DH) for h in range(NH)]
        s = [
            lax.dot_general(
                q_ref[toks, c], kbuf[n, :, c], (((1,), (1,)), ((), ())), preferred_element_type=f32
            )
            for c in heads
        ]
        s = [jnp.where(mine, x * SCALE, NEG) for x in s]
        top = [jnp.max(x, axis=1, keepdims=True) for x in s]
        p = [jnp.where(mine, jnp.exp2(x - t), 0.0) for x, t in zip(s, top)]
        total = [jnp.sum(x, axis=1, keepdims=True) for x in p]
        o = [jnp.dot(x.astype(bf16), vbuf[n, :, c], preferred_element_type=f32) for x, c in zip(p, heads)]
        stats = jnp.full((CH, DH), NEG, f32)
        for h, c in enumerate(heads):
            safe = jnp.maximum(total[h], 1e-30)
            out_ref[toks, c] = (o[h] / safe).astype(bf16)
            lse = jnp.where(total[h] > 0, top[h] + jnp.log2(safe), NEG)
            stats = jnp.where(lane % NH == h, lse, stats)
        out_ref[toks, HD:] = encode(stats, lane)


def cross(table, q, keys, values, got):
    vmem = pl.BlockSpec(memory_space=pltpu.VMEM)
    return pl.pallas_call(
        cross_kernel,
        in_specs=[pl.BlockSpec(memory_space=pltpu.SMEM), vmem]
        + [pl.BlockSpec(memory_space=pl.ANY)] * 5,
        out_specs=vmem,
        out_shape=jax.ShapeDtypeStruct((TOK, HD + DH), bf16),
        scratch_shapes=[
            pltpu.VMEM((4, 2 * CH, HD), bf16),
            pltpu.VMEM((4, 2 * CH, HD), bf16),
            pltpu.SemaphoreType.DMA((8, 2)),
        ],
        compiler_params=params(),
        cost_estimate=pl.CostEstimate(flops=18 << 30, bytes_accessed=0, transcendentals=0),
        name="cross_far",
    )(table, q, keys, values, *got)


def arrived_kernel(*refs):
    pass


def arrived(xs):
    anywhere = pl.BlockSpec(memory_space=pl.ANY)
    return pl.pallas_call(
        arrived_kernel,
        in_specs=[anywhere] * len(xs),
        out_specs=[anywhere] * len(xs),
        out_shape=[jax.ShapeDtypeStruct(x.shape, x.dtype) for x in xs],
        input_output_aliases={i: i for i in range(len(xs))},
        compiler_params=params(),
        cost_estimate=pl.CostEstimate(flops=32 << 30, bytes_accessed=0, transcendentals=0),
        name="arrived",
    )(*xs)


def per_device(queries, keys, values, doc_ids, nbr_owner, nbr_local, db_keys, db_values):
    q, db_k, db_v = queries[0], db_keys[0], db_values[0]
    swap = [(d, (d + NZ) % 8) for d in range(8)]
    turn = lambda k: [(s * NZ + z, s * NZ + (z + k) % NZ) for s in range(2) for z in range(NZ)]

    asked = lax.optimization_barrier(nbr_owner * 8 + nbr_local)
    table = jnp.concatenate([asked] + [lax.ppermute(asked, "db", turn(NZ - k)) for k in SHIFTS], axis=0)
    table = lax.optimization_barrier(table)
    far_table = lax.ppermute(table, "db", swap)
    sent = pack_queries(table, q)
    swapped, far_table = lax.optimization_barrier((q, far_table))
    far_q = lax.ppermute(swapped, "db", swap)
    packed = pack_heads(sent[0], doc_ids, q, keys[0], values[0])
    sent = [lax.ppermute(x, "db", turn(k)) for x, k in zip(sent, SHIFTS)]
    heads = lax.all_to_all(packed, "ctx", split_axis=0, concat_axis=0, tiled=True)

    far = list(pack_spans(far_table, db_k, db_v, packed))
    for i in range(3):
        far[i], sent[i] = lax.optimization_barrier((far[i], sent[i]))
    far_got = [lax.ppermute(x, "db", turn(k)) for x, k in zip(far, SHIFTS)]
    *near, own = serve(table, q, db_k, db_v, sent)
    near_got = [lax.ppermute(x, "db", turn(NZ - k)) for x, k in zip(near, SHIFTS)]
    part = lax.ppermute(cross(far_table, far_q, db_k, db_v, far_got), "db", swap)

    self_rows = self_attention(heads)
    self_rows = lax.all_to_all(self_rows, "ctx", split_axis=0, concat_axis=0, tiled=True)
    self_rows = unpack_heads(self_rows)

    near_got = arrived(near_got)
    cross_rows = combine(asked, list(near_got) + [own], part)
    return self_rows[None], cross_rows[None]


def solution(mesh):
    rows = P("db", "ctx", None)
    spans = P("db", "ctx", None, None)
    return jax.shard_map(
        per_device,
        mesh=mesh,
        in_specs=(rows, rows, rows, P("db", "ctx"), rows, rows, spans, spans),
        out_specs=(rows, rows),
        check_vma=False,
    )
```

```python
import functools
import math

import jax
import jax.numpy as jnp
from jax import lax
from jax.experimental import pallas as pl
from jax.experimental.pallas import tpu as pltpu
from jax.sharding import PartitionSpec as P

DH = 128
CH = 64
NH = 16
TOK = 256
HD = 2048
NZ = 4
NC = 16
QT = 2048
CHUNK = 3 * TOK + 16
NEG = -1e30
SCALE = math.log2(math.e) / math.sqrt(DH)
VMEM = 48 << 20

f32, bf16, i32 = jnp.float32, jnp.bfloat16, jnp.int32


def params():
    return pltpu.CompilerParams(vmem_limit_bytes=VMEM)


def cost(flops, nbytes):
    return pl.CostEstimate(flops=flops // 64, bytes_accessed=nbytes // 16, transcendentals=0)


def pack_heads_kernel(token_ref, docs_ref, q_ref, k_ref, v_ref, out_ref):
    row = lax.broadcasted_iota(i32, (16, DH), 0)
    docs = docs_ref[...]
    left = jnp.broadcast_to(docs[:, :DH], (16, DH))
    right = jnp.broadcast_to(docs[:, DH:], (16, DH))
    packed = jnp.where(row == 0, left, jnp.where(row == 1, right, 4)).astype(f32).astype(bf16)
    for h in range(4):
        cols = slice(h * DH, (h + 1) * DH)
        out_ref[h, 0:TOK, :] = q_ref[:, cols]
        out_ref[h, TOK : 2 * TOK, :] = k_ref[:, cols]
        out_ref[h, 2 * TOK : 3 * TOK, :] = v_ref[:, cols]
        out_ref[h, 3 * TOK : CHUNK, :] = packed


def pack_heads(token, docs, q, k, v):
    wide = pl.BlockSpec((TOK, 4 * DH), lambda i: (0, i))
    return pl.pallas_call(
        pack_heads_kernel,
        grid=(4,),
        in_specs=[
            pl.BlockSpec((2, 4, 2), lambda i: (0, 0, 0)),
            pl.BlockSpec((1, TOK), lambda i: (0, 0)),
            wide,
            wide,
            wide,
        ],
        out_specs=pl.BlockSpec((4, CHUNK, DH), lambda i: (i, 0, 0)),
        out_shape=jax.ShapeDtypeStruct((NC, CHUNK, DH), bf16),
        compiler_params=params(),
        cost_estimate=cost(0, 6 << 20),
        name="pack_heads",
    )(token, docs, q, k, v)


def unpack_heads_kernel(x_ref, out_ref):
    for h in range(4):
        out_ref[:, h * DH : (h + 1) * DH] = x_ref[h]


def unpack_heads(x):
    return pl.pallas_call(
        unpack_heads_kernel,
        grid=(4,),
        in_specs=[pl.BlockSpec((4, TOK, DH), lambda i: (i, 0, 0))],
        out_specs=pl.BlockSpec((TOK, 4 * DH), lambda i: (0, i)),
        out_shape=jax.ShapeDtypeStruct((TOK, HD), bf16),
        compiler_params=params(),
        cost_estimate=cost(0, 2 << 20),
        name="unpack_heads",
    )(x)


def self_kernel(x_ref, o_ref):
    docs = x_ref[:, 3 * TOK : CHUNK, :].astype(f32)
    ends = [jnp.sum(jnp.where(docs < d - 0.5, 1.0, 0.0)).astype(i32) for d in (1, 2, 3)]
    per = QT // TOK

    def start_of(p):
        s = jnp.where(p >= ends[0], ends[0], 0)
        s = jnp.maximum(s, jnp.where(p >= ends[1], ends[1], 0))
        return jnp.maximum(s, jnp.where(p >= ends[2], ends[2], 0))

    def rows(j, part):
        return x_ref[pl.ds(per * j, per), part * TOK : (part + 1) * TOK, :].reshape(QT, DH)

    def lanes(p):
        return sum(p[:, c : c + DH] for c in range(0, p.shape[1], DH))

    def query_tile(i, carry):
        base = i * QT
        qs = [x_ref[per * i + u, 0:TOK, :] for u in range(per)]
        columns = [lax.broadcasted_iota(i32, (TOK, 1), 0) + u * TOK for u in range(per)]
        firsts = [start_of(base + c) for c in columns]
        lo = start_of(base) // QT
        mid = jnp.minimum((start_of(base + QT - 1) + QT - 1) // QT, i)

        def step(j, state, kind):
            k, v = rows(j, 1), rows(j, 2)
            ss = []
            for u in range(per):
                width = (u + 1) * TOK if kind == "diagonal" else QT
                s = lax.dot_general(qs[u], k[:width], (((1,), (1,)), ((), ())), preferred_element_type=f32)
                s = s * SCALE
                if kind != "open":
                    local = lax.broadcasted_iota(i32, (TOK, width), 1)
                    seen = local >= firsts[u] - j * QT
                    if kind == "diagonal":
                        seen = seen & (local <= columns[u])
                    s = jnp.where(seen, s, NEG)
                ss.append(s)
            out = []
            for u, s in enumerate(ss):
                new = jnp.max(s, axis=1, keepdims=True)
                if state is not None:
                    acc, top, total = state[u]
                    new = jnp.maximum(top, new)
                p = jnp.exp2(s - new)
                mixed = jnp.dot(p.astype(bf16), v[: s.shape[1]], preferred_element_type=f32)
                weight = lanes(p)
                if state is not None:
                    fade = jnp.exp2(top - new)
                    mixed = acc * fade + mixed
                    weight = total * fade + weight
                out.append((mixed, new, weight))
            return tuple(out)

        state = step(i, None, "diagonal")
        state = lax.fori_loop(lo, mid, functools.partial(step, kind="masked"), state)
        state = lax.fori_loop(mid, i, functools.partial(step, kind="open"), state)
        for u, (acc, top, total) in enumerate(state):
            o_ref[per * i + u] = (acc / jnp.sum(total, axis=1, keepdims=True)).astype(bf16)
        return carry

    lax.fori_loop(0, NC * TOK // QT, query_tile, 0)


def self_attention(x):
    return pl.pallas_call(
        self_kernel,
        in_specs=[pl.BlockSpec(memory_space=pltpu.VMEM)],
        out_specs=pl.BlockSpec(memory_space=pltpu.VMEM),
        out_shape=jax.ShapeDtypeStruct((NC, TOK, DH), bf16),
        compiler_params=params(),
        cost_estimate=cost(16 << 30, 4 << 20),
        name="self_attention",
    )(x)


SHIFTS = (1, 3, 2)


def pack_spans_kernel(far, *refs):
    tabs, keys_ref, values_ref = refs[:3], refs[3], refs[4]
    outs, hold, loads, stores = refs[5:8], refs[8], refs[9], refs[10]
    me = lax.axis_index("db")
    moves = []
    for i in range(3):
        first, second, seen = jnp.int32(0), jnp.int32(0), jnp.int32(0)
        for r in range(8):
            entry = tabs[i][far, r // 2, r % 2]
            hit = entry // 8 == me
            span = entry % 8
            first = jnp.where(hit & (seen == 0), span, first)
            second = jnp.where(hit & (seen == 1), span, second)
            seen = seen + jnp.where(hit, 1, 0)
        for slot, span in ((0, first), (1, second)):
            for kind, src in ((0, keys_ref), (1, values_ref)):
                at = (i, slot, kind)
                load = pltpu.make_async_copy(src.at[span], hold.at[at], loads.at[at])
                load.start()
                moves.append((load, pltpu.make_async_copy(hold.at[at], outs[i].at[slot, kind], stores.at[at])))
    for load, store in moves:
        load.wait()
        store.start()
    for load, store in moves:
        store.wait()


def pack_spans(far, tables, keys, values):
    anywhere = pl.BlockSpec(memory_space=pl.ANY)
    return pl.pallas_call(
        functools.partial(pack_spans_kernel, int(far)),
        in_specs=[pl.BlockSpec(memory_space=pltpu.SMEM)] * 3 + [anywhere, anywhere],
        out_specs=[anywhere] * 3,
        out_shape=[jax.ShapeDtypeStruct((2, 2, CH, HD), bf16)] * 3,
        scratch_shapes=[
            pltpu.VMEM((3, 2, 2, CH, HD), bf16),
            pltpu.SemaphoreType.DMA((3, 2, 2)),
            pltpu.SemaphoreType.DMA((3, 2, 2)),
        ],
        compiler_params=pltpu.CompilerParams(vmem_limit_bytes=60 << 20),
        cost_estimate=cost(0, 7 << 20),
        name="pack_far" if far else "pack_near",
    )(*tables, keys, values)


def cross_kernel(far, tab_ref, q_ref, *refs):
    keys_ref, values_ref = refs[:2]
    got = refs[2:5]
    if far:
        out_ref, kbuf, vbuf, sems = refs[5:]
    else:
        part_ref, out_ref, kbuf, vbuf, sems = refs[5:]
    me = lax.axis_index("db")
    plane, z = me // NZ, me % NZ
    row = 1 if far else 0
    here = []
    for r in range(8):
        owner = tab_ref[row, r // 2, r % 2] // 8
        slot = jnp.int32(0)
        for earlier in range(r):
            slot = slot + jnp.where(tab_ref[row, earlier // 2, earlier % 2] // 8 == owner, 1, 0)
        here.append(jnp.where(owner // NZ == plane, 1, 0))
        shift = (z - owner % NZ + NZ) % NZ
        place = pl.ds((r % 2) * CH, CH)
        span = tab_ref[row, r // 2, r % 2] % 8

        @pl.when(shift == 0)
        def _(span=span, place=place, r=r):
            pltpu.make_async_copy(keys_ref.at[span], kbuf.at[r // 2, place], sems.at[r, 0]).start()
            pltpu.make_async_copy(values_ref.at[span], vbuf.at[r // 2, place], sems.at[r, 1]).start()

        for i, k in enumerate(SHIFTS):

            @pl.when(shift == k)
            def _(i=i, slot=slot, place=place, r=r):
                pltpu.make_async_copy(got[i].at[slot, 0], kbuf.at[r // 2, place], sems.at[r, 0]).start()
                pltpu.make_async_copy(got[i].at[slot, 1], vbuf.at[r // 2, place], sems.at[r, 1]).start()

    lane = lax.broadcasted_iota(i32, (1, DH), 1)
    for n in range(4):
        for r in (2 * n, 2 * n + 1):
            place = pl.ds((r % 2) * CH, CH)
            pltpu.make_async_copy(keys_ref.at[0], kbuf.at[n, place], sems.at[r, 0]).wait()
            pltpu.make_async_copy(values_ref.at[0], vbuf.at[n, place], sems.at[r, 1]).wait()
        mine = jnp.where(lane < CH, here[2 * n], here[2 * n + 1]) > 0
        toks = slice(n * CH, (n + 1) * CH)
        heads = [slice(h * DH, (h + 1) * DH) for h in range(NH)]
        s = [
            lax.dot_general(
                q_ref[toks, c], kbuf[n, :, c], (((1,), (1,)), ((), ())), preferred_element_type=f32
            )
            for c in heads
        ]
        s = [jnp.where(mine, x * SCALE, NEG) for x in s]
        top = [jnp.max(x, axis=1, keepdims=True) for x in s]
        p = [jnp.where(mine, jnp.exp2(x - t), 0.0) for x, t in zip(s, top)]
        total = [jnp.sum(x, axis=1, keepdims=True) for x in p]
        o = [jnp.dot(x.astype(bf16), vbuf[n, :, c], preferred_element_type=f32) for x, c in zip(p, heads)]
        if far:
            stats = jnp.full((CH, DH), NEG, f32)
            for h, c in enumerate(heads):
                safe = jnp.maximum(total[h], 1e-30)
                out_ref[toks, c] = (o[h] / safe).astype(bf16)
                lse = jnp.where(total[h] > 0, top[h] + jnp.log2(safe), NEG)
                stats = jnp.where(lane % NH == h, lse, stats)
            high = stats.astype(bf16).astype(f32)
            low = (stats - high).astype(bf16).astype(f32)
            rest = stats - high - low
            stats = jnp.where(lane < NH, high, jnp.where(lane < 2 * NH, low, rest))
            out_ref[toks, HD:] = stats.astype(bf16)
        else:
            stats = part_ref[toks, HD:].astype(f32)
            other = (stats[:, :NH] + stats[:, NH : 2 * NH]) + stats[:, 2 * NH : 3 * NH]
            tops = jnp.full((CH, NH), NEG, f32)
            sums = jnp.zeros((CH, NH), f32)
            slot = lax.broadcasted_iota(i32, (1, NH), 1)
            for h in range(NH):
                tops = jnp.where(slot == h, top[h], tops)
                sums = jnp.where(slot == h, total[h], sums)
            high = jnp.maximum(tops, other)
            a, b = jnp.exp2(tops - high), jnp.exp2(other - high)
            inverse = 1.0 / (sums * a + b)
            a, b = a * inverse, b * inverse
            for h, c in enumerate(heads):
                mixed = o[h] * a[:, h : h + 1] + part_ref[toks, c].astype(f32) * b[:, h : h + 1]
                out_ref[toks, c] = mixed.astype(bf16)


def cross(far, table, q, keys, values, got, part=()):
    vmem = pl.BlockSpec(memory_space=pltpu.VMEM)
    return pl.pallas_call(
        functools.partial(cross_kernel, far),
        in_specs=[pl.BlockSpec(memory_space=pltpu.SMEM), vmem]
        + [pl.BlockSpec(memory_space=pl.ANY)] * 5
        + [vmem] * len(part),
        out_specs=vmem,
        out_shape=jax.ShapeDtypeStruct((TOK, HD + DH if far else HD), bf16),
        scratch_shapes=[
            pltpu.VMEM((4, 2 * CH, HD), bf16),
            pltpu.VMEM((4, 2 * CH, HD), bf16),
            pltpu.SemaphoreType.DMA((8, 2)),
        ],
        compiler_params=params(),
        cost_estimate=pl.CostEstimate(flops=32 << 30 if far else 1 << 26, bytes_accessed=0, transcendentals=0),
        name="cross_far" if far else "cross_near",
    )(table, q, keys, values, *got, *part)


def arrived_kernel(*refs):
    pass


def arrived(xs):
    anywhere = pl.BlockSpec(memory_space=pl.ANY)
    return pl.pallas_call(
        arrived_kernel,
        in_specs=[anywhere] * len(xs),
        out_specs=[anywhere] * len(xs),
        out_shape=[jax.ShapeDtypeStruct(x.shape, x.dtype) for x in xs],
        input_output_aliases={i: i for i in range(len(xs))},
        compiler_params=params(),
        cost_estimate=pl.CostEstimate(flops=32 << 30, bytes_accessed=0, transcendentals=0),
        name="arrived",
    )(*xs)


def per_device(queries, keys, values, doc_ids, nbr_owner, nbr_local, db_keys, db_values):
    q, db_k, db_v = queries[0], db_keys[0], db_values[0]
    swap = [(d, (d + NZ) % 8) for d in range(8)]
    turn = lambda k: [(s * NZ + z, s * NZ + (z + k) % NZ) for s in range(2) for z in range(NZ)]
    far_q = lax.ppermute(q, "db", swap)

    asked = lax.optimization_barrier(nbr_owner * 8 + nbr_local)
    table = jnp.concatenate([asked, lax.ppermute(asked, "db", swap)], axis=0)
    tables = [lax.ppermute(table, "db", turn(NZ - k)) for k in SHIFTS]
    far = pack_spans(True, tables, db_k, db_v)
    far_got = [lax.ppermute(x, "db", turn(k)) for x, k in zip(far, SHIFTS)]

    heads = pack_heads(table, doc_ids, q, keys[0], values[0])
    heads = lax.all_to_all(heads, "ctx", split_axis=0, concat_axis=0, tiled=True)

    near = pack_spans(False, tables, db_k, db_v)
    near_got = []
    for i, k in enumerate(SHIFTS):
        near_got.append(lax.ppermute(near[i], "db", turn(k)))
    part = lax.ppermute(cross(True, table, far_q, db_k, db_v, far_got), "db", swap)

    self_rows = self_attention(heads)
    self_rows = lax.all_to_all(self_rows, "ctx", split_axis=0, concat_axis=0, tiled=True)
    self_rows = unpack_heads(self_rows)

    near_got = arrived(near_got)
    cross_rows = cross(False, table, q, db_k, db_v, near_got, (part,))
    return self_rows[None], cross_rows[None]


def solution(mesh):
    rows = P("db", "ctx", None)
    spans = P("db", "ctx", None, None)
    return jax.shard_map(
        per_device,
        mesh=mesh,
        in_specs=(rows, rows, rows, P("db", "ctx"), rows, rows, spans, spans),
        out_specs=(rows, rows),
        check_vma=False,
    )
```

```python
import functools
import math

import jax
import jax.numpy as jnp
from jax import lax
from jax.experimental import pallas as pl
from jax.experimental.pallas import tpu as pltpu
from jax.sharding import PartitionSpec as P

DH = 128
CH = 64
NH = 16
TOK = 256
HD = 2048
NZ = 4
NC = 16
QT = 2048
CHUNK = 3 * TOK + 16
NEG = -1e30
SCALE = math.log2(math.e) / math.sqrt(DH)
VMEM = 48 << 20

f32, bf16, i32 = jnp.float32, jnp.bfloat16, jnp.int32


def params():
    return pltpu.CompilerParams(vmem_limit_bytes=VMEM)


def cost(flops, nbytes):
    return pl.CostEstimate(flops=flops // 64, bytes_accessed=nbytes // 16, transcendentals=0)


def pack_heads_kernel(token_ref, docs_ref, q_ref, k_ref, v_ref, out_ref):
    row = lax.broadcasted_iota(i32, (16, DH), 0)
    docs = docs_ref[...]
    left = jnp.broadcast_to(docs[:, :DH], (16, DH))
    right = jnp.broadcast_to(docs[:, DH:], (16, DH))
    packed = jnp.where(row == 0, left, jnp.where(row == 1, right, 4)).astype(f32).astype(bf16)
    for h in range(4):
        cols = slice(h * DH, (h + 1) * DH)
        out_ref[h, 0:TOK, :] = q_ref[:, cols]
        out_ref[h, TOK : 2 * TOK, :] = k_ref[:, cols]
        out_ref[h, 2 * TOK : 3 * TOK, :] = v_ref[:, cols]
        out_ref[h, 3 * TOK : CHUNK, :] = packed


def pack_heads(token, docs, q, k, v):
    wide = pl.BlockSpec((TOK, 4 * DH), lambda i: (0, i))
    return pl.pallas_call(
        pack_heads_kernel,
        grid=(4,),
        in_specs=[
            pl.BlockSpec((2, 4, 2), lambda i: (0, 0, 0)),
            pl.BlockSpec((1, TOK), lambda i: (0, 0)),
            wide,
            wide,
            wide,
        ],
        out_specs=pl.BlockSpec((4, CHUNK, DH), lambda i: (i, 0, 0)),
        out_shape=jax.ShapeDtypeStruct((NC, CHUNK, DH), bf16),
        compiler_params=params(),
        cost_estimate=cost(0, 6 << 20),
        name="pack_heads",
    )(token, docs, q, k, v)


def unpack_heads_kernel(x_ref, out_ref):
    for h in range(4):
        out_ref[:, h * DH : (h + 1) * DH] = x_ref[h]


def unpack_heads(x):
    return pl.pallas_call(
        unpack_heads_kernel,
        grid=(4,),
        in_specs=[pl.BlockSpec((4, TOK, DH), lambda i: (i, 0, 0))],
        out_specs=pl.BlockSpec((TOK, 4 * DH), lambda i: (0, i)),
        out_shape=jax.ShapeDtypeStruct((TOK, HD), bf16),
        compiler_params=params(),
        cost_estimate=cost(0, 2 << 20),
        name="unpack_heads",
    )(x)


def self_kernel(x_ref, o_ref):
    docs = x_ref[:, 3 * TOK : CHUNK, :].astype(f32)
    ends = [jnp.sum(jnp.where(docs < d - 0.5, 1.0, 0.0)).astype(i32) for d in (1, 2, 3)]
    per = QT // TOK

    def start_of(p):
        s = jnp.where(p >= ends[0], ends[0], 0)
        s = jnp.maximum(s, jnp.where(p >= ends[1], ends[1], 0))
        return jnp.maximum(s, jnp.where(p >= ends[2], ends[2], 0))

    def rows(j, part):
        return x_ref[pl.ds(per * j, per), part * TOK : (part + 1) * TOK, :].reshape(QT, DH)

    def lanes(p):
        return sum(p[:, c : c + DH] for c in range(0, p.shape[1], DH))

    def query_tile(i, carry):
        base = i * QT
        qs = [x_ref[per * i + u, 0:TOK, :] for u in range(per)]
        columns = [lax.broadcasted_iota(i32, (TOK, 1), 0) + u * TOK for u in range(per)]
        firsts = [start_of(base + c) for c in columns]
        lo = start_of(base) // QT
        mid = jnp.minimum((start_of(base + QT - 1) + QT - 1) // QT, i)

        def step(j, state, kind):
            k, v = rows(j, 1), rows(j, 2)
            ss = []
            for u in range(per):
                width = (u + 1) * TOK if kind == "diagonal" else QT
                s = lax.dot_general(qs[u], k[:width], (((1,), (1,)), ((), ())), preferred_element_type=f32)
                s = s * SCALE
                if kind != "open":
                    local = lax.broadcasted_iota(i32, (TOK, width), 1)
                    seen = local >= firsts[u] - j * QT
                    if kind == "diagonal":
                        seen = seen & (local <= columns[u])
                    s = jnp.where(seen, s, NEG)
                ss.append(s)
            out = []
            for u, s in enumerate(ss):
                new = jnp.max(s, axis=1, keepdims=True)
                if state is not None:
                    acc, top, total = state[u]
                    new = jnp.maximum(top, new)
                p = jnp.exp2(s - new)
                mixed = jnp.dot(p.astype(bf16), v[: s.shape[1]], preferred_element_type=f32)
                weight = lanes(p)
                if state is not None:
                    fade = jnp.exp2(top - new)
                    mixed = acc * fade + mixed
                    weight = total * fade + weight
                out.append((mixed, new, weight))
            return tuple(out)

        state = step(i, None, "diagonal")
        state = lax.fori_loop(lo, mid, functools.partial(step, kind="masked"), state)
        state = lax.fori_loop(mid, i, functools.partial(step, kind="open"), state)
        for u, (acc, top, total) in enumerate(state):
            o_ref[per * i + u] = (acc / jnp.sum(total, axis=1, keepdims=True)).astype(bf16)
        return carry

    lax.fori_loop(0, NC * TOK // QT, query_tile, 0)


def self_attention(x):
    return pl.pallas_call(
        self_kernel,
        in_specs=[pl.BlockSpec(memory_space=pltpu.VMEM)],
        out_specs=pl.BlockSpec(memory_space=pltpu.VMEM),
        out_shape=jax.ShapeDtypeStruct((NC, TOK, DH), bf16),
        compiler_params=params(),
        cost_estimate=cost(16 << 30, 4 << 20),
        name="self_attention",
    )(x)


SHIFTS = (1, 3, 2)


def pack_spans_kernel(far, *refs):
    tab_ref, keys_ref, values_ref = refs[:3]
    outs, hold, loads, stores = refs[3:6], refs[6], refs[7], refs[8]
    me = lax.axis_index("db")
    moves = []
    for i in range(3):
        first, second, seen = jnp.int32(0), jnp.int32(0), jnp.int32(0)
        for r in range(8):
            entry = tab_ref[2 * i + far, r // 2, r % 2]
            hit = (entry >> 3) == me
            span = entry & 7
            first = jnp.where(hit & (seen == 0), span, first)
            second = jnp.where(hit & (seen == 1), span, second)
            seen = seen + jnp.where(hit, 1, 0)
        for slot, span in ((0, first), (1, second)):
            for kind, src in ((0, keys_ref), (1, values_ref)):
                at = (i, slot, kind)
                load = pltpu.make_async_copy(src.at[span], hold.at[at], loads.at[at])
                load.start()
                moves.append((load, pltpu.make_async_copy(hold.at[at], outs[i].at[slot, kind], stores.at[at])))
    for load, store in moves:
        load.wait()
        store.start()
    for load, store in moves:
        store.wait()


def pack_spans(far, table, keys, values):
    anywhere = pl.BlockSpec(memory_space=pl.ANY)
    return pl.pallas_call(
        functools.partial(pack_spans_kernel, int(far)),
        in_specs=[pl.BlockSpec(memory_space=pltpu.SMEM), anywhere, anywhere],
        out_specs=[anywhere] * 3,
        out_shape=[jax.ShapeDtypeStruct((2, 2, CH, HD), bf16)] * 3,
        scratch_shapes=[
            pltpu.VMEM((3, 2, 2, CH, HD), bf16),
            pltpu.SemaphoreType.DMA((3, 2, 2)),
            pltpu.SemaphoreType.DMA((3, 2, 2)),
        ],
        compiler_params=pltpu.CompilerParams(vmem_limit_bytes=60 << 20),
        cost_estimate=cost(0, 7 << 20),
        name="pack_far" if far else "pack_near",
    )(table, keys, values)


def cross_kernel(far, tab_ref, q_ref, *refs):
    keys_ref, values_ref = refs[:2]
    got = refs[2:5]
    if far:
        out_ref, kbuf, vbuf, sems = refs[5:]
    else:
        part_ref, out_ref, kbuf, vbuf, sems = refs[5:]
    me = lax.axis_index("db")
    plane, z = me >> 2, me & 3
    row = 1 if far else 0
    here = []
    entries = [tab_ref[row, r // 2, r % 2] for r in range(8)]
    owners = [entry >> 3 for entry in entries]
    for r in range(8):
        owner = owners[r]
        slot = jnp.int32(0)
        for earlier in range(r):
            slot = slot + jnp.where(owners[earlier] == owner, 1, 0)
        here.append(jnp.where((owner >> 2) == plane, 1, 0))
        shift = (z - owner) & 3
        place = pl.ds((r % 2) * CH, CH)
        span = entries[r] & 7

        @pl.when(shift == 0)
        def _(span=span, place=place, r=r):
            pltpu.make_async_copy(keys_ref.at[span], kbuf.at[r // 2, place], sems.at[r, 0]).start()
            pltpu.make_async_copy(values_ref.at[span], vbuf.at[r // 2, place], sems.at[r, 1]).start()

        for i, k in enumerate(SHIFTS):

            @pl.when(shift == k)
            def _(i=i, slot=slot, place=place, r=r):
                pltpu.make_async_copy(got[i].at[slot, 0], kbuf.at[r // 2, place], sems.at[r, 0]).start()
                pltpu.make_async_copy(got[i].at[slot, 1], vbuf.at[r // 2, place], sems.at[r, 1]).start()

    lane = lax.broadcasted_iota(i32, (1, DH), 1)
    for n in range(4):
        for r in (2 * n, 2 * n + 1):
            place = pl.ds((r % 2) * CH, CH)
            pltpu.make_async_copy(keys_ref.at[0], kbuf.at[n, place], sems.at[r, 0]).wait()
            pltpu.make_async_copy(values_ref.at[0], vbuf.at[n, place], sems.at[r, 1]).wait()
        mine = jnp.where(lane < CH, here[2 * n], here[2 * n + 1]) > 0
        toks = slice(n * CH, (n + 1) * CH)
        heads = [slice(h * DH, (h + 1) * DH) for h in range(NH)]
        s = [
            lax.dot_general(
                q_ref[toks, c], kbuf[n, :, c], (((1,), (1,)), ((), ())), preferred_element_type=f32
            )
            for c in heads
        ]
        s = [jnp.where(mine, x * SCALE, NEG) for x in s]
        top = [jnp.max(x, axis=1, keepdims=True) for x in s]
        p = [jnp.where(mine, jnp.exp2(x - t), 0.0) for x, t in zip(s, top)]
        total = [jnp.sum(x, axis=1, keepdims=True) for x in p]
        o = [jnp.dot(x.astype(bf16), vbuf[n, :, c], preferred_element_type=f32) for x, c in zip(p, heads)]
        if far:
            stats = jnp.full((CH, DH), NEG, f32)
            for h, c in enumerate(heads):
                safe = jnp.maximum(total[h], 1e-30)
                out_ref[toks, c] = (o[h] / safe).astype(bf16)
                lse = jnp.where(total[h] > 0, top[h] + jnp.log2(safe), NEG)
                stats = jnp.where(lane % NH == h, lse, stats)
            high = stats.astype(bf16).astype(f32)
            low = (stats - high).astype(bf16).astype(f32)
            rest = stats - high - low
            stats = jnp.where(lane < NH, high, jnp.where(lane < 2 * NH, low, rest))
            out_ref[toks, HD:] = stats.astype(bf16)
        else:
            stats = part_ref[toks, HD:].astype(f32)
            other = (stats[:, :NH] + stats[:, NH : 2 * NH]) + stats[:, 2 * NH : 3 * NH]
            tops = jnp.full((CH, NH), NEG, f32)
            sums = jnp.zeros((CH, NH), f32)
            slot = lax.broadcasted_iota(i32, (1, NH), 1)
            for h in range(NH):
                tops = jnp.where(slot == h, top[h], tops)
                sums = jnp.where(slot == h, total[h], sums)
            high = jnp.maximum(tops, other)
            a, b = jnp.exp2(tops - high), jnp.exp2(other - high)
            inverse = 1.0 / (sums * a + b)
            a, b = a * inverse, b * inverse
            for h, c in enumerate(heads):
                mixed = o[h] * a[:, h : h + 1] + part_ref[toks, c].astype(f32) * b[:, h : h + 1]
                out_ref[toks, c] = mixed.astype(bf16)


def cross(far, table, q, keys, values, got, part=()):
    vmem = pl.BlockSpec(memory_space=pltpu.VMEM)
    return pl.pallas_call(
        functools.partial(cross_kernel, far),
        in_specs=[pl.BlockSpec(memory_space=pltpu.SMEM), vmem]
        + [pl.BlockSpec(memory_space=pl.ANY)] * 5
        + [vmem] * len(part),
        out_specs=vmem,
        out_shape=jax.ShapeDtypeStruct((TOK, HD + DH if far else HD), bf16),
        scratch_shapes=[
            pltpu.VMEM((4, 2 * CH, HD), bf16),
            pltpu.VMEM((4, 2 * CH, HD), bf16),
            pltpu.SemaphoreType.DMA((8, 2)),
        ],
        compiler_params=params(),
        cost_estimate=pl.CostEstimate(flops=32 << 30 if far else 1 << 26, bytes_accessed=0, transcendentals=0),
        name="cross_far" if far else "cross_near",
    )(table, q, keys, values, *got, *part)


def arrived_kernel(*refs):
    pass


def arrived(xs):
    anywhere = pl.BlockSpec(memory_space=pl.ANY)
    return pl.pallas_call(
        arrived_kernel,
        in_specs=[anywhere] * len(xs),
        out_specs=[anywhere] * len(xs),
        out_shape=[jax.ShapeDtypeStruct(x.shape, x.dtype) for x in xs],
        input_output_aliases={i: i for i in range(len(xs))},
        compiler_params=params(),
        cost_estimate=pl.CostEstimate(flops=32 << 30, bytes_accessed=0, transcendentals=0),
        name="arrived",
    )(*xs)


def per_device(queries, keys, values, doc_ids, nbr_owner, nbr_local, db_keys, db_values):
    q, db_k, db_v = queries[0], db_keys[0], db_values[0]
    swap = [(d, (d + NZ) % 8) for d in range(8)]
    turn = lambda k: [(s * NZ + z, s * NZ + (z + k) % NZ) for s in range(2) for z in range(NZ)]
    far_q = lax.ppermute(q, "db", swap)

    asked = lax.optimization_barrier(nbr_owner * 8 + nbr_local)
    table = jnp.concatenate([asked, lax.ppermute(asked, "db", swap)], axis=0)
    tables = jnp.concatenate([lax.ppermute(table, "db", turn(NZ - k)) for k in SHIFTS], axis=0)
    far = pack_spans(True, tables, db_k, db_v)
    far_got = [lax.ppermute(x, "db", turn(k)) for x, k in zip(far, SHIFTS)]

    heads = pack_heads(table, doc_ids, q, keys[0], values[0])
    heads = lax.all_to_all(heads, "ctx", split_axis=0, concat_axis=0, tiled=True)

    near = pack_spans(False, tables, db_k, db_v)
    near_got = []
    for i, k in enumerate(SHIFTS):
        near_got.append(lax.ppermute(near[i], "db", turn(k)))
    part = lax.ppermute(cross(True, table, far_q, db_k, db_v, far_got), "db", swap)

    self_rows = self_attention(heads)
    self_rows = lax.all_to_all(self_rows, "ctx", split_axis=0, concat_axis=0, tiled=True)
    self_rows = unpack_heads(self_rows)

    near_got = arrived(near_got)
    cross_rows = cross(False, table, q, db_k, db_v, near_got, (part,))
    return self_rows[None], cross_rows[None]


def solution(mesh):
    rows = P("db", "ctx", None)
    spans = P("db", "ctx", None, None)
    return jax.shard_map(
        per_device,
        mesh=mesh,
        in_specs=(rows, rows, rows, P("db", "ctx"), rows, rows, spans, spans),
        out_specs=(rows, rows),
        check_vma=False,
    )
```

```python
import functools
import math

import jax
import jax.numpy as jnp
from jax import lax
from jax.experimental import pallas as pl
from jax.experimental.pallas import tpu as pltpu
from jax.sharding import PartitionSpec as P

DH = 128
CH = 64
NH = 16
TOK = 256
HD = 2048
NZ = 4
NC = 16
QT = 2048
CHUNK = 3 * TOK + 16
NEG = -1e30
SCALE = math.log2(math.e) / math.sqrt(DH)
VMEM = 48 << 20
GRANT = 60

f32, bf16, i32 = jnp.float32, jnp.bfloat16, jnp.int32


def params():
    return pltpu.CompilerParams(vmem_limit_bytes=VMEM)


def cost(flops, nbytes):
    return pl.CostEstimate(flops=flops // 64, bytes_accessed=nbytes // 16, transcendentals=0)


def pack_heads_kernel(token_ref, docs_ref, q_ref, k_ref, v_ref, out_ref):
    row = lax.broadcasted_iota(i32, (16, DH), 0)
    docs = docs_ref[...]
    left = jnp.broadcast_to(docs[:, :DH], (16, DH))
    right = jnp.broadcast_to(docs[:, DH:], (16, DH))
    packed = jnp.where(row == 0, left, jnp.where(row == 1, right, 4)).astype(f32).astype(bf16)
    for h in range(4):
        cols = slice(h * DH, (h + 1) * DH)
        out_ref[h, 0:TOK, :] = q_ref[:, cols]
        out_ref[h, TOK : 2 * TOK, :] = k_ref[:, cols]
        out_ref[h, 2 * TOK : 3 * TOK, :] = v_ref[:, cols]
        out_ref[h, 3 * TOK : CHUNK, :] = packed


def pack_heads(token, docs, q, k, v):
    wide = pl.BlockSpec((TOK, 4 * DH), lambda i: (0, i))
    return pl.pallas_call(
        pack_heads_kernel,
        grid=(4,),
        in_specs=[
            pl.BlockSpec((2, 4, 2), lambda i: (0, 0, 0)),
            pl.BlockSpec((1, TOK), lambda i: (0, 0)),
            wide,
            wide,
            wide,
        ],
        out_specs=pl.BlockSpec((4, CHUNK, DH), lambda i: (i, 0, 0)),
        out_shape=jax.ShapeDtypeStruct((NC, CHUNK, DH), bf16),
        compiler_params=params(),
        cost_estimate=cost(0, 6 << 20),
        name="pack_heads",
    )(token, docs, q, k, v)


def unpack_heads_kernel(x_ref, out_ref):
    for h in range(4):
        out_ref[:, h * DH : (h + 1) * DH] = x_ref[h]


def unpack_heads(x):
    return pl.pallas_call(
        unpack_heads_kernel,
        grid=(4,),
        in_specs=[pl.BlockSpec((4, TOK, DH), lambda i: (i, 0, 0))],
        out_specs=pl.BlockSpec((TOK, 4 * DH), lambda i: (0, i)),
        out_shape=jax.ShapeDtypeStruct((TOK, HD), bf16),
        compiler_params=params(),
        cost_estimate=cost(0, 2 << 20),
        name="unpack_heads",
    )(x)


def self_kernel(x_ref, o_ref):
    docs = x_ref[:, 3 * TOK : CHUNK, :].astype(f32)
    ends = [jnp.sum(jnp.where(docs < d - 0.5, 1.0, 0.0)).astype(i32) for d in (1, 2, 3)]
    per = QT // TOK

    def start_of(p):
        s = jnp.where(p >= ends[0], ends[0], 0)
        s = jnp.maximum(s, jnp.where(p >= ends[1], ends[1], 0))
        return jnp.maximum(s, jnp.where(p >= ends[2], ends[2], 0))

    def rows(j, part):
        return x_ref[pl.ds(per * j, per), part * TOK : (part + 1) * TOK, :].reshape(QT, DH)

    def lanes(p):
        return sum(p[:, c : c + DH] for c in range(0, p.shape[1], DH))

    def query_tile(i, carry):
        base = i * QT
        qs = [x_ref[per * i + u, 0:TOK, :] for u in range(per)]
        columns = [lax.broadcasted_iota(i32, (TOK, 1), 0) + u * TOK for u in range(per)]
        firsts = [start_of(base + c) for c in columns]
        lo = start_of(base) // QT
        mid = jnp.minimum((start_of(base + QT - 1) + QT - 1) // QT, i)

        def step(j, state, kind):
            k, v = rows(j, 1), rows(j, 2)
            ss = []
            for u in range(per):
                width = (u + 1) * TOK if kind == "diagonal" else QT
                s = lax.dot_general(qs[u], k[:width], (((1,), (1,)), ((), ())), preferred_element_type=f32)
                s = s * SCALE
                if kind != "open":
                    local = lax.broadcasted_iota(i32, (TOK, width), 1)
                    seen = local >= firsts[u] - j * QT
                    if kind == "diagonal":
                        seen = seen & (local <= columns[u])
                    s = jnp.where(seen, s, NEG)
                ss.append(s)
            out = []
            for u, s in enumerate(ss):
                new = jnp.max(s, axis=1, keepdims=True)
                if state is not None:
                    acc, top, total = state[u]
                    new = jnp.maximum(top, new)
                p = jnp.exp2(s - new)
                mixed = jnp.dot(p.astype(bf16), v[: s.shape[1]], preferred_element_type=f32)
                weight = lanes(p)
                if state is not None:
                    fade = jnp.exp2(top - new)
                    mixed = acc * fade + mixed
                    weight = total * fade + weight
                out.append((mixed, new, weight))
            return tuple(out)

        state = step(i, None, "diagonal")
        state = lax.fori_loop(lo, mid, functools.partial(step, kind="masked"), state)
        state = lax.fori_loop(mid, i, functools.partial(step, kind="open"), state)
        for u, (acc, top, total) in enumerate(state):
            o_ref[per * i + u] = (acc / jnp.sum(total, axis=1, keepdims=True)).astype(bf16)
        return carry

    lax.fori_loop(0, NC * TOK // QT, query_tile, 0)


def self_attention(x):
    return pl.pallas_call(
        self_kernel,
        in_specs=[pl.BlockSpec(memory_space=pltpu.VMEM)],
        out_specs=pl.BlockSpec(memory_space=pltpu.VMEM),
        out_shape=jax.ShapeDtypeStruct((NC, TOK, DH), bf16),
        compiler_params=params(),
        cost_estimate=cost(16 << 30, 4 << 20),
        name="self_attention",
    )(x)


SHIFTS = (1, 3, 2)


def pack_spans_kernel(far, tab_ref, keys_ref, values_ref, out_ref, hold, loads, stores):
    me = lax.axis_index("db")
    first, second, seen = jnp.int32(0), jnp.int32(0), jnp.int32(0)
    for r in range(8):
        entry = tab_ref[far, r // 2, r % 2]
        hit = (entry >> 3) == me
        span = entry & 7
        first = jnp.where(hit & (seen == 0), span, first)
        second = jnp.where(hit & (seen == 1), span, second)
        seen = seen + jnp.where(hit, 1, 0)
    moves = []
    for slot, span in ((0, first), (1, second)):
        for kind, src in ((0, keys_ref), (1, values_ref)):
            at = (slot, kind)
            load = pltpu.make_async_copy(src.at[span], hold.at[at], loads.at[at])
            load.start()
            moves.append((load, pltpu.make_async_copy(hold.at[at], out_ref.at[at], stores.at[at])))
    for load, store in moves:
        load.wait()
        store.start()
    for load, store in moves:
        store.wait()


def pack_spans(far, table, keys, values):
    anywhere = pl.BlockSpec(memory_space=pl.ANY)
    return pl.pallas_call(
        functools.partial(pack_spans_kernel, int(far)),
        in_specs=[pl.BlockSpec(memory_space=pltpu.SMEM), anywhere, anywhere],
        out_specs=anywhere,
        out_shape=jax.ShapeDtypeStruct((2, 2, CH, HD), bf16),
        scratch_shapes=[
            pltpu.VMEM((2, 2, CH, HD), bf16),
            pltpu.SemaphoreType.DMA((2, 2)),
            pltpu.SemaphoreType.DMA((2, 2)),
        ],
        compiler_params=pltpu.CompilerParams(vmem_limit_bytes=GRANT << 20),
        cost_estimate=cost(0, 3 << 20),
        name="pack_far" if far else "pack_near",
    )(table, keys, values)


def cross_kernel(far, tab_ref, q_ref, *refs):
    keys_ref, values_ref = refs[:2]
    got = refs[2:5]
    if far:
        out_ref, kbuf, vbuf, sems = refs[5:]
    else:
        part_ref, out_ref, kbuf, vbuf, sems = refs[5:]
    me = lax.axis_index("db")
    plane, z = me >> 2, me & 3
    row = 1 if far else 0
    here = []
    entries = [tab_ref[row, r // 2, r % 2] for r in range(8)]
    owners = [entry >> 3 for entry in entries]
    for r in range(8):
        owner = owners[r]
        slot = jnp.int32(0)
        for earlier in range(r):
            slot = slot + jnp.where(owners[earlier] == owner, 1, 0)
        here.append(jnp.where((owner >> 2) == plane, 1, 0))
        shift = (z - owner) & 3
        place = pl.ds((r % 2) * CH, CH)
        span = entries[r] & 7

        @pl.when(shift == 0)
        def _(span=span, place=place, r=r):
            pltpu.make_async_copy(keys_ref.at[span], kbuf.at[r // 2, place], sems.at[r, 0]).start()
            pltpu.make_async_copy(values_ref.at[span], vbuf.at[r // 2, place], sems.at[r, 1]).start()

        for i, k in enumerate(SHIFTS):

            @pl.when(shift == k)
            def _(i=i, slot=slot, place=place, r=r):
                pltpu.make_async_copy(got[i].at[slot, 0], kbuf.at[r // 2, place], sems.at[r, 0]).start()
                pltpu.make_async_copy(got[i].at[slot, 1], vbuf.at[r // 2, place], sems.at[r, 1]).start()

    lane = lax.broadcasted_iota(i32, (1, DH), 1)
    for n in range(4):
        for r in (2 * n, 2 * n + 1):
            place = pl.ds((r % 2) * CH, CH)
            pltpu.make_async_copy(keys_ref.at[0], kbuf.at[n, place], sems.at[r, 0]).wait()
            pltpu.make_async_copy(values_ref.at[0], vbuf.at[n, place], sems.at[r, 1]).wait()
        mine = jnp.where(lane < CH, here[2 * n], here[2 * n + 1]) > 0
        toks = slice(n * CH, (n + 1) * CH)
        heads = [slice(h * DH, (h + 1) * DH) for h in range(NH)]
        s = [
            lax.dot_general(
                q_ref[toks, c], kbuf[n, :, c], (((1,), (1,)), ((), ())), preferred_element_type=f32
            )
            for c in heads
        ]
        s = [jnp.where(mine, x * SCALE, NEG) for x in s]
        top = [jnp.max(x, axis=1, keepdims=True) for x in s]
        p = [jnp.where(mine, jnp.exp2(x - t), 0.0) for x, t in zip(s, top)]
        total = [jnp.sum(x, axis=1, keepdims=True) for x in p]
        o = [jnp.dot(x.astype(bf16), vbuf[n, :, c], preferred_element_type=f32) for x, c in zip(p, heads)]
        if far:
            stats = jnp.full((CH, DH), NEG, f32)
            for h, c in enumerate(heads):
                safe = jnp.maximum(total[h], 1e-30)
                out_ref[toks, c] = (o[h] / safe).astype(bf16)
                lse = jnp.where(total[h] > 0, top[h] + jnp.log2(safe), NEG)
                stats = jnp.where(lane % NH == h, lse, stats)
            high = stats.astype(bf16).astype(f32)
            low = (stats - high).astype(bf16).astype(f32)
            rest = stats - high - low
            stats = jnp.where(lane < NH, high, jnp.where(lane < 2 * NH, low, rest))
            out_ref[toks, HD:] = stats.astype(bf16)
        else:
            stats = part_ref[toks, HD:].astype(f32)
            other = (stats[:, :NH] + stats[:, NH : 2 * NH]) + stats[:, 2 * NH : 3 * NH]
            tops = jnp.full((CH, NH), NEG, f32)
            sums = jnp.zeros((CH, NH), f32)
            slot = lax.broadcasted_iota(i32, (1, NH), 1)
            for h in range(NH):
                tops = jnp.where(slot == h, top[h], tops)
                sums = jnp.where(slot == h, total[h], sums)
            high = jnp.maximum(tops, other)
            a, b = jnp.exp2(tops - high), jnp.exp2(other - high)
            inverse = 1.0 / (sums * a + b)
            a, b = a * inverse, b * inverse
            for h, c in enumerate(heads):
                mixed = o[h] * a[:, h : h + 1] + part_ref[toks, c].astype(f32) * b[:, h : h + 1]
                out_ref[toks, c] = mixed.astype(bf16)


def cross(far, table, q, keys, values, got, part=()):
    vmem = pl.BlockSpec(memory_space=pltpu.VMEM)
    return pl.pallas_call(
        functools.partial(cross_kernel, far),
        in_specs=[pl.BlockSpec(memory_space=pltpu.SMEM), vmem]
        + [pl.BlockSpec(memory_space=pl.ANY)] * 5
        + [vmem] * len(part),
        out_specs=vmem,
        out_shape=jax.ShapeDtypeStruct((TOK, HD + DH if far else HD), bf16),
        scratch_shapes=[
            pltpu.VMEM((4, 2 * CH, HD), bf16),
            pltpu.VMEM((4, 2 * CH, HD), bf16),
            pltpu.SemaphoreType.DMA((8, 2)),
        ],
        compiler_params=params(),
        cost_estimate=pl.CostEstimate(flops=32 << 30 if far else 1 << 26, bytes_accessed=0, transcendentals=0),
        name="cross_far" if far else "cross_near",
    )(table, q, keys, values, *got, *part)


def arrived_kernel(*refs):
    pass


def arrived(xs):
    anywhere = pl.BlockSpec(memory_space=pl.ANY)
    return pl.pallas_call(
        arrived_kernel,
        in_specs=[anywhere] * len(xs),
        out_specs=[anywhere] * len(xs),
        out_shape=[jax.ShapeDtypeStruct(x.shape, x.dtype) for x in xs],
        input_output_aliases={i: i for i in range(len(xs))},
        compiler_params=params(),
        cost_estimate=pl.CostEstimate(flops=32 << 30, bytes_accessed=0, transcendentals=0),
        name="arrived",
    )(*xs)


def per_device(queries, keys, values, doc_ids, nbr_owner, nbr_local, db_keys, db_values):
    q, db_k, db_v = queries[0], db_keys[0], db_values[0]
    swap = [(d, (d + NZ) % 8) for d in range(8)]
    turn = lambda k: [(s * NZ + z, s * NZ + (z + k) % NZ) for s in range(2) for z in range(NZ)]
    far_q = lax.ppermute(q, "db", swap)

    asked = lax.optimization_barrier(nbr_owner * 8 + nbr_local)
    table = jnp.concatenate([asked, lax.ppermute(asked, "db", swap)], axis=0)
    tables = [lax.ppermute(table, "db", turn(NZ - k)) for k in SHIFTS]
    far = [pack_spans(True, t, db_k, db_v) for t in tables]
    far_got = [lax.ppermute(x, "db", turn(k)) for x, k in zip(far, SHIFTS)]

    heads = pack_heads(table, doc_ids, q, keys[0], values[0])
    heads = lax.all_to_all(heads, "ctx", split_axis=0, concat_axis=0, tiled=True)

    near = [pack_spans(False, t, db_k, db_v) for t in tables]
    near_got = []
    for i, k in enumerate(SHIFTS):
        near_got.append(lax.ppermute(near[i], "db", turn(k)))
    part = lax.ppermute(cross(True, table, far_q, db_k, db_v, far_got), "db", swap)

    self_rows = self_attention(heads)
    self_rows = lax.all_to_all(self_rows, "ctx", split_axis=0, concat_axis=0, tiled=True)
    self_rows = unpack_heads(self_rows)

    near_got = arrived(near_got)
    cross_rows = cross(False, table, q, db_k, db_v, near_got, (part,))
    return self_rows[None], cross_rows[None]


def solution(mesh):
    rows = P("db", "ctx", None)
    spans = P("db", "ctx", None, None)
    return jax.shard_map(
        per_device,
        mesh=mesh,
        in_specs=(rows, rows, rows, P("db", "ctx"), rows, rows, spans, spans),
        out_specs=(rows, rows),
        check_vma=False,
    )
```

```python
import functools
import math

import jax
import jax.numpy as jnp
from jax import lax
from jax.experimental import pallas as pl
from jax.experimental.pallas import tpu as pltpu
from jax.sharding import PartitionSpec as P

DH = 128
CH = 64
NH = 16
TOK = 256
HD = 2048
NZ = 4
NC = 16
QT = 2048
CHUNK = 3 * TOK + 16
NEG = -1e30
SCALE = math.log2(math.e) / math.sqrt(DH)
VMEM = 48 << 20
GRANT = 60

f32, bf16, i32 = jnp.float32, jnp.bfloat16, jnp.int32


def params():
    return pltpu.CompilerParams(vmem_limit_bytes=VMEM)


def cost(flops, nbytes):
    return pl.CostEstimate(flops=flops // 64, bytes_accessed=nbytes // 16, transcendentals=0)


def pack_heads_kernel(token_ref, docs_ref, q_ref, k_ref, v_ref, out_ref):
    row = lax.broadcasted_iota(i32, (16, DH), 0)
    docs = docs_ref[...]
    left = jnp.broadcast_to(docs[:, :DH], (16, DH))
    right = jnp.broadcast_to(docs[:, DH:], (16, DH))
    packed = jnp.where(row == 0, left, jnp.where(row == 1, right, 4)).astype(f32).astype(bf16)
    for h in range(4):
        cols = slice(h * DH, (h + 1) * DH)
        out_ref[h, 0:TOK, :] = q_ref[:, cols]
        out_ref[h, TOK : 2 * TOK, :] = k_ref[:, cols]
        out_ref[h, 2 * TOK : 3 * TOK, :] = v_ref[:, cols]
        out_ref[h, 3 * TOK : CHUNK, :] = packed


def pack_heads(token, docs, q, k, v):
    wide = pl.BlockSpec((TOK, 4 * DH), lambda i: (0, i))
    return pl.pallas_call(
        pack_heads_kernel,
        grid=(4,),
        in_specs=[
            pl.BlockSpec((2, 4, 2), lambda i: (0, 0, 0)),
            pl.BlockSpec((1, TOK), lambda i: (0, 0)),
            wide,
            wide,
            wide,
        ],
        out_specs=pl.BlockSpec((4, CHUNK, DH), lambda i: (i, 0, 0)),
        out_shape=jax.ShapeDtypeStruct((NC, CHUNK, DH), bf16),
        compiler_params=params(),
        cost_estimate=cost(0, 6 << 20),
        name="pack_heads",
    )(token, docs, q, k, v)


def unpack_heads_kernel(x_ref, out_ref):
    for h in range(4):
        out_ref[:, h * DH : (h + 1) * DH] = x_ref[h]


def unpack_heads(x):
    return pl.pallas_call(
        unpack_heads_kernel,
        grid=(4,),
        in_specs=[pl.BlockSpec((4, TOK, DH), lambda i: (i, 0, 0))],
        out_specs=pl.BlockSpec((TOK, 4 * DH), lambda i: (0, i)),
        out_shape=jax.ShapeDtypeStruct((TOK, HD), bf16),
        compiler_params=params(),
        cost_estimate=cost(0, 2 << 20),
        name="unpack_heads",
    )(x)


def self_kernel(x_ref, o_ref):
    docs = x_ref[:, 3 * TOK : CHUNK, :].astype(f32)
    ends = [jnp.sum(jnp.where(docs < d - 0.5, 1.0, 0.0)).astype(i32) for d in (1, 2, 3)]
    per = QT // TOK

    def start_of(p):
        s = jnp.where(p >= ends[0], ends[0], 0)
        s = jnp.maximum(s, jnp.where(p >= ends[1], ends[1], 0))
        return jnp.maximum(s, jnp.where(p >= ends[2], ends[2], 0))

    def rows(j, part):
        return x_ref[pl.ds(per * j, per), part * TOK : (part + 1) * TOK, :].reshape(QT, DH)

    def lanes(p):
        return sum(p[:, c : c + DH] for c in range(0, p.shape[1], DH))

    def query_tile(i, carry):
        base = i * QT
        qs = [x_ref[per * i + u, 0:TOK, :] for u in range(per)]
        columns = [lax.broadcasted_iota(i32, (TOK, 1), 0) + u * TOK for u in range(per)]
        firsts = [start_of(base + c) for c in columns]
        lo = start_of(base) // QT
        mid = jnp.minimum((start_of(base + QT - 1) + QT - 1) // QT, i)

        def step(j, state, kind):
            k, v = rows(j, 1), rows(j, 2)
            ss = []
            for u in range(per):
                width = (u + 1) * TOK if kind == "diagonal" else QT
                s = lax.dot_general(qs[u], k[:width], (((1,), (1,)), ((), ())), preferred_element_type=f32)
                s = s * SCALE
                if kind != "open":
                    local = lax.broadcasted_iota(i32, (TOK, width), 1)
                    seen = local >= firsts[u] - j * QT
                    if kind == "diagonal":
                        seen = seen & (local <= columns[u])
                    s = jnp.where(seen, s, NEG)
                ss.append(s)
            out = []
            for u, s in enumerate(ss):
                new = jnp.max(s, axis=1, keepdims=True)
                if state is not None:
                    acc, top, total = state[u]
                    new = jnp.maximum(top, new)
                p = jnp.exp2(s - new)
                mixed = jnp.dot(p.astype(bf16), v[: s.shape[1]], preferred_element_type=f32)
                weight = lanes(p)
                if state is not None:
                    fade = jnp.exp2(top - new)
                    mixed = acc * fade + mixed
                    weight = total * fade + weight
                out.append((mixed, new, weight))
            return tuple(out)

        state = step(i, None, "diagonal")
        state = lax.fori_loop(lo, mid, functools.partial(step, kind="masked"), state)
        state = lax.fori_loop(mid, i, functools.partial(step, kind="open"), state)
        for u, (acc, top, total) in enumerate(state):
            o_ref[per * i + u] = (acc / jnp.sum(total, axis=1, keepdims=True)).astype(bf16)
        return carry

    lax.fori_loop(0, NC * TOK // QT, query_tile, 0)


def self_attention(x):
    return pl.pallas_call(
        self_kernel,
        in_specs=[pl.BlockSpec(memory_space=pltpu.VMEM)],
        out_specs=pl.BlockSpec(memory_space=pltpu.VMEM),
        out_shape=jax.ShapeDtypeStruct((NC, TOK, DH), bf16),
        compiler_params=params(),
        cost_estimate=cost(16 << 30, 4 << 20),
        name="self_attention",
    )(x)


SHIFTS = (1, 3, 2)


def pack_spans_kernel(far, tab_ref, keys_ref, values_ref, *refs):
    out_ref, hold, loads, stores = refs[-4:]
    me = lax.axis_index("db")
    first, second, seen = jnp.int32(0), jnp.int32(0), jnp.int32(0)
    for r in range(8):
        entry = tab_ref[far, r // 2, r % 2]
        hit = (entry >> 3) == me
        span = entry & 7
        first = jnp.where(hit & (seen == 0), span, first)
        second = jnp.where(hit & (seen == 1), span, second)
        seen = seen + jnp.where(hit, 1, 0)
    moves = []
    for slot, span in ((0, first), (1, second)):
        for kind, src in ((0, keys_ref), (1, values_ref)):
            at = (slot, kind)
            load = pltpu.make_async_copy(src.at[span], hold.at[at], loads.at[at])
            load.start()
            moves.append((load, pltpu.make_async_copy(hold.at[at], out_ref.at[at], stores.at[at])))
    for load, store in moves:
        load.wait()
        store.start()
    for load, store in moves:
        store.wait()


def pack_spans(far, table, keys, values, *after):
    anywhere = pl.BlockSpec(memory_space=pl.ANY)
    return pl.pallas_call(
        functools.partial(pack_spans_kernel, int(far)),
        in_specs=[pl.BlockSpec(memory_space=pltpu.SMEM)] + [anywhere] * (2 + len(after)),
        out_specs=anywhere,
        out_shape=jax.ShapeDtypeStruct((2, 2, CH, HD), bf16),
        scratch_shapes=[
            pltpu.VMEM((2, 2, CH, HD), bf16),
            pltpu.SemaphoreType.DMA((2, 2)),
            pltpu.SemaphoreType.DMA((2, 2)),
        ],
        compiler_params=pltpu.CompilerParams(vmem_limit_bytes=GRANT << 20),
        cost_estimate=cost(0, 3 << 20),
        name="pack_far" if far else "pack_near",
    )(table, keys, values, *after)


def cross_kernel(far, tab_ref, q_ref, *refs):
    keys_ref, values_ref = refs[:2]
    got = refs[2:5]
    if far:
        out_ref, kbuf, vbuf, sems = refs[5:]
    else:
        part_ref, out_ref, kbuf, vbuf, sems = refs[5:]
    me = lax.axis_index("db")
    plane, z = me >> 2, me & 3
    row = 1 if far else 0
    here = []
    entries = [tab_ref[row, r // 2, r % 2] for r in range(8)]
    owners = [entry >> 3 for entry in entries]
    for r in range(8):
        owner = owners[r]
        slot = jnp.int32(0)
        for earlier in range(r):
            slot = slot + jnp.where(owners[earlier] == owner, 1, 0)
        here.append(jnp.where((owner >> 2) == plane, 1, 0))
        shift = (z - owner) & 3
        place = pl.ds((r % 2) * CH, CH)
        span = entries[r] & 7

        @pl.when(shift == 0)
        def _(span=span, place=place, r=r):
            pltpu.make_async_copy(keys_ref.at[span], kbuf.at[r // 2, place], sems.at[r, 0]).start()
            pltpu.make_async_copy(values_ref.at[span], vbuf.at[r // 2, place], sems.at[r, 1]).start()

        for i, k in enumerate(SHIFTS):

            @pl.when(shift == k)
            def _(i=i, slot=slot, place=place, r=r):
                pltpu.make_async_copy(got[i].at[slot, 0], kbuf.at[r // 2, place], sems.at[r, 0]).start()
                pltpu.make_async_copy(got[i].at[slot, 1], vbuf.at[r // 2, place], sems.at[r, 1]).start()

    lane = lax.broadcasted_iota(i32, (1, DH), 1)
    for n in range(4):
        for r in (2 * n, 2 * n + 1):
            place = pl.ds((r % 2) * CH, CH)
            pltpu.make_async_copy(keys_ref.at[0], kbuf.at[n, place], sems.at[r, 0]).wait()
            pltpu.make_async_copy(values_ref.at[0], vbuf.at[n, place], sems.at[r, 1]).wait()
        mine = jnp.where(lane < CH, here[2 * n], here[2 * n + 1]) > 0
        toks = slice(n * CH, (n + 1) * CH)
        heads = [slice(h * DH, (h + 1) * DH) for h in range(NH)]
        s = [
            lax.dot_general(
                q_ref[toks, c], kbuf[n, :, c], (((1,), (1,)), ((), ())), preferred_element_type=f32
            )
            for c in heads
        ]
        s = [jnp.where(mine, x * SCALE, NEG) for x in s]
        top = [jnp.max(x, axis=1, keepdims=True) for x in s]
        p = [jnp.where(mine, jnp.exp2(x - t), 0.0) for x, t in zip(s, top)]
        total = [jnp.sum(x, axis=1, keepdims=True) for x in p]
        o = [jnp.dot(x.astype(bf16), vbuf[n, :, c], preferred_element_type=f32) for x, c in zip(p, heads)]
        if far:
            stats = jnp.full((CH, DH), NEG, f32)
            for h, c in enumerate(heads):
                safe = jnp.maximum(total[h], 1e-30)
                out_ref[toks, c] = (o[h] / safe).astype(bf16)
                lse = jnp.where(total[h] > 0, top[h] + jnp.log2(safe), NEG)
                stats = jnp.where(lane % NH == h, lse, stats)
            high = stats.astype(bf16).astype(f32)
            low = (stats - high).astype(bf16).astype(f32)
            rest = stats - high - low
            stats = jnp.where(lane < NH, high, jnp.where(lane < 2 * NH, low, rest))
            out_ref[toks, HD:] = stats.astype(bf16)
        else:
            stats = part_ref[toks, HD:].astype(f32)
            other = (stats[:, :NH] + stats[:, NH : 2 * NH]) + stats[:, 2 * NH : 3 * NH]
            tops = jnp.full((CH, NH), NEG, f32)
            sums = jnp.zeros((CH, NH), f32)
            slot = lax.broadcasted_iota(i32, (1, NH), 1)
            for h in range(NH):
                tops = jnp.where(slot == h, top[h], tops)
                sums = jnp.where(slot == h, total[h], sums)
            high = jnp.maximum(tops, other)
            a, b = jnp.exp2(tops - high), jnp.exp2(other - high)
            inverse = 1.0 / (sums * a + b)
            a, b = a * inverse, b * inverse
            for h, c in enumerate(heads):
                mixed = o[h] * a[:, h : h + 1] + part_ref[toks, c].astype(f32) * b[:, h : h + 1]
                out_ref[toks, c] = mixed.astype(bf16)


def cross(far, table, q, keys, values, got, part=()):
    vmem = pl.BlockSpec(memory_space=pltpu.VMEM)
    return pl.pallas_call(
        functools.partial(cross_kernel, far),
        in_specs=[pl.BlockSpec(memory_space=pltpu.SMEM), vmem]
        + [pl.BlockSpec(memory_space=pl.ANY)] * 5
        + [vmem] * len(part),
        out_specs=vmem,
        out_shape=jax.ShapeDtypeStruct((TOK, HD + DH if far else HD), bf16),
        scratch_shapes=[
            pltpu.VMEM((4, 2 * CH, HD), bf16),
            pltpu.VMEM((4, 2 * CH, HD), bf16),
            pltpu.SemaphoreType.DMA((8, 2)),
        ],
        compiler_params=params(),
        cost_estimate=pl.CostEstimate(flops=32 << 30 if far else 1 << 26, bytes_accessed=0, transcendentals=0),
        name="cross_far" if far else "cross_near",
    )(table, q, keys, values, *got, *part)


def arrived_kernel(*refs):
    pass


def arrived(xs):
    anywhere = pl.BlockSpec(memory_space=pl.ANY)
    return pl.pallas_call(
        arrived_kernel,
        in_specs=[anywhere] * len(xs),
        out_specs=[anywhere] * len(xs),
        out_shape=[jax.ShapeDtypeStruct(x.shape, x.dtype) for x in xs],
        input_output_aliases={i: i for i in range(len(xs))},
        compiler_params=params(),
        cost_estimate=pl.CostEstimate(flops=32 << 30, bytes_accessed=0, transcendentals=0),
        name="arrived",
    )(*xs)


def per_device(queries, keys, values, doc_ids, nbr_owner, nbr_local, db_keys, db_values):
    q, db_k, db_v = queries[0], db_keys[0], db_values[0]
    swap = [(d, (d + NZ) % 8) for d in range(8)]
    turn = lambda k: [(s * NZ + z, s * NZ + (z + k) % NZ) for s in range(2) for z in range(NZ)]
    far_q = lax.ppermute(q, "db", swap)

    asked = lax.optimization_barrier(nbr_owner * 8 + nbr_local)
    table = jnp.concatenate([asked, lax.ppermute(asked, "db", swap)], axis=0)
    tables = [lax.ppermute(table, "db", turn(NZ - k)) for k in SHIFTS]
    heads = pack_heads(table, doc_ids, q, keys[0], values[0])
    far = [pack_spans(True, t, db_k, db_v, heads) for t in tables[:2]]
    far.append(pack_spans(True, tables[2], db_k, db_v))
    far_got = [lax.ppermute(x, "db", turn(k)) for x, k in zip(far, SHIFTS)]

    heads = lax.all_to_all(heads, "ctx", split_axis=0, concat_axis=0, tiled=True)

    near = [pack_spans(False, t, db_k, db_v) for t in tables]
    near_got = []
    for i, k in enumerate(SHIFTS):
        near_got.append(lax.ppermute(near[i], "db", turn(k)))
    part = lax.ppermute(cross(True, table, far_q, db_k, db_v, far_got), "db", swap)

    self_rows = self_attention(heads)
    self_rows = lax.all_to_all(self_rows, "ctx", split_axis=0, concat_axis=0, tiled=True)
    self_rows = unpack_heads(self_rows)

    near_got = arrived(near_got)
    cross_rows = cross(False, table, q, db_k, db_v, near_got, (part,))
    return self_rows[None], cross_rows[None]


def solution(mesh):
    rows = P("db", "ctx", None)
    spans = P("db", "ctx", None, None)
    return jax.shard_map(
        per_device,
        mesh=mesh,
        in_specs=(rows, rows, rows, P("db", "ctx"), rows, rows, spans, spans),
        out_specs=(rows, rows),
        check_vma=False,
    )
```
